32 devices in a mesh: bulk: 4 (over y, core), front: 8 (over z, x).
Axes of the slice: x: 2, y: 2, z: 4, core: 2. Of those that a mesh axis runs over, the one named last changes fastest.
Arguments:
- child_pivot: float32 [4, 2048, 2048], P('bulk', 'front'), may hold values from -20 to 40, as said below
- child_coupling: float32 [4, 2048, 2048], P('bulk', 'front'), may hold values from -0.75 to 0.75
- parent_arrow: float32 [8192, 1024], P(('bulk', 'front')), may hold values from -600 to 3000, as said below
- row_map: int32 [4, 2048], P('bulk', 'front'), may hold values from 0 to 8191, as said below
- block_pattern: int32 [64, 8], replicated, may hold values from 0 to 1, as said below
Outputs:
- child_factor_pivot: float32 [4, 2048, 2048], P('bulk', 'front')
- child_factor_coupling: float32 [4, 2048, 2048], P('bulk', 'front')
- parent_factor: float32 [8192, 1024], P(('bulk', 'front'))
The draws below stay inside these ranges and needn't reach their ends.
Inputs may be any that keep to these rules, and one draw needn't show every extreme that they name: `child_pivot`: each child's matrix is symmetric and positive definite. `parent_arrow`: the first 1024 rows hold a symmetric block that stays positive definite when contribution is added. `row_map`: A child's 2048 entries are distinct. Entry i of a child names a row r with (r // 256) % (8) == i // 256. `block_pattern`: every block (i, i) with i < 8 is 1.
All inputs are finite; a program needn't handle non-finite values.
Results may differ from the reference program's by a relative error of at most 0.00022.
Values sent between devices are 32-bit elements; how exact they have to be, the bound alone decides.
No kernel may reach another device: no remote copies, remote signals or barrier semaphores. Data moves between devices by JAX's collectives and lax.ppermute only.
A program may use at most 128 MiB of HBM per device.

```python
import jax
import jax.numpy as jnp
from jax import lax

EC = 2048
UC = 2048
PO = 8192
PE = 1024
BLOCK = 128
CHILDREN = 4
N_BULK = 4
N_FRONT = 8


def draw_child_pivot(key, part):
    key_basis, key_shift = jax.random.split(key, 2)
    samples = EC + EC // 4
    basis = jax.random.normal(key_basis, (N_BULK, EC, samples), jnp.float32)
    gram = jnp.einsum('cik,cjk->cij', basis, basis, precision=lax.Precision.HIGHEST) / samples
    shift = jax.random.uniform(key_shift, (N_BULK, EC), jnp.float32, 0.02, 0.08)
    matrix = gram + shift[:, :, None] * jnp.eye(EC, dtype=jnp.float32)[None]
    return matrix


def draw_parent_arrow(key, part):
    key_top, key_diag, key_rest = jax.random.split(key, 3)
    samples = PE + PE // 4
    basis = jax.random.normal(key_top, (PE, samples), jnp.float32)
    gram = jnp.dot(basis, basis.T, precision=lax.Precision.HIGHEST) / samples
    offset = jax.random.uniform(key_diag, (PE,), jnp.float32, 150.0, 250.0)
    upper_block = 500.0 * gram + jnp.diag(offset)
    lower_rows = jnp.clip(3.0 * jax.random.normal(key_rest, (PO - PE, PE), jnp.float32), -18.0, 18.0)
    return jnp.concatenate([upper_block, lower_rows], axis=0)


def draw_row_map(key, part):
    row_count = PO // (N_BULK * N_FRONT)
    candidates = N_BULK * row_count
    per_block = UC // N_FRONT
    forced = jnp.full((N_BULK * N_FRONT,), -1, jnp.int32).at[0].set(0).at[N_FRONT - 1].set(candidates - 1)
    block_keys = jax.random.split(key, N_BULK * N_FRONT)

    def pick_rows(one_key, forced_value):
        order = jax.random.permutation(one_key, candidates).astype(jnp.int32)
        where_forced = jnp.argmax(order == forced_value)
        leading = order[0]
        order = order.at[where_forced].set(leading)
        order = order.at[0].set(jnp.where(forced_value >= 0, forced_value, leading))
        return order[:per_block]
    chosen = jax.vmap(pick_rows)(block_keys, forced).reshape(N_BULK, N_FRONT, per_block)
    group_index = chosen // row_count
    inside = chosen % row_count
    front_index = jnp.arange(N_FRONT, dtype=jnp.int32)[None, :, None]
    parent_rows = (group_index * N_FRONT + front_index) * row_count + inside
    return parent_rows.reshape(N_BULK, UC).astype(jnp.int32)


def draw_block_pattern(key, part):
    block_rows = PO // BLOCK
    block_cols = PE // BLOCK
    levels = jax.random.randint(key, (block_rows, block_cols), 0, 4)
    present = levels > 0
    on_diagonal = jnp.arange(block_rows)[:, None] == jnp.arange(block_cols)[None, :]
    return jnp.where(on_diagonal | present, 1, 0).astype(jnp.int32)


def shard_levels(rng, extent, cuts, least, high):
    gain = 1.0
    for axis_at, shards_of in cuts:
        heights = jax.random.uniform(jax.random.fold_in(jax.random.fold_in(rng, 6), axis_at), (shards_of,), jnp.float32, least / len(cuts), high / len(cuts))
        gain = gain * jnp.repeat(jnp.exp(heights), extent[axis_at] // shards_of).reshape((-1,) + (1,) * (len(extent) - 1 - axis_at))
    return gain


def noise(rng, extent, scale, limit, cuts=(), held_as=jnp.bfloat16):
    values = jax.random.normal(rng, extent, jnp.float32) * scale
    if len(cuts) > 0:
        values = shard_levels(rng, extent, cuts, -0.22, 0.18) * values
    return jnp.clip(values, min=-limit, max=limit).astype(held_as)


def setup_inputs(seed: int = 0) -> dict:
    arg_keys = jax.random.split(jax.random.key(seed), 6)
    return {
        "child_pivot": draw_child_pivot(jax.random.fold_in(arg_keys[5], 71), 0),
        "child_coupling": noise(arg_keys[1], (CHILDREN, UC, EC), (2.3 * EC ** -0.5), 0.75, ((0, 4), (1, 8)), jnp.float32),
        "parent_arrow": draw_parent_arrow(jax.random.fold_in(arg_keys[5], 71), 0),
        "row_map": draw_row_map(jax.random.fold_in(arg_keys[5], 71), 0),
        "block_pattern": draw_block_pattern(jax.random.fold_in(arg_keys[5], 71), 0),
    }


HIGHEST_PRECISION = lax.Precision.HIGHEST

def mirror_lower(matrix):
    return jnp.tril(matrix) + jnp.tril(matrix, -1).T

def reference(child_pivot, child_coupling, parent_arrow, row_map, block_pattern):

    def factor_child(operands):
        pivot_block, coupling_rows = operands
        lower_factor = jnp.linalg.cholesky(mirror_lower(pivot_block))
        coupling = jax.scipy.linalg.solve_triangular(lower_factor, coupling_rows.T, lower=True).T
        return (lower_factor, coupling)
    factors, couplings = lax.map(factor_child, (child_pivot, child_coupling))

    def add_child(total, operands):
        coupling, row_index = operands
        landing_top = jnp.zeros((PE, EC), jnp.float32).at[row_index].set(coupling, mode='drop')
        term_rows = -jnp.dot(coupling, landing_top.T, precision=HIGHEST_PRECISION)
        return (total.at[row_index].add(term_rows), None)
    contribution, _ = lax.scan(add_child, jnp.zeros((PO, PE), jnp.float32), (couplings, row_map))
    full_mask = jnp.repeat(jnp.repeat(block_pattern.astype(jnp.float32), BLOCK, axis=0), BLOCK, axis=1)
    assembled = parent_arrow * full_mask + contribution
    parent_lower = jnp.linalg.cholesky(mirror_lower(assembled[:PE]))
    parent_rest = jax.scipy.linalg.solve_triangular(parent_lower, assembled[PE:].T, lower=True).T
    return (factors, couplings, jnp.concatenate([parent_lower, parent_rest], axis=0))
```

```python
import functools

import jax
import jax.numpy as jnp
import numpy as np
from jax import lax
from jax.experimental import pallas as pl
from jax.experimental.pallas import tpu as pltpu
from jax.sharding import PartitionSpec as P

BLOCK = 128
STAGE = 512
CAP = 128
LANES = 128
SUB = 8
VMEM_LIMIT = 60 << 20

HIGHEST_PRECISION = lax.Precision.HIGHEST
NT = (((1,), (1,)), ((), ()))
NN = (((1,), (0,)), ((), ()))
F32 = jnp.float32
BF16 = jnp.bfloat16


def split(x):
    high = x.astype(BF16)
    return high, (x - high.astype(F32)).astype(BF16)


def dot(a, b, dims):
    return lax.dot_general(a, b, dims, preferred_element_type=F32)


def dot3(a, b, dims):
    return dot(a[0], b[0], dims) + (dot(a[0], b[1], dims) + dot(a[1], b[0], dims))


def ds(start, size):
    return pl.ds(pl.multiple_of(start, size), size)


def tiles(rows, cols, body, tile=256):
    tr, tc = min(tile, rows), min(tile, cols)
    nr, nc = rows // tr, cols // tc

    def step(t, carry):
        body((t // nc) * tr, tr, (t % nc) * tc, tc)
        return carry

    lax.fori_loop(0, nr * nc, step, 0)


def lane(x, c):
    return jnp.broadcast_to(x[:, c : c + 1], x.shape)


def sub(x, r):
    return jnp.broadcast_to(x[r : r + 1, :], x.shape)


def tree_sum(terms):
    terms = list(terms)
    while len(terms) > 1:
        terms = [
            terms[i] + terms[i + 1] if i + 1 < len(terms) else terms[i]
            for i in range(0, len(terms), 2)
        ]
    return terms[0]


def small_inverse_factor(s):
    n = len(s)
    s = [list(row) for row in s]
    low = [[None] * n for _ in range(n)]
    inv_diag = [None] * n
    for j in range(n):
        inv_diag[j] = lax.rsqrt(s[j][j])
        for i in range(j + 1, n):
            low[i][j] = s[i][j] * inv_diag[j]
        for i in range(j + 1, n):
            for k in range(j + 1, i + 1):
                s[i][k] = s[i][k] - low[i][j] * low[k][j]
    inv = [[None] * n for _ in range(n)]
    for j in range(n):
        inv[j][j] = inv_diag[j]
        for i in range(j + 1, n):
            inv[i][j] = -tree_sum(low[i][k] * inv[k][j] for k in range(j, i)) * inv_diag[i]
    return inv


def factor_block(rows):
    n = len(rows)
    row_id = lax.broadcasted_iota(jnp.int32, (SUB, LANES), 0)
    col_id = lax.broadcasted_iota(jnp.int32, (SUB, LANES), 1)
    a = list(rows)
    e = [jnp.where(row_id + SUB * s == col_id, 1.0, 0.0).astype(F32) for s in range(n)]
    out = []
    for s in range(n):
        cols = [lane(a[s], SUB * s + r) for r in range(SUB)]
        inv = small_inverse_factor([[sub(cols[j], i) for j in range(i + 1)] for i in range(SUB)])
        ra = [sub(a[s], r) for r in range(SUB)]
        re = [sub(e[s], r) for r in range(SUB)]
        ua = [tree_sum(inv[r][q] * ra[q] for q in range(r + 1)) for r in range(SUB)]
        ue = [tree_sum(inv[r][q] * re[q] for q in range(r + 1)) for r in range(SUB)]
        done = ue[0]
        for r in range(1, SUB):
            done = jnp.where(row_id == r, ue[r], done)
        out.append(done)
        if s + 1 == n:
            break
        ya = [tree_sum(inv[r][q] * ua[r] for r in range(q, SUB)) for q in range(SUB)]
        ye = [tree_sum(inv[r][q] * ue[r] for r in range(q, SUB)) for q in range(SUB)]
        for i in range(s + 1, n):
            w = [lane(a[i], SUB * s + r) for r in range(SUB)]
            a[i] = a[i] - tree_sum(w[r] * ya[r] for r in range(SUB))
            e[i] = e[i] - tree_sum(w[r] * ye[r] for r in range(SUB))
    return out


def subtract_products(dst, rows, cols, ah, al, bh, bl, depth):
    if depth == 0:
        return

    def body(r, nr, c, nc):
        a = (ah[ds(r, nr), :depth], al[ds(r, nr), :depth])
        b = (bh[ds(c, nc), :depth], bl[ds(c, nc), :depth])
        dst[ds(r, nr), ds(c, nc)] = dst[ds(r, nr), ds(c, nc)] - dot3(a, b, NT)

    tiles(rows, cols, body)


def times_inverse(src, outh, outl, out_at, rows, width, invh, invl):
    def body(r, nr, c, nc):
        a = split(src[ds(r, nr), :])
        b = (invh[ds(c, nc), :], invl[ds(c, nc), :])
        high, low = split(dot3(a, b, NT))
        outh[ds(r, nr), pl.ds(pl.multiple_of(out_at + c, nc), nc)] = high
        outl[ds(r, nr), pl.ds(pl.multiple_of(out_at + c, nc), nc)] = low

    tiles(rows, width, body)


def factor_diagonal(s_ref, at, width, lh, ll, invh, invl):
    invh[...] = jnp.zeros(invh.shape, BF16)
    invl[...] = jnp.zeros(invl.shape, BF16)
    row_id = lax.broadcasted_iota(jnp.int32, (width, LANES), 0)
    col_id = lax.broadcasted_iota(jnp.int32, (width, LANES), 1)
    wide_id = lax.broadcasted_iota(jnp.int32, (LANES, width), 1)

    def panel(p, carry):
        first = p * LANES
        here = ds(first, LANES)
        block = [
            s_ref[pl.ds(pl.multiple_of(first + SUB * i, SUB), SUB), here]
            for i in range(LANES // SUB)
        ]
        inv = jnp.concatenate(factor_block(block), axis=0)
        inv2 = split(inv)
        solved = dot3(split(s_ref[:, here]), inv2, NT)
        solved = jnp.where(row_id >= col_id + first, solved, 0.0)
        high, low = split(solved)
        lh[:, pl.ds(pl.multiple_of(at + first, LANES), LANES)] = high
        ll[:, pl.ds(pl.multiple_of(at + first, LANES), LANES)] = low
        below = row_id >= first + LANES
        bh = jnp.where(below, high, jnp.zeros_like(high))
        bl = jnp.where(below, low, jnp.zeros_like(low))

        def update(c, carry2):
            cols = ds(c * LANES, LANES)
            s_ref[:, cols] = s_ref[:, cols] - dot3(
                (bh, bl),
                (
                    jnp.where(c > p, lh[cols, pl.ds(pl.multiple_of(at + first, LANES), LANES)], 0),
                    jnp.where(c > p, ll[cols, pl.ds(pl.multiple_of(at + first, LANES), LANES)], 0),
                ),
                NT,
            )
            return carry2

        lax.fori_loop(p + 1, width // LANES, update, 0)
        left = wide_id < first
        rh = lh[here, at : at + width]
        rl = ll[here, at : at + width]
        rh = jnp.where(left, rh, jnp.zeros_like(rh))
        rl = jnp.where(left, rl, jnp.zeros_like(rl))
        mixed = dot3((rh, rl), (invh[...], invl[...]), NN)
        row = -dot3(inv2, split(mixed), NN)
        high, low = split(row)
        invh[here, :] = high
        invl[here, :] = low
        invh[here, here] = inv2[0]
        invl[here, here] = inv2[1]
        return carry

    lax.fori_loop(0, width // LANES, panel, 0)


def vmem_call(body, out_shapes, in_kinds, scratch, cost=None):
    specs = [pl.BlockSpec(memory_space=pltpu.SMEM if k else pltpu.VMEM) for k in in_kinds]
    return pl.pallas_call(
        body,
        out_shape=out_shapes,
        in_specs=specs,
        out_specs=[pl.BlockSpec(memory_space=pltpu.VMEM)] * len(out_shapes),
        scratch_shapes=scratch,
        compiler_params=pltpu.CompilerParams(vmem_limit_bytes=VMEM_LIMIT),
        cost_estimate=cost,
    )


def shaped(shape, dtype):
    return jax.ShapeDtypeStruct(shape, dtype)


def send_plan(groups, per_stage):
    pairs = [
        (j, i)
        for i in range(groups)
        for j in range(i)
        if not (i == j + 1 and j % 2 == 0)
    ]
    pairs.sort(key=lambda pair: (pair[1] // per_stage, pair))
    taken = {}

    def place(pair, limit, seen):
        for rnd in range(limit):
            for dev in (pair[1], pair[0]):
                slot = (rnd, dev)
                if slot in seen:
                    continue
                seen.add(slot)
                if slot not in taken or place(taken[slot], limit, seen):
                    taken[slot] = pair
                    return True
        return False

    limit = 1
    for pair in pairs:
        while not place(pair, limit, set()):
            limit += 1
    rounds = 1 + max((slot[0] for slot in taken), default=-1)
    table = np.full((max(rounds, 1), groups), -1, np.int32)
    for (rnd, dev), (j, i) in taken.items():
        table[rnd, dev] = j if dev == i else i
    return table[:rounds]


def ring_order(groups):
    return [i for i in range(0, groups, 2)] + [i for i in range(groups - 1, 0, -2)]


def ring_gather(chunk, axis, groups):
    order = ring_order(groups)
    ahead = [(order[i], order[(i + 1) % groups]) for i in range(groups)]
    back = [(b, a) for a, b in ahead]
    out = [chunk]
    going, coming = chunk, chunk
    steps_ahead = groups // 2
    steps_back = groups - 1 - steps_ahead
    aheads, backs = [], []
    for step in range(steps_ahead):
        going = lax.ppermute(going, axis, ahead)
        aheads.append(going)
        if step < steps_back:
            coming = lax.ppermute(coming, axis, back)
            backs.append(coming)
    return out + aheads + backs


def slot_owners(axis, groups):
    order = np.array(ring_order(groups), np.int32)
    place = np.argsort(order)
    me = jnp.asarray(place)[lax.axis_index(axis)]
    steps_ahead = groups // 2
    steps_back = groups - 1 - steps_ahead
    shifts = [0] + [-s for s in range(1, steps_ahead + 1)] + list(range(1, steps_back + 1))
    return jnp.asarray(order)[(me + jnp.asarray(shifts, jnp.int32)) % groups].astype(jnp.int32)


def bulk_gather(x, axis, size):
    me = lax.axis_index(axis)
    held = x[None]
    bits = size.bit_length() - 1
    for bit in range(bits - 1, -1, -1):
        step = 1 << bit
        other = lax.ppermute(held, axis, [(i, i ^ step) for i in range(size)])
        mine_high = (me >> bit) & 1
        held = jnp.where(
            mine_high == 1,
            jnp.concatenate([other, held], axis=0),
            jnp.concatenate([held, other], axis=0),
        )
    order = []
    for k in range(size):
        index = 0
        for bit in range(bits):
            if (k >> (bits - 1 - bit)) & 1:
                index |= 1 << bit
        order.append(index)
    back = np.argsort(np.array(order))
    return held, [int(v) for v in back]


def child_stage(q, width, own, groups, cap, chunk_counts, refs):
    per_stage = width // own
    refs = list(refs)

    def take(count):
        out, refs[:count] = refs[:count], []
        return out

    (owner_ref, table_ref, place_ref) = take(3)
    chunks = [take(count) for count in chunk_counts]
    prev_lh, prev_ll, prev_ih, prev_il, prev_xh, prev_xl = (take(q) for _ in range(6))
    (b_ref, pick_ref) = take(2)
    (lh, ll, invh, invl, xh, xl, top_ref, own_ref) = take(8)
    (a_ref, s_ref) = take(2)
    first_group = q * per_stage

    for k in range(groups):
        f = owner_ref[k]

        @pl.when(f // per_stage == q)
        def _(f=f, k=k):
            chunk = chunks[0][k]
            at = (f - first_group) * own
            a_ref[ds(at, own), ds(f * own, own)] = chunk[:, :own]
            half = own // 2
            odd = f % 2
            row = (f - odd + 1 - first_group) * own + odd * half
            a_ref[ds(row, half), ds((f - odd) * own, own)] = chunk[:, own:].T

    for rnd in range(1, len(chunks)):
        if not chunks[rnd]:
            continue
        for k in range(groups):
            f = owner_ref[k]
            c = table_ref[rnd - 1, f]
            high = jnp.maximum(f, c)
            low = jnp.minimum(f, c)
            mine = jnp.logical_and(c >= 0, high // per_stage == q)
            row = jnp.clip((high - first_group) * own, 0, width - own)
            col = jnp.clip(low * own, 0, (q + 1) * width - own)

            @pl.when(jnp.logical_and(mine, f > c))
            def _(rnd=rnd, k=k, row=row, col=col):
                a_ref[ds(row, own), ds(col, own)] = chunks[rnd][k][...]

            @pl.when(jnp.logical_and(mine, f < c))
            def _(rnd=rnd, k=k, row=row, col=col):
                a_ref[ds(row, own), ds(col, own)] = chunks[rnd][k][...].T

    for j in range(q):
        part = a_ref.at[:, j * width : (j + 1) * width]
        subtract_products(part, width, width, lh, ll, prev_lh[j], prev_ll[j], j * width)
        times_inverse(part, lh, ll, j * width, width, width, prev_ih[j], prev_il[j])
    s_ref[...] = a_ref[:, q * width : (q + 1) * width]
    subtract_products(s_ref, width, width, lh, ll, lh, ll, q * width)
    factor_diagonal(s_ref, q * width, width, lh, ll, invh, invl)

    rest = s_ref.at[:own, :]
    rest[...] = b_ref[...]
    for j in range(q):
        part = slice(j * width, (j + 1) * width)

        def body(r, nr, c, nc, j=j, part=part):
            a = (prev_xh[j][ds(r, nr), :], prev_xl[j][ds(r, nr), :])
            b = (lh[ds(c, nc), part], ll[ds(c, nc), part])
            rest[ds(r, nr), ds(c, nc)] = rest[ds(r, nr), ds(c, nc)] - dot3(a, b, NT)

        tiles(own, width, body)
    times_inverse(rest, xh, xl, 0, own, width, invh, invl)
    pick = pick_ref[...]
    top_ref[...] = dot(pick, xh[...], NN) + dot(pick, xl[...], NN)
    at = place_ref[0]
    own_ref[...] = lh[ds(at, own), :].astype(F32) + ll[ds(at, own), :].astype(F32)


def cross_kernel(stages, own, cap, sources, groups, refs):
    refs = list(refs)

    def take(count):
        out, refs[:count] = refs[:count], []
        return out

    (owner_ref,) = take(1)
    xh, xl = take(stages), take(stages)
    slots = [take(groups) for _ in range(stages)]
    con_ref, sq_ref = take(2)
    th, tl = take(2)
    width = xh[0].shape[1]
    total = sources * cap
    for k in range(groups):
        f = owner_ref[k]

        @pl.when(f < sources)
        def _(f=f, k=k):
            for q in range(stages):
                high, low = split(slots[q][k][...])
                th[ds(f * cap, cap), q * width : (q + 1) * width] = high
                tl[ds(f * cap, cap), q * width : (q + 1) * width] = low

    for c in range(total // LANES):
        rows = slice(c * LANES, (c + 1) * LANES)
        acc = jnp.zeros((own, LANES), F32)
        for q in range(stages):
            cols = slice(q * width, (q + 1) * width)
            acc = acc + dot3((xh[q][...], xl[q][...]), (th[rows, cols], tl[rows, cols]), NT)
        con_ref[:, rows] = acc

    def square(t, carry):
        i = carry[0]
        j = carry[1]
        a = (th[ds(i * LANES, LANES), :], tl[ds(i * LANES, LANES), :])
        b = (th[ds(j * LANES, LANES), :], tl[ds(j * LANES, LANES), :])
        sq_ref[t] = dot3(a, b, NT)
        end = j == i
        return (jnp.where(end, i + 1, i), jnp.where(end, 0, j + 1))

    blocks = total // LANES
    lax.fori_loop(0, blocks * (blocks + 1) // 2, square, (jnp.int32(0), jnp.int32(0)))


def parent_kernel(children, blocks, width, refs):
    top_ref, spread_ref, sq_ref, lh, ll, invh, invl, lower, s_ref = refs
    pivots = top_ref.shape[0]
    dense = pivots // blocks
    for i in range(blocks):
        for j in range(i + 1):
            at = i * (i + 1) // 2 + j
            parts = []
            for c in range(children):
                left = spread_ref[i, :, c * LANES : (c + 1) * LANES]
                high, low = split(sq_ref[c, at])
                parts.append(dot(left, high, NN) + dot(left, low, NN))
            high, low = split(jnp.concatenate(parts, axis=1))
            right = spread_ref[j]
            rows = slice(i * dense, (i + 1) * dense)
            cols = slice(j * dense, (j + 1) * dense)
            s_ref[rows, cols] = top_ref[rows, cols] - (
                dot(high, right, NT) + dot(low, right, NT)
            )
    for q in range(pivots // width):
        rows = slice(q * width, (q + 1) * width)
        lhq, llq = lh.at[rows, :], ll.at[rows, :]
        if q + 1 < pivots // width:
            lhq[:, (q + 1) * width :] = jnp.zeros((width, pivots - (q + 1) * width), BF16)
            llq[:, (q + 1) * width :] = jnp.zeros((width, pivots - (q + 1) * width), BF16)
        for j in range(q):
            part = s_ref.at[rows, j * width : (j + 1) * width]
            cut = slice(j * width, (j + 1) * width)
            subtract_products(part, width, width, lhq, llq, lh.at[cut, :], ll.at[cut, :], j * width)
            times_inverse(part, lhq, llq, j * width, width, width, invh.at[j], invl.at[j])
        part = s_ref.at[rows, q * width : (q + 1) * width]
        subtract_products(part, width, width, lhq, llq, lhq, llq, q * width)
        factor_diagonal(part, q * width, width, lhq, llq, invh.at[q], invl.at[q])
    lower[...] = lh[...].astype(F32) + ll[...].astype(F32)


def rest_kernel(children, blocks, width, refs):
    place_ref, rows_ref, route_ref, con_ref, spread_ref, lh, ll, invh, invl, out_ref, s_ref, xh, xl = refs
    pivots = lh.shape[0]
    own = con_ref.shape[1]
    count = rows_ref.shape[0]
    dense = pivots // blocks
    at = place_ref[1]

    @pl.when(at < pivots)
    def _():
        row = ds(jnp.minimum(at, pivots - count), count)
        out_ref[...] = lh[row, :].astype(F32) + ll[row, :].astype(F32)

    @pl.when(at >= pivots)
    def _():
        routed = []
        for c in range(children):
            high, low = split(con_ref[c])
            route = route_ref[c]
            routed.append(split(dot(route, high, NN) + dot(route, low, NN)))
        for b in range(blocks):
            lanes = slice(b * LANES, (b + 1) * LANES)
            high = jnp.concatenate([routed[c][0][:, lanes] for c in range(children)], axis=1)
            low = jnp.concatenate([routed[c][1][:, lanes] for c in range(children)], axis=1)
            right = spread_ref[b]
            cols = slice(b * dense, (b + 1) * dense)
            s_ref[:, cols] = rows_ref[:, cols] - (dot(high, right, NT) + dot(low, right, NT))
        for q in range(pivots // width):
            cut = slice(q * width, (q + 1) * width)
            part = s_ref.at[:, cut]
            subtract_products(part, count, width, xh, xl, lh.at[cut, :], ll.at[cut, :], q * width)
            times_inverse(part, xh, xl, q * width, count, width, invh.at[q], invl.at[q])
        out_ref[...] = xh[...].astype(F32) + xl[...].astype(F32)


def on_device(child_pivot, child_coupling, parent_arrow, row_map, block_pattern):
    front = lax.axis_size("front")
    bulk = lax.axis_size("bulk")
    me = lax.axis_index("front")
    mine = child_pivot[0]
    coupling = child_coupling[0]
    own, total = mine.shape
    count, pivots = parent_arrow.shape
    width = min(STAGE, total)
    stages = total // width
    per_stage = width // own
    first_row = (lax.axis_index("bulk") * front + me) * count
    sources = pivots // count
    cap = min(CAP, count, own)
    blocks = sources * cap // LANES

    maps = lax.all_gather(row_map[0], ("bulk", "front"), axis=0).reshape(bulk, front, own)
    lands = maps[:, :sources] < pivots
    rank = jnp.cumsum(lands.astype(jnp.int32), axis=2) - 1
    overflow = jnp.any(rank[:, :, -1] >= cap)
    chosen = jnp.where(lands[:, :, None, :], rank[:, :, None, :], -1) == jnp.arange(cap)[:, None]
    target = jnp.max(jnp.where(chosen, maps[:, :sources, None, :], -1), axis=3)
    target = jnp.where(overflow, -1, target).reshape(bulk, blocks, LANES)
    dense = pivots // blocks
    rows_of = (jnp.arange(blocks)[:, None] * dense + jnp.arange(dense)[None, :])[:, :, None, None]
    spread = (jnp.transpose(target, (1, 0, 2))[:, None] == rows_of).astype(BF16)
    spread = spread.reshape(blocks, dense, bulk * LANES)
    own_map = row_map[0]
    own_rank = jnp.where(own_map < pivots, jnp.cumsum((own_map < pivots).astype(jnp.int32)) - 1, -1)
    pick = (own_rank[None, :] == jnp.arange(cap)[:, None]).astype(BF16)
    route = (
        lax.dynamic_index_in_dim(maps, me, 1, False)[:, None, :]
        == (first_row + jnp.arange(count))[None, :, None]
    ).astype(BF16)

    table = send_plan(front, per_stage)
    half = own // 2
    own_block = lax.dynamic_slice_in_dim(mine, me * own, own, 1)
    even = lax.dynamic_slice_in_dim(mine, jnp.minimum(me + 1, front - 1) * own, half, 1)
    odd = lax.dynamic_slice_in_dim(mine[half:], jnp.maximum(me - 1, 0) * own, own, 1).T
    chunks = [jnp.concatenate([own_block, jnp.where(me % 2 == 0, even, odd)], axis=1)]
    for rnd in range(table.shape[0]):
        col = jnp.maximum(jnp.asarray(table[rnd])[me], 0)
        chunks.append(lax.dynamic_slice_in_dim(mine, col * own, own, 1))
    owners = slot_owners("front", front)
    gathered = [ring_gather(chunk, "front", front) for chunk in chunks]
    table_in = jnp.asarray(table if table.shape[0] else np.zeros((1, front), np.int32))
    place = jnp.stack([(me % per_stage) * own, first_row]).astype(jnp.int32)

    lh, ll, ih, il, xh, xl, tops, owned = ([] for _ in range(8))
    for q in range(stages):
        used = [gathered[0]]
        for rnd in range(table.shape[0]):
            needed = any(
                c >= 0 and max(f, c) // per_stage == q for f, c in enumerate(table[rnd])
            )
            used.append(gathered[rnd + 1] if needed else [])
        counts = [len(u) for u in used]
        flat = [x for u in used for x in u]
        operands = (
            [owners, table_in, place]
            + flat
            + lh + ll + ih + il + xh + xl
            + [coupling[:, q * width : (q + 1) * width], pick]
        )
        deep = (q + 1) * width
        out = vmem_call(
            functools.partial(
                lambda *refs, q, counts: child_stage(q, width, own, front, cap, counts, refs),
                q=q,
                counts=counts,
            ),
            [
                shaped((width, deep), BF16),
                shaped((width, deep), BF16),
                shaped((width, width), BF16),
                shaped((width, width), BF16),
                shaped((own, width), BF16),
                shaped((own, width), BF16),
                shaped((cap, width), F32),
                shaped((own, deep), F32),
            ],
            [True] * 3 + [False] * (len(operands) - 3),
            [pltpu.VMEM((width, deep), F32), pltpu.VMEM((width, width), F32)],
        )(*operands)
        for held, new in zip((lh, ll, ih, il, xh, xl, tops, owned), out, strict=True):
            held.append(new)

    x_own = jnp.concatenate([h.astype(F32) + l.astype(F32) for h, l in zip(xh, xl, strict=True)], axis=1)
    lower_rows = jnp.zeros((own, total), F32)
    for q in range(stages):
        padded = jnp.pad(owned[q], ((0, 0), (0, total - (q + 1) * width)))
        lower_rows = jnp.where(me // per_stage == q, padded, lower_rows)

    slots = [x for top in tops for x in ring_gather(top, "front", front)]
    con, squares = vmem_call(
        lambda *refs: cross_kernel(stages, own, cap, sources, front, refs),
        [
            shaped((own, sources * cap), F32),
            shaped((blocks * (blocks + 1) // 2, LANES, LANES), F32),
        ],
        [True] + [False] * (2 * stages + len(slots)),
        [pltpu.VMEM((sources * cap, total), BF16)] * 2,
    )(owners, *xh, *xl, *slots)

    block_rows = (first_row + jnp.arange(count)) // BLOCK
    row_mask = jnp.take(block_pattern, block_rows, axis=0).astype(F32)
    arrow = parent_arrow * jnp.repeat(row_mask, BLOCK, axis=1)
    piece = count // bulk
    part = arrow[:piece]
    for g in range(1, bulk):
        moved = lax.ppermute(arrow[g * piece : (g + 1) * piece], "bulk", [(0, g)])
        part = jnp.where(lax.axis_index("bulk") == g, moved, part)
    ring = ring_gather(part, "front", front)
    line = jnp.zeros((front, piece, pivots), F32)
    for k, value in enumerate(ring):
        line = lax.dynamic_update_index_in_dim(line, value, owners[k], 0)
    held, back = bulk_gather(line[:sources], "bulk", bulk)
    top = jnp.stack([held[b] for b in back], axis=1).reshape(pivots, pivots)

    def unchanged(top, arrow, x_own):
        return top, arrow

    def landing_whole(top, arrow, x_own):
        slot = own_map - me * count
        hits = (slot[:, None] == jnp.arange(count)[None, :]).astype(F32)
        piece_rows = jnp.dot(hits.T, x_own, precision=HIGHEST_PRECISION)
        whole = lax.all_gather(piece_rows, "front", axis=0, tiled=True)[:pivots]
        reached = jnp.dot(x_own, whole.T, precision=HIGHEST_PRECISION)
        slot_index = own_map // count // front * count + own_map % count
        routing = (slot_index[:, None] == jnp.arange(bulk * count)[None, :]).astype(F32)
        added = lax.psum_scatter(
            jnp.dot(routing.T, reached, precision=HIGHEST_PRECISION),
            "bulk",
            scatter_dimension=0,
            tiled=True,
        )
        whole_square = lax.psum(jnp.dot(whole, whole.T, precision=HIGHEST_PRECISION), "bulk")
        return top - whole_square, arrow - added

    top, arrow = lax.cond(overflow, landing_whole, unchanged, top, arrow, x_own)

    held, back = bulk_gather(squares, "bulk", bulk)
    sq_all = jnp.stack([held[b] for b in back], axis=0)
    plh, pll, pih, pil, plow = vmem_call(
        lambda *refs: parent_kernel(bulk, blocks, width, refs),
        [
            shaped((pivots, pivots), BF16),
            shaped((pivots, pivots), BF16),
            shaped((pivots // width, width, width), BF16),
            shaped((pivots // width, width, width), BF16),
            shaped((pivots, pivots), F32),
        ],
        [False] * 3,
        [pltpu.VMEM((pivots, pivots), F32)],
    )(top, spread, sq_all)

    held, back = bulk_gather(con, "bulk", bulk)
    con_all = jnp.stack([held[b] for b in back], axis=0)
    (parent_rows,) = vmem_call(
        lambda *refs: rest_kernel(bulk, blocks, width, refs),
        [shaped((count, pivots), F32)],
        [True] + [False] * 8,
        [
            pltpu.VMEM((count, pivots), F32),
            pltpu.VMEM((count, pivots), BF16),
            pltpu.VMEM((count, pivots), BF16),
        ],
    )(place, arrow, route, con_all, spread, plh, pll, pih, pil)
    return (lower_rows[None], x_own[None], parent_rows)


def solution(mesh):
    placed = (
        P("bulk", "front", None),
        P("bulk", "front", None),
        P(("bulk", "front"), None),
        P("bulk", "front"),
        P(),
    )
    return jax.shard_map(
        on_device,
        mesh=mesh,
        in_specs=placed,
        out_specs=(P("bulk", "front", None), P("bulk", "front", None), P(("bulk", "front"), None)),
        check_vma=False,
    )
```

```python
import functools

import jax
import jax.numpy as jnp
import numpy as np
from jax import lax
from jax.experimental import pallas as pl
from jax.experimental.pallas import tpu as pltpu
from jax.sharding import PartitionSpec as P

BLOCK = 128
STAGE = 512
CAP = 128
LANES = 128
SUB = 8
VMEM_LIMIT = 60 << 20

HIGHEST_PRECISION = lax.Precision.HIGHEST
NT = (((1,), (1,)), ((), ()))
NN = (((1,), (0,)), ((), ()))
F32 = jnp.float32
BF16 = jnp.bfloat16


def split(x):
    high = x.astype(BF16)
    return high, (x - high.astype(F32)).astype(BF16)


def dot(a, b, dims):
    return lax.dot_general(a, b, dims, preferred_element_type=F32)


def dot3(a, b, dims):
    return dot(a[0], b[0], dims) + (dot(a[0], b[1], dims) + dot(a[1], b[0], dims))


def ds(start, size):
    return pl.ds(pl.multiple_of(start, size), size)


def tiles(rows, cols, body, tile=256):
    tr, tc = min(tile, rows), min(tile, cols)
    nr, nc = rows // tr, cols // tc

    def step(t, carry):
        body((t // nc) * tr, tr, (t % nc) * tc, tc)
        return carry

    lax.fori_loop(0, nr * nc, step, 0)


def lane(x, c):
    return jnp.broadcast_to(x[:, c : c + 1], x.shape)


def sub(x, r):
    return jnp.broadcast_to(x[r : r + 1, :], x.shape)


def tree_sum(terms):
    terms = list(terms)
    while len(terms) > 1:
        terms = [
            terms[i] + terms[i + 1] if i + 1 < len(terms) else terms[i]
            for i in range(0, len(terms), 2)
        ]
    return terms[0]


def small_inverse_factor(s):
    n = len(s)
    s = [list(row) for row in s]
    low = [[None] * n for _ in range(n)]
    inv_diag = [None] * n
    for j in range(n):
        inv_diag[j] = lax.rsqrt(s[j][j])
        for i in range(j + 1, n):
            low[i][j] = s[i][j] * inv_diag[j]
        for i in range(j + 1, n):
            for k in range(j + 1, i + 1):
                s[i][k] = s[i][k] - low[i][j] * low[k][j]
    inv = [[None] * n for _ in range(n)]
    for j in range(n):
        inv[j][j] = inv_diag[j]
        for i in range(j + 1, n):
            inv[i][j] = -tree_sum(low[i][k] * inv[k][j] for k in range(j, i)) * inv_diag[i]
    return inv


def factor_block(rows):
    n = len(rows)
    row_id = lax.broadcasted_iota(jnp.int32, (SUB, LANES), 0)
    col_id = lax.broadcasted_iota(jnp.int32, (SUB, LANES), 1)
    a = list(rows)
    e = [jnp.where(row_id + SUB * s == col_id, 1.0, 0.0).astype(F32) for s in range(n)]
    out = []
    for s in range(n):
        cols = [lane(a[s], SUB * s + r) for r in range(SUB)]
        inv = small_inverse_factor([[sub(cols[j], i) for j in range(i + 1)] for i in range(SUB)])
        ra = [sub(a[s], r) for r in range(SUB)]
        re = [sub(e[s], r) for r in range(SUB)]
        ua = [tree_sum(inv[r][q] * ra[q] for q in range(r + 1)) for r in range(SUB)]
        ue = [tree_sum(inv[r][q] * re[q] for q in range(r + 1)) for r in range(SUB)]
        done = ue[0]
        for r in range(1, SUB):
            done = jnp.where(row_id == r, ue[r], done)
        out.append(done)
        if s + 1 == n:
            break
        ya = [tree_sum(inv[r][q] * ua[r] for r in range(q, SUB)) for q in range(SUB)]
        ye = [tree_sum(inv[r][q] * ue[r] for r in range(q, SUB)) for q in range(SUB)]
        for i in range(s + 1, n):
            w = [lane(a[i], SUB * s + r) for r in range(SUB)]
            a[i] = a[i] - tree_sum(w[r] * ya[r] for r in range(SUB))
            e[i] = e[i] - tree_sum(w[r] * ye[r] for r in range(SUB))
    return out


def subtract_products(dst, rows, cols, ah, al, bh, bl, depth):
    if depth == 0:
        return

    def body(r, nr, c, nc):
        a = (ah[ds(r, nr), :depth], al[ds(r, nr), :depth])
        b = (bh[ds(c, nc), :depth], bl[ds(c, nc), :depth])
        dst[ds(r, nr), ds(c, nc)] = dst[ds(r, nr), ds(c, nc)] - dot3(a, b, NT)

    tiles(rows, cols, body)


def times_inverse(src, outh, outl, out_at, rows, width, invh, invl):
    def body(r, nr, c, nc):
        a = split(src[ds(r, nr), :])
        b = (invh[ds(c, nc), :], invl[ds(c, nc), :])
        high, low = split(dot3(a, b, NT))
        outh[ds(r, nr), pl.ds(pl.multiple_of(out_at + c, nc), nc)] = high
        outl[ds(r, nr), pl.ds(pl.multiple_of(out_at + c, nc), nc)] = low

    tiles(rows, width, body)


def factor_diagonal(s_ref, at, width, lh, ll, invh, invl):
    invh[...] = jnp.zeros(invh.shape, BF16)
    invl[...] = jnp.zeros(invl.shape, BF16)
    row_id = lax.broadcasted_iota(jnp.int32, (width, LANES), 0)
    col_id = lax.broadcasted_iota(jnp.int32, (width, LANES), 1)
    wide_id = lax.broadcasted_iota(jnp.int32, (LANES, width), 1)

    def panel(p, carry):
        first = p * LANES
        here = ds(first, LANES)
        block = [
            s_ref[pl.ds(pl.multiple_of(first + SUB * i, SUB), SUB), here]
            for i in range(LANES // SUB)
        ]
        inv = jnp.concatenate(factor_block(block), axis=0)
        inv2 = split(inv)
        solved = dot3(split(s_ref[:, here]), inv2, NT)
        solved = jnp.where(row_id >= col_id + first, solved, 0.0)
        high, low = split(solved)
        lh[:, pl.ds(pl.multiple_of(at + first, LANES), LANES)] = high
        ll[:, pl.ds(pl.multiple_of(at + first, LANES), LANES)] = low
        below = row_id >= first + LANES
        bh = jnp.where(below, high, jnp.zeros_like(high))
        bl = jnp.where(below, low, jnp.zeros_like(low))

        def update(c, carry2):
            cols = ds(c * LANES, LANES)
            s_ref[:, cols] = s_ref[:, cols] - dot3(
                (bh, bl),
                (
                    jnp.where(c > p, lh[cols, pl.ds(pl.multiple_of(at + first, LANES), LANES)], 0),
                    jnp.where(c > p, ll[cols, pl.ds(pl.multiple_of(at + first, LANES), LANES)], 0),
                ),
                NT,
            )
            return carry2

        lax.fori_loop(p + 1, width // LANES, update, 0)
        left = wide_id < first
        rh = lh[here, at : at + width]
        rl = ll[here, at : at + width]
        rh = jnp.where(left, rh, jnp.zeros_like(rh))
        rl = jnp.where(left, rl, jnp.zeros_like(rl))
        mixed = dot3((rh, rl), (invh[...], invl[...]), NN)
        row = -dot3(inv2, split(mixed), NN)
        high, low = split(row)
        invh[here, :] = high
        invl[here, :] = low
        invh[here, here] = inv2[0]
        invl[here, here] = inv2[1]
        return carry

    lax.fori_loop(0, width // LANES, panel, 0)


def vmem_call(body, out_shapes, in_kinds, scratch, cost=None):
    specs = [pl.BlockSpec(memory_space=pltpu.SMEM if k else pltpu.VMEM) for k in in_kinds]
    return pl.pallas_call(
        body,
        out_shape=out_shapes,
        in_specs=specs,
        out_specs=[pl.BlockSpec(memory_space=pltpu.VMEM)] * len(out_shapes),
        scratch_shapes=scratch,
        compiler_params=pltpu.CompilerParams(vmem_limit_bytes=VMEM_LIMIT),
        cost_estimate=cost,
    )


def shaped(shape, dtype):
    return jax.ShapeDtypeStruct(shape, dtype)


def send_plan(groups, per_stage):
    pairs = [
        (j, i)
        for i in range(groups)
        for j in range(i)
        if not (i == j + 1 and j % 2 == 0)
    ]
    pairs.sort(key=lambda pair: (pair[1] // per_stage, pair))
    taken = {}

    last = {}

    def place(pair, seen):
        for rnd in range(last[pair]):
            for dev in (pair[1], pair[0]):
                slot = (rnd, dev)
                if slot in seen:
                    continue
                seen.add(slot)
                if slot not in taken or place(taken[slot], seen):
                    taken[slot] = pair
                    return True
        return False

    limit = 1
    for pair in pairs:
        last[pair] = limit
        while not place(pair, set()):
            limit += 1
            last[pair] = limit
    rounds = 1 + max((slot[0] for slot in taken), default=-1)
    table = np.full((max(rounds, 1), groups), -1, np.int32)
    for (rnd, dev), (j, i) in taken.items():
        table[rnd, dev] = j if dev == i else i
    return table[:rounds]


def ring_order(groups):
    return [i for i in range(0, groups, 2)] + [i for i in range(groups - 1, 0, -2)]


def ring_gather(chunk, axis, groups):
    order = ring_order(groups)
    ahead = [(order[i], order[(i + 1) % groups]) for i in range(groups)]
    back = [(b, a) for a, b in ahead]
    out = [chunk]
    going, coming = chunk, chunk
    steps_ahead = groups // 2
    steps_back = groups - 1 - steps_ahead
    aheads, backs = [], []
    for step in range(steps_ahead):
        going = lax.ppermute(going, axis, ahead)
        aheads.append(going)
        if step < steps_back:
            coming = lax.ppermute(coming, axis, back)
            backs.append(coming)
    return out + aheads + backs


def slot_owners(axis, groups):
    order = np.array(ring_order(groups), np.int32)
    place = np.argsort(order)
    me = jnp.asarray(place)[lax.axis_index(axis)]
    steps_ahead = groups // 2
    steps_back = groups - 1 - steps_ahead
    shifts = [0] + [-s for s in range(1, steps_ahead + 1)] + list(range(1, steps_back + 1))
    return jnp.asarray(order)[(me + jnp.asarray(shifts, jnp.int32)) % groups].astype(jnp.int32)


def direct_gather(x, axis, groups, sources):
    moved = [
        lax.ppermute(x, axis, [(s, (s + k) % groups) for s in range(sources)])
        for k in range(1, groups)
    ]
    return [x] + moved


def bulk_gather(x, axis, size):
    held = {0: x}
    step = size // 2
    while step:
        for mask in list(held):
            held[mask | step] = lax.ppermute(held[mask], axis, [(i, i ^ step) for i in range(size)])
        step //= 2
    return [held[m] for m in range(size)]


def after(x, dep):
    return lax.optimization_barrier((x, dep))[0]


def child_stage(q, width, own, groups, early, chunk_counts, refs):
    per_stage = width // own
    refs = list(refs)

    def take(count):
        out, refs[:count] = refs[:count], []
        return out

    (owner_ref, table_ref, place_ref) = take(3)
    chunks = [take(count) for count in chunk_counts]
    prev_lh, prev_ll, prev_ih, prev_il, prev_xh, prev_xl = (take(q) for _ in range(6))
    (b_ref,) = take(1)
    (lh, ll, invh, invl, xh, xl, own_ref) = take(7)
    (a_ref, s_ref) = take(2)
    first_group = q * per_stage

    def block(rnd, k):
        if rnd <= early:
            return chunks[rnd][k][...]
        return chunks[rnd][0][k * own : (k + 1) * own, :]

    for k in range(groups):
        f = owner_ref[k]

        @pl.when(f // per_stage == q)
        def _(f=f, k=k):
            chunk = chunks[0][k]
            at = (f - first_group) * own
            a_ref[ds(at, own), ds(f * own, own)] = chunk[:, :own]
            half = own // 2
            odd = f % 2
            row = (f - odd + 1 - first_group) * own + odd * half
            a_ref[ds(row, half), ds((f - odd) * own, own)] = chunk[:, own:].T

    for rnd in range(1, len(chunks)):
        if not chunks[rnd]:
            continue
        for k in range(groups):
            f = owner_ref[k] if rnd <= early else k
            c = table_ref[rnd - 1, f]
            high = jnp.maximum(f, c)
            low = jnp.minimum(f, c)
            mine = jnp.logical_and(c >= 0, high // per_stage == q)
            row = jnp.clip((high - first_group) * own, 0, width - own)
            col = jnp.clip(low * own, 0, (q + 1) * width - own)

            @pl.when(jnp.logical_and(mine, f > c))
            def _(rnd=rnd, k=k, row=row, col=col):
                a_ref[ds(row, own), ds(col, own)] = block(rnd, k)

            @pl.when(jnp.logical_and(mine, f < c))
            def _(rnd=rnd, k=k, row=row, col=col):
                a_ref[ds(row, own), ds(col, own)] = block(rnd, k).T

    for j in range(q):
        part = a_ref.at[:, j * width : (j + 1) * width]
        subtract_products(part, width, width, lh, ll, prev_lh[j], prev_ll[j], j * width)
        times_inverse(part, lh, ll, j * width, width, width, prev_ih[j], prev_il[j])
    s_ref[...] = a_ref[:, q * width : (q + 1) * width]
    subtract_products(s_ref, width, width, lh, ll, lh, ll, q * width)
    factor_diagonal(s_ref, q * width, width, lh, ll, invh, invl)

    rest = s_ref.at[:own, :]
    rest[...] = b_ref[...]
    for j in range(q):
        part = slice(j * width, (j + 1) * width)

        def body(r, nr, c, nc, j=j, part=part):
            a = (prev_xh[j][ds(r, nr), :], prev_xl[j][ds(r, nr), :])
            b = (lh[ds(c, nc), part], ll[ds(c, nc), part])
            rest[ds(r, nr), ds(c, nc)] = rest[ds(r, nr), ds(c, nc)] - dot3(a, b, NT)

        tiles(own, width, body)
    times_inverse(rest, xh, xl, 0, own, width, invh, invl)
    at = place_ref[0]
    own_ref[...] = lh[ds(at, own), :].astype(F32) + ll[ds(at, own), :].astype(F32)


def cross_kernel(stages, cap, sources, groups, refs):
    refs = list(refs)

    def take(count):
        out, refs[:count] = refs[:count], []
        return out

    (raw_ref,) = take(1)
    lh, ll, ih, il, xh, xl = (take(stages) for _ in range(6))
    con_ref, sq_ref = take(2)
    t_ref, th, tl = take(3)
    own, width = xh[0].shape
    total = sources * cap
    share = raw_ref.shape[0] // groups
    for f in range(groups):
        at = (f % sources) * cap + (f // sources) * share
        t_ref[at : at + share, :] = raw_ref[f * share : (f + 1) * share, :]
    for q in range(stages):
        part = t_ref.at[:, q * width : (q + 1) * width]
        subtract_products(part, total, width, th, tl, lh[q], ll[q], q * width)
        times_inverse(part, th, tl, q * width, total, width, ih[q], il[q])

    for c in range(total // LANES):
        rows = slice(c * LANES, (c + 1) * LANES)
        acc = jnp.zeros((own, LANES), F32)
        for q in range(stages):
            cols = slice(q * width, (q + 1) * width)
            acc = acc + dot3((xh[q][...], xl[q][...]), (th[rows, cols], tl[rows, cols]), NT)
        con_ref[:, rows] = acc

    def square(t, carry):
        i, j = carry
        a = (th[ds(i * LANES, LANES), :], tl[ds(i * LANES, LANES), :])
        b = (th[ds(j * LANES, LANES), :], tl[ds(j * LANES, LANES), :])
        sq_ref[t] = dot3(a, b, NT)
        end = j == i
        return (jnp.where(end, i + 1, i), jnp.where(end, 0, j + 1))

    blocks = total // LANES
    lax.fori_loop(0, blocks * (blocks + 1) // 2, square, (jnp.int32(0), jnp.int32(0)))


def parent_kernel(children, blocks, width, refs):
    refs = list(refs)
    place_ref, spread_ref = refs[:2]
    tops, squares = refs[2 : 2 + children], refs[2 + children : 2 + 2 * children]
    lh, ll, invh, invl, lower, s_ref, top_ref = refs[2 + 2 * children :]
    pivots = lh.shape[0]
    dense = pivots // blocks
    sources, piece, _ = tops[0].shape
    for m in range(children):
        g = place_ref[2] ^ m
        for s in range(sources):
            top_ref[ds(s * (children * piece) + g * piece, piece), :] = tops[m][s]
    for i in range(blocks):
        for j in range(i + 1):
            at = i * (i + 1) // 2 + j
            parts = []
            for c in range(children):
                left = spread_ref[i, :, c * LANES : (c + 1) * LANES]
                high, low = split(squares[c][at])
                parts.append(dot(left, high, NN) + dot(left, low, NN))
            high, low = split(jnp.concatenate(parts, axis=1))
            right = spread_ref[j]
            rows = slice(i * dense, (i + 1) * dense)
            cols = slice(j * dense, (j + 1) * dense)
            s_ref[rows, cols] = top_ref[rows, cols] - (
                dot(high, right, NT) + dot(low, right, NT)
            )
    for q in range(pivots // width):
        rows = slice(q * width, (q + 1) * width)
        lhq, llq = lh.at[rows, :], ll.at[rows, :]
        if q + 1 < pivots // width:
            lhq[:, (q + 1) * width :] = jnp.zeros((width, pivots - (q + 1) * width), BF16)
            llq[:, (q + 1) * width :] = jnp.zeros((width, pivots - (q + 1) * width), BF16)
        for j in range(q):
            part = s_ref.at[rows, j * width : (j + 1) * width]
            cut = slice(j * width, (j + 1) * width)
            subtract_products(part, width, width, lhq, llq, lh.at[cut, :], ll.at[cut, :], j * width)
            times_inverse(part, lhq, llq, j * width, width, width, invh.at[j], invl.at[j])
        part = s_ref.at[rows, q * width : (q + 1) * width]
        subtract_products(part, width, width, lhq, llq, lhq, llq, q * width)
        factor_diagonal(part, q * width, width, lhq, llq, invh.at[q], invl.at[q])
    lower[...] = lh[...].astype(F32) + ll[...].astype(F32)


def rest_kernel(children, blocks, width, refs):
    refs = list(refs)
    place_ref, rows_ref, route_ref, spread_ref = refs[:4]
    con_refs = refs[4 : 4 + children]
    lh, ll, invh, invl, out_ref, s_ref, xh, xl = refs[4 + children :]
    pivots = lh.shape[0]
    count = rows_ref.shape[0]
    dense = pivots // blocks
    at = place_ref[1]

    @pl.when(at < pivots)
    def _():
        row = ds(jnp.minimum(at, pivots - count), count)
        out_ref[...] = lh[row, :].astype(F32) + ll[row, :].astype(F32)

    @pl.when(at >= pivots)
    def _():
        routed = []
        for c in range(children):
            high, low = split(con_refs[c][...])
            route = route_ref[c]
            routed.append(split(dot(route, high, NN) + dot(route, low, NN)))
        for b in range(blocks):
            lanes = slice(b * LANES, (b + 1) * LANES)
            high = jnp.concatenate([routed[c][0][:, lanes] for c in range(children)], axis=1)
            low = jnp.concatenate([routed[c][1][:, lanes] for c in range(children)], axis=1)
            right = spread_ref[b]
            cols = slice(b * dense, (b + 1) * dense)
            s_ref[:, cols] = rows_ref[:, cols] - (dot(high, right, NT) + dot(low, right, NT))
        for q in range(pivots // width):
            cut = slice(q * width, (q + 1) * width)
            part = s_ref.at[:, cut]
            subtract_products(part, count, width, xh, xl, lh.at[cut, :], ll.at[cut, :], q * width)
            times_inverse(part, xh, xl, q * width, count, width, invh.at[q], invl.at[q])
        out_ref[...] = xh[...].astype(F32) + xl[...].astype(F32)


def on_device(child_pivot, child_coupling, parent_arrow, row_map, block_pattern):
    front = lax.axis_size("front")
    bulk = lax.axis_size("bulk")
    me = lax.axis_index("front")
    mine = child_pivot[0]
    coupling = child_coupling[0]
    own, total = mine.shape
    count, pivots = parent_arrow.shape
    width = min(STAGE, total)
    stages = total // width
    per_stage = width // own
    first_row = (lax.axis_index("bulk") * front + me) * count
    sources = pivots // count
    cap = min(CAP, count, own)
    blocks = sources * cap // LANES

    table = send_plan(front, per_stage)
    rounds = table.shape[0]
    early = max(
        (r + 1 for r in range(rounds) for f, c in enumerate(table[r]) if c >= 0 and max(f, c) // per_stage == 1),
        default=0,
    )
    half = own // 2
    own_block = lax.dynamic_slice_in_dim(mine, me * own, own, 1)
    even = lax.dynamic_slice_in_dim(mine, jnp.minimum(me + 1, front - 1) * own, half, 1)
    odd = lax.dynamic_slice_in_dim(mine[half:], jnp.maximum(me - 1, 0) * own, own, 1).T
    chunks = [jnp.concatenate([own_block, jnp.where(me % 2 == 0, even, odd)], axis=1)]
    for rnd in range(rounds):
        col = jnp.maximum(jnp.asarray(table[rnd])[me], 0)
        chunks.append(lax.dynamic_slice_in_dim(mine, col * own, own, 1))
    owners = slot_owners("front", front)
    gathered = []
    for rnd in range(early + 1):
        chunk = chunks[rnd] if rnd == 0 else after(chunks[rnd], gathered[-1][-1])
        gathered.append(ring_gather(chunk, "front", front))
    started = gathered[0][-1]
    late = started
    if early < rounds:
        late = after(jnp.concatenate(chunks[early + 1 :], axis=1), started)
        late = lax.all_gather(late, "front", axis=0, tiled=True)
        for rnd in range(rounds - early):
            gathered.append([late[:, rnd * own : (rnd + 1) * own]])
    table_in = jnp.asarray(table if rounds else np.zeros((1, front), np.int32))
    bulk_me = lax.axis_index("bulk")
    place = jnp.stack([(me % per_stage) * own, first_row, bulk_me]).astype(jnp.int32)

    own_map = row_map[0]
    own_lands = own_map < pivots
    own_rank = jnp.where(own_lands, jnp.cumsum(own_lands.astype(jnp.int32)) - 1, -1)
    pick = (own_rank[None, :] == jnp.arange(cap)[:, None]).astype(F32)
    compact = jnp.dot(pick, coupling, precision=HIGHEST_PRECISION)
    spreads = front // sources
    share = cap // spreads
    part = compact[:share]
    for k in range(1, spreads):
        moved = lax.ppermute(
            compact[k * share : (k + 1) * share],
            "front",
            [(s, s + k * sources) for s in range(sources)],
        )
        part = jnp.where(me // sources == k, moved, part)
    raw_landing = lax.all_gather(after(part, late), "front", axis=0, tiled=True)

    block_rows = (first_row + jnp.arange(count)) // BLOCK
    row_mask = jnp.take(block_pattern, block_rows, axis=0).astype(F32)
    arrow = parent_arrow * jnp.repeat(row_mask, BLOCK, axis=1)
    piece = count // bulk
    part = arrow[:piece]
    for g in range(1, bulk):
        moved = lax.ppermute(arrow[g * piece : (g + 1) * piece], "bulk", [(0, g)])
        part = jnp.where(bulk_me == g, moved, part)
    slots = direct_gather(after(part, gathered[early][-1]), "front", front, sources)
    stacked = jnp.stack(slots)
    line = jnp.stack(
        [lax.dynamic_index_in_dim(stacked, (me - s) % front, 0, False) for s in range(sources)]
    )

    my_maps = jnp.stack(ring_gather(after(own_map, started), "front", front))
    ordered = jnp.zeros((front, own), jnp.int32)
    for k in range(front):
        ordered = lax.dynamic_update_index_in_dim(ordered, my_maps[k], owners[k], 0)
    maps = jnp.stack(bulk_gather(ordered, "bulk", bulk))
    lands = maps[:, :sources] < pivots
    rank = jnp.cumsum(lands.astype(jnp.int32), axis=2) - 1
    overflow = jnp.any(rank[:, :, -1] >= cap)
    chosen = jnp.where(lands, rank, -1)[:, :, None, :] == jnp.arange(cap)[:, None]
    target = jnp.max(jnp.where(chosen, maps[:, :sources, None, :], -1), axis=3)
    target = jnp.where(overflow, -1, target).reshape(bulk, blocks, LANES)
    dense = pivots // blocks
    rows_of = (jnp.arange(blocks)[:, None] * dense + jnp.arange(dense)[None, :])[:, :, None, None]
    spread = (jnp.transpose(target, (1, 0, 2))[:, None] == rows_of).astype(BF16)
    spread = spread.reshape(blocks, dense, bulk * LANES)
    route = (
        lax.dynamic_index_in_dim(maps, me, 1, False)[:, None, :]
        == (first_row + jnp.arange(count))[None, :, None]
    ).astype(BF16)

    lh, ll, ih, il, xh, xl, owned = ([] for _ in range(7))
    for q in range(stages):
        used = [gathered[0]]
        for rnd in range(rounds):
            needed = any(
                c >= 0 and max(f, c) // per_stage == q for f, c in enumerate(table[rnd])
            )
            used.append(gathered[rnd + 1] if needed else [])
        counts = [len(u) for u in used]
        flat = [x for u in used for x in u]
        operands = (
            [owners, table_in, place]
            + flat
            + lh + ll + ih + il + xh + xl
            + [coupling[:, q * width : (q + 1) * width]]
        )
        deep = (q + 1) * width
        out = vmem_call(
            functools.partial(
                lambda *refs, q, counts: child_stage(q, width, own, front, early, counts, refs),
                q=q,
                counts=counts,
            ),
            [
                shaped((width, deep), BF16),
                shaped((width, deep), BF16),
                shaped((width, width), BF16),
                shaped((width, width), BF16),
                shaped((own, width), BF16),
                shaped((own, width), BF16),
                shaped((own, deep), F32),
            ],
            [True] * 3 + [False] * (len(operands) - 3),
            [pltpu.VMEM((width, deep), F32), pltpu.VMEM((width, width), F32)],
            pl.CostEstimate(flops=30_000_000_000, bytes_accessed=1 << 24, transcendentals=0),
        )(*operands)
        for held, new in zip((lh, ll, ih, il, xh, xl, owned), out, strict=True):
            held.append(new)

    x_own = jnp.concatenate([h.astype(F32) + l.astype(F32) for h, l in zip(xh, xl, strict=True)], axis=1)
    lower_rows = jnp.zeros((own, total), F32)
    for q in range(stages):
        padded = jnp.pad(owned[q], ((0, 0), (0, total - (q + 1) * width)))
        lower_rows = jnp.where(me // per_stage == q, padded, lower_rows)

    con, squares = vmem_call(
        lambda *refs: cross_kernel(stages, cap, sources, front, refs),
        [
            shaped((own, sources * cap), F32),
            shaped((blocks * (blocks + 1) // 2, LANES, LANES), F32),
        ],
        [False] * (1 + 6 * stages),
        [pltpu.VMEM((sources * cap, total), F32)] + [pltpu.VMEM((sources * cap, total), BF16)] * 2,
    )(raw_landing, *lh, *ll, *ih, *il, *xh, *xl)

    def unchanged(lines, arrow, x_own):
        return lines, arrow

    def landing_whole(lines, arrow, x_own):
        slot = own_map - me * count
        hits = (slot[:, None] == jnp.arange(count)[None, :]).astype(F32)
        piece_rows = jnp.dot(hits.T, x_own, precision=HIGHEST_PRECISION)
        whole = lax.all_gather(piece_rows, "front", axis=0, tiled=True)[:pivots]
        reached = jnp.dot(x_own, whole.T, precision=HIGHEST_PRECISION)
        slot_index = own_map // count // front * count + own_map % count
        routing = (slot_index[:, None] == jnp.arange(bulk * count)[None, :]).astype(F32)
        added = lax.psum_scatter(
            jnp.dot(routing.T, reached, precision=HIGHEST_PRECISION),
            "bulk",
            scatter_dimension=0,
            tiled=True,
        )
        square = lax.psum(jnp.dot(whole, whole.T, precision=HIGHEST_PRECISION), "bulk")
        square = square.reshape(sources, bulk, piece, pivots)
        changed = [
            lines[m] - lax.dynamic_index_in_dim(square, bulk_me ^ m, 1, False) for m in range(bulk)
        ]
        return changed, arrow - added

    lines = bulk_gather(line, "bulk", bulk)
    lines, arrow = lax.cond(overflow, landing_whole, unchanged, lines, arrow, x_own)

    all_squares = bulk_gather(squares, "bulk", bulk)
    all_con = bulk_gather(after(con, all_squares[-1]), "bulk", bulk)
    plh, pll, pih, pil, plow = vmem_call(
        lambda *refs: parent_kernel(bulk, blocks, width, refs),
        [
            shaped((pivots, pivots), BF16),
            shaped((pivots, pivots), BF16),
            shaped((pivots // width, width, width), BF16),
            shaped((pivots // width, width, width), BF16),
            shaped((pivots, pivots), F32),
        ],
        [True] + [False] * (1 + 2 * bulk),
        [pltpu.VMEM((pivots, pivots), F32)] * 2,
        pl.CostEstimate(flops=60_000_000_000, bytes_accessed=1 << 24, transcendentals=0),
    )(place, spread, *lines, *all_squares)

    (parent_rows,) = vmem_call(
        lambda *refs: rest_kernel(bulk, blocks, width, refs),
        [shaped((count, pivots), F32)],
        [True] + [False] * (7 + bulk),
        [
            pltpu.VMEM((count, pivots), F32),
            pltpu.VMEM((count, pivots), BF16),
            pltpu.VMEM((count, pivots), BF16),
        ],
    )(place, arrow, route, spread, *all_con, plh, pll, pih, pil)
    return (lower_rows[None], x_own[None], parent_rows)


def solution(mesh):
    placed = (
        P("bulk", "front", None),
        P("bulk", "front", None),
        P(("bulk", "front"), None),
        P("bulk", "front"),
        P(),
    )
    return jax.shard_map(
        on_device,
        mesh=mesh,
        in_specs=placed,
        out_specs=(P("bulk", "front", None), P("bulk", "front", None), P(("bulk", "front"), None)),
        check_vma=False,
    )
```

```python
import functools

import jax
import jax.numpy as jnp
import numpy as np
from jax import lax
from jax.experimental import pallas as pl
from jax.experimental.pallas import tpu as pltpu
from jax.sharding import PartitionSpec as P

BLOCK = 128
STAGE = 512
CAP = 128
LANES = 128
SUB = 8
VMEM_LIMIT = 60 << 20

HIGHEST_PRECISION = lax.Precision.HIGHEST
NT = (((1,), (1,)), ((), ()))
NN = (((1,), (0,)), ((), ()))
F32 = jnp.float32
BF16 = jnp.bfloat16


def split(x):
    high = x.astype(BF16)
    return high, (x - high.astype(F32)).astype(BF16)


def dot(a, b, dims):
    return lax.dot_general(a, b, dims, preferred_element_type=F32)


def dot3(a, b, dims):
    return dot(a[0], b[0], dims) + (dot(a[0], b[1], dims) + dot(a[1], b[0], dims))


def ds(start, size):
    return pl.ds(pl.multiple_of(start, size), size)


def tiles(rows, cols, body, tile=256):
    tr, tc = min(tile, rows), min(tile, cols)
    nr, nc = rows // tr, cols // tc

    def step(t, carry):
        body((t // nc) * tr, tr, (t % nc) * tc, tc)
        return carry

    lax.fori_loop(0, nr * nc, step, 0)


def lane(x, c):
    return jnp.broadcast_to(x[:, c : c + 1], x.shape)


def sub(x, r):
    return jnp.broadcast_to(x[r : r + 1, :], x.shape)


def tree_sum(terms):
    terms = list(terms)
    while len(terms) > 1:
        terms = [
            terms[i] + terms[i + 1] if i + 1 < len(terms) else terms[i]
            for i in range(0, len(terms), 2)
        ]
    return terms[0]


def invert_small(s):
    n = len(s)
    s = list(s)
    row_id = lax.broadcasted_iota(jnp.int32, (SUB, LANES), 0)
    m = [None] * n
    for p in range(0, n, 2):
        q = p + 1
        a, b, d = sub(s[p], p), sub(s[q], p), sub(s[q], q)
        det = a * d - b * b
        scale = 1.0 / det
        ra = lax.rsqrt(a)
        rq = lax.rsqrt(det) * (a * ra)
        ba = b * ra * ra
        at_p, at_q = row_id == p, row_id == q
        sp, sq = s[p], s[q]
        fp, fq = (sp * d - sq * b) * scale, (sq * a - sp * b) * scale
        for k in range(n):
            if k in (p, q):
                continue
            u, v = sub(s[k], p), sub(s[k], q)
            if k < p:
                m[k] = jnp.where(at_p, -(u * ra), jnp.where(at_q, (u * ba - v) * rq, m[k]))
            s[k] = jnp.where(at_p, sub(fp, k), jnp.where(at_q, sub(fq, k), s[k] - (fp * u + fq * v)))
        s[p] = jnp.where(at_p, -(d * scale), jnp.where(at_q, b * scale, fp))
        s[q] = jnp.where(at_q, -(a * scale), jnp.where(at_p, b * scale, fq))
        m[p] = jnp.where(at_p, ra, jnp.where(at_q, -(ba * rq), 0.0))
        m[q] = jnp.where(at_q, rq, 0.0)
    return s, m


def factor_block(rows):
    n = len(rows)
    row_id = lax.broadcasted_iota(jnp.int32, (SUB, LANES), 0)
    lane_id = lax.broadcasted_iota(jnp.int32, (SUB, LANES), 1)
    a = list(rows)
    out = []
    for s in range(n):
        here = jnp.logical_and(lane_id >= SUB * s, lane_id < SUB * (s + 1))
        cols = [lane(a[s], SUB * s + r) for r in range(SUB)]
        r = jnp.where(here, jnp.where(row_id + SUB * s == lane_id, 1.0, 0.0), a[s])
        rb = [sub(r, q) for q in range(SUB)]
        t, m = invert_small(cols)
        v = tree_sum(m[q] * rb[q] for q in range(SUB))
        out.append(jnp.where(lane_id < SUB * (s + 1), v, 0.0))
        if s + 1 == n:
            break
        y = tree_sum(t[q] * rb[q] for q in range(SUB))
        yb = [sub(y, q) for q in range(SUB)]
        for i in range(s + 1, n):
            w = [lane(a[i], SUB * s + q) for q in range(SUB)]
            a[i] = jnp.where(here, 0.0, a[i]) + tree_sum(w[q] * yb[q] for q in range(SUB))
    return out


def subtract_products(dst, rows, cols, ah, al, bh, bl, depth):
    if depth == 0:
        return

    def body(r, nr, c, nc):
        a = (ah[ds(r, nr), :depth], al[ds(r, nr), :depth])
        b = (bh[ds(c, nc), :depth], bl[ds(c, nc), :depth])
        dst[ds(r, nr), ds(c, nc)] = dst[ds(r, nr), ds(c, nc)] - dot3(a, b, NT)

    tiles(rows, cols, body)


def times_inverse(src, outh, outl, out_at, rows, width, invh, invl):
    def body(r, nr, c, nc):
        a = split(src[ds(r, nr), :])
        b = (invh[ds(c, nc), :], invl[ds(c, nc), :])
        high, low = split(dot3(a, b, NT))
        outh[ds(r, nr), pl.ds(pl.multiple_of(out_at + c, nc), nc)] = high
        outl[ds(r, nr), pl.ds(pl.multiple_of(out_at + c, nc), nc)] = low

    tiles(rows, width, body)


def clear_inverse(invh, invl):
    invh[...] = jnp.zeros(invh.shape, BF16)
    invl[...] = jnp.zeros(invl.shape, BF16)


def inverse_row(r, at, width, lh, ll, invh, invl):
    here = ds(r * LANES, LANES)
    left = lax.broadcasted_iota(jnp.int32, (LANES, width), 1) < r * LANES
    none = jnp.zeros((LANES, width), BF16)
    low = tuple(jnp.where(left, ref[here, at : at + width], none) for ref in (lh, ll))
    mixed = split(dot3(low, (invh[...], invl[...]), NN))
    high, low = split(-dot3((invh[here, here], invl[here, here]), mixed, NN))
    invh[here, :] = jnp.where(left, high, invh[here, :])
    invl[here, :] = jnp.where(left, low, invl[here, :])


def factor_panels(start, stop, s_ref, at, width, lh, ll, invh, invl, job=None):
    row_id = lax.broadcasted_iota(jnp.int32, (width, LANES), 0)
    col_id = lax.broadcasted_iota(jnp.int32, (width, LANES), 1)
    none = jnp.zeros((width, LANES), BF16)
    last = width // LANES - 1

    def panel(p, carry):
        first = p * LANES
        here = ds(first, LANES)
        block = [
            s_ref[pl.ds(pl.multiple_of(first + SUB * i, SUB), SUB), here]
            for i in range(LANES // SUB)
        ]
        before = jnp.maximum(p - 1, 0)
        done = ds(at + before * LANES, LANES)
        later = jnp.logical_and(row_id >= first + LANES, p > 0)
        old = tuple(jnp.where(later, ref[:, done], none) for ref in (lh, ll))
        for c in range(1, last + 1):
            cols = slice(c * LANES, (c + 1) * LANES)
            some = (old[0][cols], old[1][cols])
            s_ref[c * LANES :, cols] = s_ref[c * LANES :, cols] - dot3(
                (old[0][c * LANES :], old[1][c * LANES :]), some, NT
            )
        inverse_row(before, at, width, lh, ll, invh, invl)
        if job is not None:
            job(p)

        inv = split(jnp.concatenate(factor_block(block), axis=0))
        invh[here, here] = inv[0]
        invl[here, here] = inv[1]
        solved = dot3(split(s_ref[:, here]), inv, NT)
        high, low = split(jnp.where(row_id >= col_id + first, solved, 0.0))
        lh[:, ds(at + first, LANES)] = high
        ll[:, ds(at + first, LANES)] = low
        below = row_id >= first + LANES
        following = ds(jnp.minimum(p + 1, last) * LANES, LANES)
        some = (lh[following, ds(at + first, LANES)], ll[following, ds(at + first, LANES)])
        s_ref[:, following] = s_ref[:, following] - dot3(
            (jnp.where(below, high, none), jnp.where(below, low, none)), some, NT
        )
        return carry

    lax.fori_loop(start, stop, panel, 0)
    if stop == last + 1:
        inverse_row(last, at, width, lh, ll, invh, invl)


def solve_some(rows, src, q, width, xh, xl, l_rows, inv):
    part = src
    if q > 0:
        deep = q * width
        part = part - dot3(
            (xh[rows, :deep], xl[rows, :deep]), (l_rows[0][:, :deep], l_rows[1][:, :deep]), NT
        )
    high, low = split(dot3(split(part), (inv[0][...], inv[1][...]), NT))
    xh[rows, q * width : (q + 1) * width] = high
    xl[rows, q * width : (q + 1) * width] = low


def vmem_call(body, out_shapes, in_kinds, scratch, cost=None, aliases=None):
    specs = [pl.BlockSpec(memory_space=pltpu.SMEM if k else pltpu.VMEM) for k in in_kinds]
    return pl.pallas_call(
        body,
        out_shape=out_shapes,
        in_specs=specs,
        out_specs=[pl.BlockSpec(memory_space=pltpu.VMEM)] * len(out_shapes),
        scratch_shapes=scratch,
        compiler_params=pltpu.CompilerParams(vmem_limit_bytes=VMEM_LIMIT),
        cost_estimate=cost,
        input_output_aliases=aliases or {},
    )


def shaped(shape, dtype):
    return jax.ShapeDtypeStruct(shape, dtype)


def send_plan(groups, per_stage):
    pairs = [
        (j, i)
        for i in range(groups)
        for j in range(i)
        if not (i == j + 1 and j % 2 == 0)
    ]
    pairs.sort(key=lambda pair: (pair[1] // per_stage, pair))
    taken = {}

    last = {}

    def place(pair, seen):
        for rnd in range(last[pair]):
            for dev in (pair[1], pair[0]):
                slot = (rnd, dev)
                if slot in seen:
                    continue
                seen.add(slot)
                if slot not in taken or place(taken[slot], seen):
                    taken[slot] = pair
                    return True
        return False

    limit = 1
    for pair in pairs:
        last[pair] = limit
        while not place(pair, set()):
            limit += 1
            last[pair] = limit
    rounds = 1 + max((slot[0] for slot in taken), default=-1)
    table = np.full((max(rounds, 1), groups), -1, np.int32)
    for (rnd, dev), (j, i) in taken.items():
        table[rnd, dev] = j if dev == i else i
    return table[:rounds]


def ring_order(groups):
    return [i for i in range(0, groups, 2)] + [i for i in range(groups - 1, 0, -2)]


def ring_gather(chunk, axis, groups):
    order = ring_order(groups)
    ahead = [(order[i], order[(i + 1) % groups]) for i in range(groups)]
    back = [(b, a) for a, b in ahead]
    out = [chunk]
    going, coming = chunk, chunk
    steps_ahead = groups // 2
    steps_back = groups - 1 - steps_ahead
    aheads, backs = [], []
    for step in range(steps_ahead):
        going = lax.ppermute(going, axis, ahead)
        aheads.append(going)
        if step < steps_back:
            coming = lax.ppermute(coming, axis, back)
            backs.append(coming)
    return out + aheads + backs


class Ring:
    def __init__(self, chunk, axis, groups):
        order = ring_order(groups)
        self.axis = axis
        self.ahead = [(order[i], order[(i + 1) % groups]) for i in range(groups)]
        self.back = [(b, a) for a, b in self.ahead]
        self.steps = groups // 2
        self.steps_back = groups - 1 - self.steps
        self.own = chunk
        self.aheads, self.backs = [], []
        self.going = self.coming = chunk

    def advance(self, token):
        if len(self.aheads) < self.steps:
            self.going = lax.ppermute(self.going, self.axis, self.ahead)
            self.aheads.append(self.going)
            if len(self.backs) < self.steps_back:
                self.coming = lax.ppermute(self.coming, self.axis, self.back)
                self.backs.append(self.coming)
        return token

    def arrive(self, token, beside):
        token, self.going, self.coming, _ = lax.optimization_barrier((token, self.going, self.coming, beside))
        return token

    def finish(self):
        while len(self.aheads) < self.steps:
            self.advance(None)

    def slots(self):
        return [self.own] + self.aheads + self.backs


def slot_owners(axis, groups):
    order = np.array(ring_order(groups), np.int32)
    place = np.argsort(order)
    me = jnp.asarray(place)[lax.axis_index(axis)]
    steps_ahead = groups // 2
    steps_back = groups - 1 - steps_ahead
    shifts = [0] + [-s for s in range(1, steps_ahead + 1)] + list(range(1, steps_back + 1))
    return jnp.asarray(order)[(me + jnp.asarray(shifts, jnp.int32)) % groups].astype(jnp.int32)


def direct_gather(x, axis, groups, sources):
    moved = [
        lax.ppermute(x, axis, [(s, (s + k) % groups) for s in range(sources)])
        for k in range(1, groups)
    ]
    return [x] + moved


def bulk_gather(x, axis, size):
    held = {0: x}
    step = size // 2
    while step:
        for mask in list(held):
            held[mask | step] = lax.ppermute(held[mask], axis, [(i, i ^ step) for i in range(size)])
        step //= 2
    return [held[m] for m in range(size)]


def after(x, dep):
    return lax.optimization_barrier((x, dep))[0]


def assemble_rows(q, width, own, groups, owner_ref, table_ref, chunks, late_rounds, a_ref):
    per_stage = width // own
    first_group = q * per_stage
    for k in range(groups):
        f = owner_ref[k]

        @pl.when(f // per_stage == q)
        def _(f=f, k=k):
            chunk = chunks[0][k]
            at = (f - first_group) * own
            a_ref[ds(at, own), ds(f * own, own)] = chunk[:own, :own]
            half = own // 2
            odd = f % 2
            row = (f - odd + 1 - first_group) * own + odd * half
            a_ref[ds(row, half), ds((f - odd) * own, own)] = chunk[:own, own:].T

    sent = [(rnd, chunk, 0) for rnd, chunk in enumerate(chunks[1:-1]) if chunk]
    sent += [(rnd, chunks[-1], at * own) for at, rnd in late_rounds]
    for rnd, chunk, cut in sent:
        for k in range(groups):
            f = owner_ref[k]
            c = table_ref[rnd, f]
            high = jnp.maximum(f, c)
            low = jnp.minimum(f, c)
            mine = jnp.logical_and(c >= 0, high // per_stage == q)
            row = jnp.clip((high - first_group) * own, 0, width - own)
            col = jnp.clip(low * own, 0, (q + 1) * width - own)

            @pl.when(jnp.logical_and(mine, f > c))
            def _(chunk=chunk, cut=cut, k=k, row=row, col=col):
                a_ref[ds(row, own), ds(col, own)] = chunk[k][:, cut : cut + own]

            @pl.when(jnp.logical_and(mine, f < c))
            def _(chunk=chunk, cut=cut, k=k, row=row, col=col):
                a_ref[ds(row, own), ds(col, own)] = chunk[k][:, cut : cut + own].T


def child_stage(q, width, own, groups, late_rounds, counts, span, shapes, couples, landing, refs):
    start, stop = span
    panels = width // LANES
    refs = list(refs)

    def take(count):
        out, refs[:count] = refs[:count], []
        return out

    (place_ref,) = take(1)
    if start == 0:
        owner_ref, table_ref = take(2)
        chunks = [take(count) for count in counts]
    else:
        state = take(5)
    prev_lh, prev_ll, prev_ih, prev_il = (take(q) for _ in range(4))
    if couples:
        b_ref = take(1)[0]
        old_x = take(2) if q > 1 else None
    if landing:
        raw_ref = take(1)[0]
    s_out, lh, ll, invh, invl = take(5)
    if couples:
        xh, xl = take(2)
    if stop == panels:
        own_ref = take(1)[0]
    if landing:
        th, tl, sq_ref = take(3)
    if start == 0:
        a_ref = take(1)[0]
    if landing:
        t_ref = take(1)[0]

    if start == 0:
        assemble_rows(q, width, own, groups, owner_ref, table_ref, chunks, late_rounds, a_ref)
        for j in range(q):
            part = a_ref.at[:, j * width : (j + 1) * width]
            subtract_products(part, width, width, lh, ll, prev_lh[j], prev_ll[j], j * width)
            times_inverse(part, lh, ll, j * width, width, width, prev_ih[j], prev_il[j])
        s_out[...] = a_ref[:, q * width : (q + 1) * width]
        subtract_products(s_out, width, width, lh, ll, lh, ll, q * width)
        clear_inverse(invh, invl)
    else:
        for new, held in zip((s_out, lh, ll, invh, invl), state, strict=True):
            new[...] = held[...]
    if couples and q > 1:
        xh[:, : (q - 1) * width] = old_x[0][...]
        xl[:, : (q - 1) * width] = old_x[1][...]
    if landing:
        total, front, sources, cap = shapes
        share = cap * sources // front
        for f in range(front):
            at = (f % sources) * cap + (f // sources) * share
            t_ref[at : at + share, :] = raw_ref[f * share : (f + 1) * share, :]

    def job(p):
        if couples:
            some = own // (stop - start)
            rows = ds((p - start) * some, some)
            solve_some(
                rows, b_ref[rows, :], q - 1, width, xh, xl,
                (prev_lh[q - 1], prev_ll[q - 1]), (prev_ih[q - 1], prev_il[q - 1]),
            )
        if landing:
            some = total // (stop - start)
            rows = ds((p - start) * some, some)
            for j in range(q):
                solve_some(
                    rows, t_ref[rows, j * width : (j + 1) * width], j, width, th, tl,
                    (prev_lh[j], prev_ll[j]), (prev_ih[j], prev_il[j]),
                )

    factor_panels(start, stop, s_out, q * width, width, lh, ll, invh, invl, job)
    if stop == panels:
        at = place_ref[0]
        own_ref[...] = lh[ds(at, own), :].astype(F32) + ll[ds(at, own), :].astype(F32)
    if landing:
        part = t_ref.at[:, q * width : (q + 1) * width]
        subtract_products(part, total, width, th, tl, lh, ll, q * width)
        times_inverse(part, th, tl, q * width, total, width, invh, invl)

        def square(t, carry):
            i, j = carry
            a = (th[ds(i * LANES, LANES), :], tl[ds(i * LANES, LANES), :])
            b = (th[ds(j * LANES, LANES), :], tl[ds(j * LANES, LANES), :])
            sq_ref[t] = dot3(a, b, NT)
            end = j == i
            return (jnp.where(end, i + 1, i), jnp.where(end, 0, j + 1))

        blocks = total // LANES
        lax.fori_loop(0, blocks * (blocks + 1) // 2, square, (jnp.int32(0), jnp.int32(0)))


def own_kernel(first, stages, width, refs):
    refs = list(refs)

    def take(count):
        out, refs[:count] = refs[:count], []
        return out

    (b_ref,) = take(1)
    old_h, old_l = take(2) if first > 0 else (None, None)
    left = stages - first
    lh, ll, ih, il = (take(left) for _ in range(4))
    th, tl = take(2)
    x_ref, con_ref = take(2)
    xh, xl = take(2)
    own = b_ref.shape[0]
    if first > 0:
        xh[:, : first * width] = old_h[...]
        xl[:, : first * width] = old_l[...]
    for k in range(left):
        q = first + k
        for c in range(1):
            part = b_ref.at[:, k * width : (k + 1) * width]
            x_ref[:, q * width : (q + 1) * width] = part[...]
            part = x_ref.at[:, q * width : (q + 1) * width]
            subtract_products(part, own, width, xh, xl, lh[k], ll[k], q * width)
            times_inverse(part, xh, xl, q * width, own, width, ih[k], il[k])
    x_ref[...] = xh[...].astype(F32) + xl[...].astype(F32)

    def body(r, nr, c, nc):
        a = (xh[ds(r, nr), :], xl[ds(r, nr), :])
        b = (th[ds(c, nc), :], tl[ds(c, nc), :])
        con_ref[ds(r, nr), ds(c, nc)] = dot3(a, b, NT)

    tiles(own, con_ref.shape[1], body)


def parent_kernel(children, blocks, width, sources, refs):
    refs = list(refs)
    place_ref, spread_ref = refs[:2]
    tops, squares = refs[2 : 2 + children], refs[2 + children : 2 + 2 * children]
    lh, ll, invh, invl, lower, s_ref, top_ref = refs[2 + 2 * children :]
    pivots = lh.shape[0]
    dense = pivots // blocks
    groups, part_rows, _ = tops[0].shape
    spreads = groups // sources
    piece = part_rows * spreads
    for m in range(children):
        g = place_ref[2] ^ m
        for f in range(groups):
            at = (f % sources) * (children * piece) + g * piece + (f // sources) * part_rows
            top_ref[ds(at, part_rows), :] = tops[m][f]
    for i in range(blocks):
        for j in range(i + 1):
            at = i * (i + 1) // 2 + j
            parts = []
            for c in range(children):
                left = spread_ref[i, :, c * LANES : (c + 1) * LANES]
                high, low = split(squares[c][at])
                parts.append(dot(left, high, NN) + dot(left, low, NN))
            high, low = split(jnp.concatenate(parts, axis=1))
            right = spread_ref[j]
            rows = slice(i * dense, (i + 1) * dense)
            cols = slice(j * dense, (j + 1) * dense)
            s_ref[rows, cols] = top_ref[rows, cols] - (
                dot(high, right, NT) + dot(low, right, NT)
            )
    for q in range(pivots // width):
        rows = slice(q * width, (q + 1) * width)
        lhq, llq = lh.at[rows, :], ll.at[rows, :]
        if q + 1 < pivots // width:
            lhq[:, (q + 1) * width :] = jnp.zeros((width, pivots - (q + 1) * width), BF16)
            llq[:, (q + 1) * width :] = jnp.zeros((width, pivots - (q + 1) * width), BF16)
        for j in range(q):
            part = s_ref.at[rows, j * width : (j + 1) * width]
            cut = slice(j * width, (j + 1) * width)
            subtract_products(part, width, width, lhq, llq, lh.at[cut, :], ll.at[cut, :], j * width)
            times_inverse(part, lhq, llq, j * width, width, width, invh.at[j], invl.at[j])
        part = s_ref.at[rows, q * width : (q + 1) * width]
        subtract_products(part, width, width, lhq, llq, lhq, llq, q * width)
        clear_inverse(invh.at[q], invl.at[q])
        factor_panels(0, width // LANES, part, q * width, width, lhq, llq, invh.at[q], invl.at[q])
    lower[...] = lh[...].astype(F32) + ll[...].astype(F32)


def rest_kernel(children, blocks, width, refs):
    refs = list(refs)
    place_ref, rows_ref, route_ref, spread_ref = refs[:4]
    con_refs = refs[4 : 4 + children]
    lh, ll, invh, invl, out_ref, s_ref, xh, xl = refs[4 + children :]
    pivots = lh.shape[0]
    count = rows_ref.shape[0]
    dense = pivots // blocks
    at = place_ref[1]

    @pl.when(at < pivots)
    def _():
        row = ds(jnp.minimum(at, pivots - count), count)
        out_ref[...] = lh[row, :].astype(F32) + ll[row, :].astype(F32)

    @pl.when(at >= pivots)
    def _():
        routed = []
        for c in range(children):
            high, low = split(con_refs[c][...])
            route = route_ref[c]
            routed.append(split(dot(route, high, NN) + dot(route, low, NN)))
        for b in range(blocks):
            lanes = slice(b * LANES, (b + 1) * LANES)
            high = jnp.concatenate([routed[c][0][:, lanes] for c in range(children)], axis=1)
            low = jnp.concatenate([routed[c][1][:, lanes] for c in range(children)], axis=1)
            right = spread_ref[b]
            cols = slice(b * dense, (b + 1) * dense)
            s_ref[:, cols] = rows_ref[:, cols] - (dot(high, right, NT) + dot(low, right, NT))
        for q in range(pivots // width):
            cut = slice(q * width, (q + 1) * width)
            part = s_ref.at[:, cut]
            subtract_products(part, count, width, xh, xl, lh.at[cut, :], ll.at[cut, :], q * width)
            times_inverse(part, xh, xl, q * width, count, width, invh.at[q], invl.at[q])
        out_ref[...] = xh[...].astype(F32) + xl[...].astype(F32)


def on_device(child_pivot, child_coupling, parent_arrow, row_map, block_pattern):
    front = lax.axis_size("front")
    bulk = lax.axis_size("bulk")
    me = lax.axis_index("front")
    mine = child_pivot[0]
    coupling = child_coupling[0]
    own, total = mine.shape
    count, pivots = parent_arrow.shape
    width = min(STAGE, total)
    stages = total // width
    per_stage = width // own
    first_row = (lax.axis_index("bulk") * front + me) * count
    sources = pivots // count
    cap = min(CAP, count, own)
    blocks = sources * cap // LANES

    table = send_plan(front, per_stage)
    rounds = table.shape[0]
    bulk_me = lax.axis_index("bulk")
    early = max(
        (r + 1 for r in range(rounds) for f, c in enumerate(table[r]) if c >= 0 and max(f, c) // per_stage <= 1),
        default=0,
    )
    half = own // 2
    own_map = row_map[0]
    own_block = lax.dynamic_slice_in_dim(mine, me * own, own, 1)
    even = lax.dynamic_slice_in_dim(mine, jnp.minimum(me + 1, front - 1) * own, half, 1)
    odd = lax.dynamic_slice_in_dim(mine[half:], jnp.maximum(me - 1, 0) * own, own, 1).T
    head = jnp.concatenate([own_block, jnp.where(me % 2 == 0, even, odd)], axis=1)
    tail = jnp.pad(own_map.astype(F32)[None], ((0, SUB - 1), (0, half)))
    chunks = [jnp.concatenate([head, tail], axis=0)]
    for rnd in range(rounds):
        col = jnp.maximum(jnp.asarray(table[rnd])[me], 0)
        chunks.append(lax.dynamic_slice_in_dim(mine, col * own, own, 1))
    owners = slot_owners("front", front)
    gathered = [ring_gather(chunks[0], "front", front)]
    started = gathered[0][-1]
    for rnd in range(1, early + 1):
        gathered.append(ring_gather(after(chunks[rnd], gathered[-1][-1]), "front", front))
    late = Ring(after(jnp.concatenate(chunks[early + 1 :], axis=1), gathered[-1][-1]), "front", front)
    table_in = jnp.asarray(table)
    place = jnp.stack([(me % per_stage) * own, first_row, bulk_me]).astype(jnp.int32)

    own_lands = own_map < pivots
    own_rank = jnp.where(own_lands, jnp.cumsum(own_lands.astype(jnp.int32)) - 1, -1)
    pick = (own_rank[None, :] == jnp.arange(cap)[:, None]).astype(F32)
    spreads = front // sources

    def spread_out(x):
        rows = x.shape[0] // spreads
        part = x[:rows]
        for k in range(1, spreads):
            moved = lax.ppermute(
                x[k * rows : (k + 1) * rows],
                "front",
                [(s, s + k * sources) for s in range(sources)],
            )
            part = jnp.where(me // sources == k, moved, part)
        return part

    compact = jnp.dot(pick, coupling, precision=HIGHEST_PRECISION)
    raw_landing = lax.all_gather(spread_out(after(compact, started)), "front", axis=0, tiled=True)

    block_rows = (first_row + jnp.arange(count)) // BLOCK
    row_mask = jnp.take(block_pattern, block_rows, axis=0).astype(F32)
    arrow = parent_arrow * jnp.repeat(row_mask, BLOCK, axis=1)
    piece = count // bulk
    part = after(arrow, gathered[early][-1])
    pieces = part[:piece]
    for g in range(1, bulk):
        moved = lax.ppermute(part[g * piece : (g + 1) * piece], "bulk", [(0, g)])
        pieces = jnp.where(bulk_me == g, moved, pieces)
    line = lax.all_gather(after(spread_out(pieces), raw_landing), "front", axis=0, tiled=False)

    my_maps = jnp.stack([slot[own, :own] for slot in gathered[0]])
    ordered = jnp.sum(
        jnp.where(owners[None, :, None] == jnp.arange(front)[:, None, None], my_maps[None], 0.0), axis=1
    )
    maps = jnp.stack(bulk_gather(ordered, "bulk", bulk)).astype(jnp.int32)
    lands = maps[:, :sources] < pivots
    rank = jnp.cumsum(lands.astype(jnp.int32), axis=2) - 1
    overflow = jnp.any(rank[:, :, -1] >= cap)
    chosen = jnp.where(lands, rank, -1)[:, :, None, :] == jnp.arange(cap)[:, None]
    target = jnp.max(jnp.where(chosen, maps[:, :sources, None, :], -1), axis=3)
    target = jnp.where(overflow, -1, target).reshape(bulk, blocks, LANES)
    dense = pivots // blocks
    rows_of = (jnp.arange(blocks)[:, None] * dense + jnp.arange(dense)[None, :])[:, :, None, None]
    spread = (jnp.transpose(target, (1, 0, 2))[:, None] == rows_of).astype(BF16)
    spread = spread.reshape(blocks, dense, bulk * LANES)
    route = (
        lax.dynamic_index_in_dim(maps, me, 1, False)[:, None, :]
        == (first_row + jnp.arange(count))[None, :, None]
    ).astype(BF16)

    panels = width // LANES
    total_landing = sources * cap
    lh, ll, ih, il, owned = ([] for _ in range(5))
    xs = None
    for q in range(stages):
        final = q == stages - 1
        if q == 2 or (q < 2 and final):
            late.finish()
        split_at = [0, panels // 2, panels] if q < 2 and not final else [0, panels]
        needed = [
            any(c >= 0 and max(f, c) // per_stage == q for f, c in enumerate(row)) for row in table
        ]
        used = [gathered[0]] + [gathered[rnd + 1] if needed[rnd] else [] for rnd in range(early)]
        late_rounds = [(rnd - early, rnd) for rnd in range(early, rounds) if needed[rnd]]
        used.append(late.slots() if late_rounds else [])
        counts = [len(u) for u in used]
        deep = (q + 1) * width
        state = None
        for start, stop in zip(split_at[:-1], split_at[1:], strict=True):
            couples = 0 < q < stages - 1 and stop == panels
            landing = final
            if q < 2 and not final:
                place = late.advance(place)
            operands = [place]
            smem = 1
            aliases = {}
            if start == 0:
                operands += [owners, table_in] + [x for u in used for x in u]
                smem = 3
            else:
                operands += state
                aliases = {1 + k: k for k in range(5)}
            operands += lh + ll + ih + il
            if couples:
                operands.append(coupling[:, (q - 1) * width : q * width])
                if q > 1:
                    operands += xs
            if landing:
                operands.append(raw_landing)
            outs = [
                shaped((width, width), F32),
                shaped((width, deep), BF16),
                shaped((width, deep), BF16),
                shaped((width, width), BF16),
                shaped((width, width), BF16),
            ]
            scratch = []
            if couples:
                outs += [shaped((own, q * width), BF16)] * 2
            if stop == panels:
                outs.append(shaped((own, deep), F32))
            if landing:
                outs += [shaped((total_landing, total), BF16)] * 2
                outs.append(shaped((blocks * (blocks + 1) // 2, LANES, LANES), F32))
            if start == 0:
                scratch.append(pltpu.VMEM((width, deep), F32))
            if landing:
                scratch.append(pltpu.VMEM((total_landing, total), F32))
            out = list(
                vmem_call(
                    functools.partial(
                        lambda *refs, args: child_stage(*args, refs),
                        args=(
                            q, width, own, front, late_rounds, counts, (start, stop),
                            (total_landing, front, sources, cap), couples, landing,
                        ),
                    ),
                    outs,
                    [True] * smem + [False] * (len(operands) - smem),
                    scratch,
                    pl.CostEstimate(
                        flops=6_000_000_000 * (stop - start), bytes_accessed=1 << 20, transcendentals=0
                    ),
                    aliases,
                )(*operands)
            )
            state = out[:5]
            rest = out[5:]
            if couples:
                xs, rest = rest[:2], rest[2:]
            if stop == panels:
                owned.append(rest[0])
                rest = rest[1:]
            if landing:
                th, tl, squares = rest
            if q < 2 and not final:
                place = late.arrive(place, state[0])
        for held, new in zip((lh, ll, ih, il), state[1:], strict=True):
            held.append(new)

    lower_rows = jnp.zeros((own, total), F32)
    for q in range(stages):
        padded = jnp.pad(owned[q], ((0, 0), (0, total - (q + 1) * width)))
        lower_rows = jnp.where(me // per_stage == q, padded, lower_rows)

    all_squares = bulk_gather(squares, "bulk", bulk)
    solved = max(stages - 2, 0)
    operands = [coupling[:, solved * width :]] + (xs if solved > 0 else [])
    operands += lh[solved:] + ll[solved:] + ih[solved:] + il[solved:] + [th, tl]
    x_own, con = vmem_call(
        lambda *refs: own_kernel(solved, stages, width, refs),
        [shaped((own, total), F32), shaped((own, total_landing), F32)],
        [False] * len(operands),
        [pltpu.VMEM((own, total), BF16)] * 2,
        pl.CostEstimate(flops=10_000_000_000, bytes_accessed=1 << 20, transcendentals=0),
    )(*operands)

    def unchanged(lines, arrow, x_own):
        return lines, arrow

    def landing_whole(lines, arrow, x_own):
        slot = own_map - me * count
        hits = (slot[:, None] == jnp.arange(count)[None, :]).astype(F32)
        piece_rows = jnp.dot(hits.T, x_own, precision=HIGHEST_PRECISION)
        whole = lax.all_gather(piece_rows, "front", axis=0, tiled=True)[:pivots]
        reached = jnp.dot(x_own, whole.T, precision=HIGHEST_PRECISION)
        slot_index = own_map // count // front * count + own_map % count
        routing = (slot_index[:, None] == jnp.arange(bulk * count)[None, :]).astype(F32)
        added = lax.psum_scatter(
            jnp.dot(routing.T, reached, precision=HIGHEST_PRECISION),
            "bulk",
            scatter_dimension=0,
            tiled=True,
        )
        square = lax.psum(jnp.dot(whole, whole.T, precision=HIGHEST_PRECISION), "bulk")
        square = square.reshape(sources, bulk, spreads, piece // spreads, pivots)
        square = jnp.transpose(square, (1, 2, 0, 3, 4)).reshape(bulk, front, piece // spreads, pivots)
        changed = [
            lines[m] - lax.dynamic_index_in_dim(square, bulk_me ^ m, 0, False) for m in range(bulk)
        ]
        return changed, arrow - added

    lines = bulk_gather(line, "bulk", bulk)
    lines, arrow = lax.cond(overflow, landing_whole, unchanged, lines, arrow, x_own)

    all_con = bulk_gather(after(con, all_squares[-1]), "bulk", bulk)
    plh, pll, pih, pil, plow = vmem_call(
        lambda *refs: parent_kernel(bulk, blocks, width, sources, refs),
        [
            shaped((pivots, pivots), BF16),
            shaped((pivots, pivots), BF16),
            shaped((pivots // width, width, width), BF16),
            shaped((pivots // width, width, width), BF16),
            shaped((pivots, pivots), F32),
        ],
        [True] + [False] * (1 + 2 * bulk),
        [pltpu.VMEM((pivots, pivots), F32)] * 2,
        pl.CostEstimate(flops=60_000_000_000, bytes_accessed=1 << 24, transcendentals=0),
    )(place, spread, *lines, *all_squares)

    (parent_rows,) = vmem_call(
        lambda *refs: rest_kernel(bulk, blocks, width, refs),
        [shaped((count, pivots), F32)],
        [True] + [False] * (7 + bulk),
        [
            pltpu.VMEM((count, pivots), F32),
            pltpu.VMEM((count, pivots), BF16),
            pltpu.VMEM((count, pivots), BF16),
        ],
    )(place, arrow, route, spread, *all_con, plh, pll, pih, pil)
    return (lower_rows[None], x_own[None], parent_rows)


def solution(mesh):
    placed = (
        P("bulk", "front", None),
        P("bulk", "front", None),
        P(("bulk", "front"), None),
        P("bulk", "front"),
        P(),
    )
    return jax.shard_map(
        on_device,
        mesh=mesh,
        in_specs=placed,
        out_specs=(P("bulk", "front", None), P("bulk", "front", None), P(("bulk", "front"), None)),
        check_vma=False,
    )
```

```python
import functools

import jax
import jax.numpy as jnp
import numpy as np
from jax import lax
from jax.experimental import pallas as pl
from jax.experimental.pallas import tpu as pltpu
from jax.sharding import PartitionSpec as P

BLOCK = 128
STAGE = 512
CAP = 128
LANES = 128
SUB = 8
VMEM_LIMIT = 60 << 20

HIGHEST_PRECISION = lax.Precision.HIGHEST
NT = (((1,), (1,)), ((), ()))
NN = (((1,), (0,)), ((), ()))
F32 = jnp.float32
BF16 = jnp.bfloat16


def split(x):
    high = x.astype(BF16)
    return high, (x - high.astype(F32)).astype(BF16)


def dot(a, b, dims):
    return lax.dot_general(a, b, dims, preferred_element_type=F32)


def dot3(a, b, dims):
    return dot(a[0], b[0], dims) + (dot(a[0], b[1], dims) + dot(a[1], b[0], dims))


def ds(start, size):
    return pl.ds(pl.multiple_of(start, size), size)


def tiles(rows, cols, body, tile=256):
    tr, tc = min(tile, rows), min(tile, cols)
    nr, nc = rows // tr, cols // tc

    def step(t, carry):
        body((t // nc) * tr, tr, (t % nc) * tc, tc)
        return carry

    lax.fori_loop(0, nr * nc, step, 0)


def lane(x, c):
    return jnp.broadcast_to(x[:, c : c + 1], x.shape)


def sub(x, r):
    return jnp.broadcast_to(x[r : r + 1, :], x.shape)


def tree_sum(terms):
    terms = list(terms)
    while len(terms) > 1:
        terms = [
            terms[i] + terms[i + 1] if i + 1 < len(terms) else terms[i]
            for i in range(0, len(terms), 2)
        ]
    return terms[0]


def invert_small(s):
    n = len(s)
    s = list(s)
    row_id = lax.broadcasted_iota(jnp.int32, (SUB, LANES), 0)
    m = [None] * n
    for p in range(0, n, 2):
        q = p + 1
        a, b, d = sub(s[p], p), sub(s[q], p), sub(s[q], q)
        det = a * d - b * b
        scale = 1.0 / det
        ra = lax.rsqrt(a)
        rq = lax.rsqrt(det) * (a * ra)
        ba = b * ra * ra
        at_p, at_q = row_id == p, row_id == q
        sp, sq = s[p], s[q]
        fp, fq = (sp * d - sq * b) * scale, (sq * a - sp * b) * scale
        for k in range(n):
            if k in (p, q):
                continue
            u, v = sub(s[k], p), sub(s[k], q)
            if k < p:
                m[k] = jnp.where(at_p, -(u * ra), jnp.where(at_q, (u * ba - v) * rq, m[k]))
            s[k] = jnp.where(at_p, sub(fp, k), jnp.where(at_q, sub(fq, k), s[k] - (fp * u + fq * v)))
        s[p] = jnp.where(at_p, -(d * scale), jnp.where(at_q, b * scale, fp))
        s[q] = jnp.where(at_q, -(a * scale), jnp.where(at_p, b * scale, fq))
        m[p] = jnp.where(at_p, ra, jnp.where(at_q, -(ba * rq), 0.0))
        m[q] = jnp.where(at_q, rq, 0.0)
    return s, m


def factor_block(rows):
    n = len(rows)
    row_id = lax.broadcasted_iota(jnp.int32, (SUB, LANES), 0)
    lane_id = lax.broadcasted_iota(jnp.int32, (SUB, LANES), 1)
    a = list(rows)
    out = []
    for s in range(n):
        here = jnp.logical_and(lane_id >= SUB * s, lane_id < SUB * (s + 1))
        cols = [lane(a[s], SUB * s + r) for r in range(SUB)]
        r = jnp.where(here, jnp.where(row_id + SUB * s == lane_id, 1.0, 0.0), a[s])
        rb = [sub(r, q) for q in range(SUB)]
        t, m = invert_small(cols)
        v = tree_sum(m[q] * rb[q] for q in range(SUB))
        out.append(jnp.where(lane_id < SUB * (s + 1), v, 0.0))
        if s + 1 == n:
            break
        y = tree_sum(t[q] * rb[q] for q in range(SUB))
        yb = [sub(y, q) for q in range(SUB)]
        for i in range(s + 1, n):
            w = [lane(a[i], SUB * s + q) for q in range(SUB)]
            a[i] = jnp.where(here, 0.0, a[i]) + tree_sum(w[q] * yb[q] for q in range(SUB))
    return out


def subtract_products(dst, rows, cols, ah, al, bh, bl, depth, lower=False):
    if depth == 0:
        return
    tile = min(256, cols)
    for c in range(0, cols, tile):
        top = c if lower else 0
        a = (ah[top:rows, :depth], al[top:rows, :depth])
        b = (bh[c : c + tile, :depth], bl[c : c + tile, :depth])
        dst[top:rows, c : c + tile] = dst[top:rows, c : c + tile] - dot3(a, b, NT)


def times_inverse(src, outh, outl, out_at, rows, width, invh, invl):
    tile = min(256, width)
    a = split(src[:rows, :])
    for c in range(0, width, tile):
        part = tuple(x[:, : c + tile] for x in a)
        b = (invh[c : c + tile, : c + tile], invl[c : c + tile, : c + tile])
        high, low = split(dot3(part, b, NT))
        outh[:rows, out_at + c : out_at + c + tile] = high
        outl[:rows, out_at + c : out_at + c + tile] = low


def clear_inverse(invh, invl):
    invh[...] = jnp.zeros(invh.shape, BF16)
    invl[...] = jnp.zeros(invl.shape, BF16)


def inverse_row(r, at, width, lh, ll, invh, invl):
    here = ds(r * LANES, LANES)
    left = lax.broadcasted_iota(jnp.int32, (LANES, width), 1) < r * LANES
    none = jnp.zeros((LANES, width), BF16)
    low = tuple(jnp.where(left, ref[here, at : at + width], none) for ref in (lh, ll))
    mixed = split(dot3(low, (invh[...], invl[...]), NN))
    high, low = split(-dot3((invh[here, here], invl[here, here]), mixed, NN))
    invh[here, :] = jnp.where(left, high, invh[here, :])
    invl[here, :] = jnp.where(left, low, invl[here, :])


def factor_panels(start, stop, s_ref, at, width, lh, ll, invh, invl, job=None):
    row_id = lax.broadcasted_iota(jnp.int32, (width, LANES), 0)
    col_id = lax.broadcasted_iota(jnp.int32, (width, LANES), 1)
    none = jnp.zeros((width, LANES), BF16)
    last = width // LANES - 1

    def column(r, some):
        here = ds(r * LANES, LANES)
        inv = (invh[here, here], invl[here, here])
        solved = dot3(split(s_ref[:, here]), inv, NT)
        solved = jnp.where(jnp.logical_and(row_id >= col_id + r * LANES, some), solved, 0.0)
        high, low = split(solved)
        lh[:, ds(at + r * LANES, LANES)] = high
        ll[:, ds(at + r * LANES, LANES)] = low
        return high, low

    def panel(p, carry):
        first = p * LANES
        here = ds(first, LANES)
        block = [
            s_ref[pl.ds(pl.multiple_of(first + SUB * i, SUB), SUB), here]
            for i in range(LANES // SUB)
        ]
        before = jnp.maximum(p - 1, 0)
        high, low = column(before, p > 0)
        high = jnp.where(row_id >= first, high, none)
        low = jnp.where(row_id >= first, low, none)
        below = tuple(jnp.where(row_id >= first + LANES, x, none) for x in (high, low))
        for c in range(1, last + 1):
            rows = slice(c * LANES, None)
            cols = slice(c * LANES, (c + 1) * LANES)
            s_ref[rows, cols] = s_ref[rows, cols] - dot3(
                (below[0][rows], below[1][rows]), (high[cols], low[cols]), NT
            )
        inverse_row(before, at, width, lh, ll, invh, invl)
        if job is not None:
            job(p)

        inv = split(jnp.concatenate(factor_block(block), axis=0))
        invh[here, here] = inv[0]
        invl[here, here] = inv[1]
        following = ds(jnp.minimum(p + 1, last) * LANES, LANES)
        beside = split(jnp.where(p < last, dot3(split(s_ref[following, here]), inv, NT), 0.0))
        s_ref[following, following] = s_ref[following, following] - dot3(beside, beside, NT)
        return carry

    lax.fori_loop(start, stop, panel, 0)
    if stop == last + 1:
        column(last, True)
        inverse_row(last, at, width, lh, ll, invh, invl)


def solve_some(rows, src, q, width, xh, xl, l_rows, inv):
    part = src
    if q > 0:
        deep = q * width
        part = part - dot3(
            (xh[rows, :deep], xl[rows, :deep]), (l_rows[0][:, :deep], l_rows[1][:, :deep]), NT
        )
    high, low = split(dot3(split(part), (inv[0][...], inv[1][...]), NT))
    xh[rows, q * width : (q + 1) * width] = high
    xl[rows, q * width : (q + 1) * width] = low


def vmem_call(body, out_shapes, in_kinds, scratch, cost=None, aliases=None):
    spaces = {True: pltpu.SMEM, False: pltpu.VMEM, None: pl.ANY}
    specs = [pl.BlockSpec(memory_space=spaces[k]) for k in in_kinds]
    return pl.pallas_call(
        body,
        out_shape=out_shapes,
        in_specs=specs,
        out_specs=[pl.BlockSpec(memory_space=pltpu.VMEM)] * len(out_shapes),
        scratch_shapes=scratch,
        compiler_params=pltpu.CompilerParams(vmem_limit_bytes=VMEM_LIMIT),
        cost_estimate=cost,
        input_output_aliases=aliases or {},
    )


def shaped(shape, dtype):
    return jax.ShapeDtypeStruct(shape, dtype)


def send_plan(groups, per_stage):
    pairs = [
        (j, i)
        for i in range(groups)
        for j in range(i)
        if not (i == j + 1 and j % 2 == 0)
    ]
    pairs.sort(key=lambda pair: (pair[1] // per_stage, pair))
    taken = {}

    last = {}

    def place(pair, seen):
        for rnd in range(last[pair]):
            for dev in (pair[1], pair[0]):
                slot = (rnd, dev)
                if slot in seen:
                    continue
                seen.add(slot)
                if slot not in taken or place(taken[slot], seen):
                    taken[slot] = pair
                    return True
        return False

    limit = 1
    for pair in pairs:
        last[pair] = limit
        while not place(pair, set()):
            limit += 1
            last[pair] = limit
    rounds = 1 + max((slot[0] for slot in taken), default=-1)
    table = np.full((max(rounds, 1), groups), -1, np.int32)
    for (rnd, dev), (j, i) in taken.items():
        table[rnd, dev] = j if dev == i else i
    return table[:rounds]


def ring_order(groups):
    return [i for i in range(0, groups, 2)] + [i for i in range(groups - 1, 0, -2)]


def ring_gather(chunk, axis, groups):
    order = ring_order(groups)
    ahead = [(order[i], order[(i + 1) % groups]) for i in range(groups)]
    back = [(b, a) for a, b in ahead]
    out = [chunk]
    going, coming = chunk, chunk
    steps_ahead = groups // 2
    steps_back = groups - 1 - steps_ahead
    aheads, backs = [], []
    for step in range(steps_ahead):
        going = lax.ppermute(going, axis, ahead)
        aheads.append(going)
        if step < steps_back:
            coming = lax.ppermute(coming, axis, back)
            backs.append(coming)
    return out + aheads + backs


class Ring:
    def __init__(self, chunk, axis, groups):
        order = ring_order(groups)
        self.axis = axis
        self.ahead = [(order[i], order[(i + 1) % groups]) for i in range(groups)]
        self.back = [(b, a) for a, b in self.ahead]
        self.steps = groups // 2
        self.steps_back = groups - 1 - self.steps
        self.own = chunk
        self.aheads, self.backs = [], []
        self.going = self.coming = chunk

    def advance(self, token):
        if len(self.aheads) < self.steps:
            self.going = lax.ppermute(self.going, self.axis, self.ahead)
            self.aheads.append(self.going)
            if len(self.backs) < self.steps_back:
                self.coming = lax.ppermute(self.coming, self.axis, self.back)
                self.backs.append(self.coming)
        return token

    def arrive(self, token, beside):
        token, self.going, self.coming, _ = lax.optimization_barrier((token, self.going, self.coming, beside))
        return token

    def finish(self):
        while len(self.aheads) < self.steps:
            self.advance(None)

    def slots(self):
        return [self.own] + self.aheads + self.backs


def slot_owners(axis, groups):
    order = np.array(ring_order(groups), np.int32)
    place = np.argsort(order)
    me = jnp.asarray(place)[lax.axis_index(axis)]
    steps_ahead = groups // 2
    steps_back = groups - 1 - steps_ahead
    shifts = [0] + [-s for s in range(1, steps_ahead + 1)] + list(range(1, steps_back + 1))
    return jnp.asarray(order)[(me + jnp.asarray(shifts, jnp.int32)) % groups].astype(jnp.int32)


def direct_gather(x, axis, groups, sources):
    moved = [
        lax.ppermute(x, axis, [(s, (s + k) % groups) for s in range(sources)])
        for k in range(1, groups)
    ]
    return [x] + moved


def bulk_gather(x, axis, size, low_first=False, beside=None):
    held = {0: x}
    steps = [1 << bit for bit in range(size.bit_length() - 1)]
    for step in steps if low_first else reversed(steps):
        new = {
            mask | step: lax.ppermute(held[mask], axis, [(i, i ^ step) for i in range(size)])
            for mask in held
        }
        if beside is not None:
            new = {mask: after(value, beside()) for mask, value in new.items()}
            beside = None
        held.update(new)
    return [held[m] for m in range(size)]


def after(x, dep):
    return lax.optimization_barrier((x, dep))[0]


def assemble_rows(q, width, own, groups, owner_ref, table_ref, chunks, late_rounds, a_ref):
    per_stage = width // own
    first_group = q * per_stage
    for k in range(groups):
        f = owner_ref[k]

        @pl.when(f // per_stage == q)
        def _(f=f, k=k):
            chunk = chunks[0][k]
            at = (f - first_group) * own
            a_ref[ds(at, own), ds(f * own, own)] = chunk[:own, :own]
            half = own // 2
            odd = f % 2
            row = (f - odd + 1 - first_group) * own + odd * half
            a_ref[ds(row, half), ds((f - odd) * own, own)] = chunk[:own, own:].T

    sent = [(rnd, chunk, 0) for rnd, chunk in enumerate(chunks[1:-1]) if chunk]
    sent += [(rnd, chunks[-1], at * own) for at, rnd in late_rounds]
    for rnd, chunk, cut in sent:
        for k in range(groups):
            f = owner_ref[k]
            c = table_ref[rnd, f]
            high = jnp.maximum(f, c)
            low = jnp.minimum(f, c)
            mine = jnp.logical_and(c >= 0, high // per_stage == q)
            row = jnp.clip((high - first_group) * own, 0, width - own)
            col = jnp.clip(low * own, 0, (q + 1) * width - own)

            @pl.when(jnp.logical_and(mine, f > c))
            def _(chunk=chunk, cut=cut, k=k, row=row, col=col):
                a_ref[ds(row, own), ds(col, own)] = chunk[k][:, cut : cut + own]

            @pl.when(jnp.logical_and(mine, f < c))
            def _(chunk=chunk, cut=cut, k=k, row=row, col=col):
                a_ref[ds(row, own), ds(col, own)] = chunk[k][:, cut : cut + own].T


def child_stage(q, width, own, groups, late_rounds, counts, span, shapes, couples, landing, refs):
    start, stop = span
    panels = width // LANES
    refs = list(refs)

    def take(count):
        out, refs[:count] = refs[:count], []
        return out

    (place_ref,) = take(1)
    if start == 0:
        owner_ref, table_ref = take(2)
        chunks = [take(count) for count in counts]
    else:
        state = take(5)
    prev_lh, prev_ll, prev_ih, prev_il = (take(q) for _ in range(4))
    if couples:
        b_ref = take(1)[0]
        old_x = take(2) if q > 1 else None
    if landing:
        raw_ref = take(1)[0]
    s_out, lh, ll, invh, invl = take(5)
    if couples:
        xh, xl = take(2)
    if stop == panels:
        own_ref = take(1)[0]
    if landing:
        th, tl, sq_ref = take(3)
    if start == 0:
        a_ref = take(1)[0]
    if landing:
        t_ref, copy_sems = take(2)

    copies = []
    if landing:
        total, front, sources, cap = shapes
        share = cap * sources // front
        for f in range(front):
            at = (f % sources) * cap + (f // sources) * share
            copies.append(
                pltpu.make_async_copy(
                    raw_ref.at[f, :share, :], t_ref.at[at : at + share, :], copy_sems.at[f]
                )
            )
            copies[-1].start()
    if start == 0:
        assemble_rows(q, width, own, groups, owner_ref, table_ref, chunks, late_rounds, a_ref)
        for j in range(q):
            part = a_ref.at[:, j * width : (j + 1) * width]
            subtract_products(part, width, width, lh, ll, prev_lh[j], prev_ll[j], j * width)
            times_inverse(part, lh, ll, j * width, width, width, prev_ih[j], prev_il[j])
        s_out[...] = a_ref[:, q * width : (q + 1) * width]
        subtract_products(s_out, width, width, lh, ll, lh, ll, q * width, True)
        clear_inverse(invh, invl)
    else:
        for new, held in zip((s_out, lh, ll, invh, invl), state, strict=True):
            new[...] = held[...]
    if couples and q > 1:
        xh[:, : (q - 1) * width] = old_x[0][...]
        xl[:, : (q - 1) * width] = old_x[1][...]
    for copy in copies:
        copy.wait()

    def job(p):
        if couples:
            some = own // (stop - start)
            rows = ds((p - start) * some, some)
            solve_some(
                rows, b_ref[rows, :], q - 1, width, xh, xl,
                (prev_lh[q - 1], prev_ll[q - 1]), (prev_ih[q - 1], prev_il[q - 1]),
            )
        if landing:
            some = total // (stop - start)
            rows = ds((p - start) * some, some)
            for j in range(q):
                solve_some(
                    rows, t_ref[rows, j * width : (j + 1) * width], j, width, th, tl,
                    (prev_lh[j], prev_ll[j]), (prev_ih[j], prev_il[j]),
                )

    factor_panels(start, stop, s_out, q * width, width, lh, ll, invh, invl, job)
    if stop == panels:
        at = place_ref[0]
        own_ref[...] = lh[ds(at, own), :].astype(F32) + ll[ds(at, own), :].astype(F32)
    if landing:
        part = t_ref.at[:, q * width : (q + 1) * width]
        subtract_products(part, total, width, th, tl, lh, ll, q * width)
        times_inverse(part, th, tl, q * width, total, width, invh, invl)

        def square(t, carry):
            i, j = carry
            a = (th[ds(i * LANES, LANES), :], tl[ds(i * LANES, LANES), :])
            b = (th[ds(j * LANES, LANES), :], tl[ds(j * LANES, LANES), :])
            sq_ref[t] = dot3(a, b, NT)
            end = j == i
            return (jnp.where(end, i + 1, i), jnp.where(end, 0, j + 1))

        blocks = total // LANES
        lax.fori_loop(0, blocks * (blocks + 1) // 2, square, (jnp.int32(0), jnp.int32(0)))


def own_kernel(first, stages, width, refs):
    refs = list(refs)

    def take(count):
        out, refs[:count] = refs[:count], []
        return out

    (b_ref,) = take(1)
    old_h, old_l = take(2) if first > 0 else (None, None)
    left = stages - first
    lh, ll, ih, il = (take(left) for _ in range(4))
    th, tl = take(2)
    x_ref, con_ref = take(2)
    xh, xl = take(2)
    own = b_ref.shape[0]
    if first > 0:
        xh[:, : first * width] = old_h[...]
        xl[:, : first * width] = old_l[...]
    for k in range(left):
        q = first + k
        for c in range(1):
            part = b_ref.at[:, k * width : (k + 1) * width]
            x_ref[:, q * width : (q + 1) * width] = part[...]
            part = x_ref.at[:, q * width : (q + 1) * width]
            subtract_products(part, own, width, xh, xl, lh[k], ll[k], q * width)
            times_inverse(part, xh, xl, q * width, own, width, ih[k], il[k])
    x_ref[...] = xh[...].astype(F32) + xl[...].astype(F32)

    def body(r, nr, c, nc):
        a = (xh[ds(r, nr), :], xl[ds(r, nr), :])
        b = (th[ds(c, nc), :], tl[ds(c, nc), :])
        con_ref[ds(r, nr), ds(c, nc)] = dot3(a, b, NT)

    tiles(own, con_ref.shape[1], body)


def parent_kernel(children, blocks, width, sources, refs):
    refs = list(refs)
    place_ref, spread_ref = refs[:2]
    tops, squares = refs[2 : 2 + children], refs[2 + children : 2 + 2 * children]
    lh, ll, invh, invl, s_ref, top_ref = refs[2 + 2 * children :]
    pivots = lh.shape[0]
    dense = pivots // blocks
    groups, part_rows, _ = tops[0].shape
    spreads = groups // sources
    piece = part_rows * spreads
    for m in range(children):
        g = place_ref[2] ^ m
        for f in range(groups):
            at = (f % sources) * (children * piece) + g * piece + (f // sources) * part_rows
            top_ref[ds(at, part_rows), :] = tops[m][f]
    for i in range(blocks):
        for j in range(i + 1):
            at = i * (i + 1) // 2 + j
            parts = []
            for c in range(children):
                left = spread_ref[i, :, c * LANES : (c + 1) * LANES]
                high, low = split(squares[c][at])
                parts.append(dot(left, high, NN) + dot(left, low, NN))
            high, low = split(jnp.concatenate(parts, axis=1))
            right = spread_ref[j]
            rows = slice(i * dense, (i + 1) * dense)
            cols = slice(j * dense, (j + 1) * dense)
            s_ref[rows, cols] = top_ref[rows, cols] - (
                dot(high, right, NT) + dot(low, right, NT)
            )
    for q in range(pivots // width):
        rows = slice(q * width, (q + 1) * width)
        lhq, llq = lh.at[rows, :], ll.at[rows, :]
        if q + 1 < pivots // width:
            lhq[:, (q + 1) * width :] = jnp.zeros((width, pivots - (q + 1) * width), BF16)
            llq[:, (q + 1) * width :] = jnp.zeros((width, pivots - (q + 1) * width), BF16)
        for j in range(q):
            part = s_ref.at[rows, j * width : (j + 1) * width]
            cut = slice(j * width, (j + 1) * width)
            subtract_products(part, width, width, lhq, llq, lh.at[cut, :], ll.at[cut, :], j * width)
            times_inverse(part, lhq, llq, j * width, width, width, invh.at[j], invl.at[j])
        part = s_ref.at[rows, q * width : (q + 1) * width]
        subtract_products(part, width, width, lhq, llq, lhq, llq, q * width, True)
        clear_inverse(invh.at[q], invl.at[q])
        factor_panels(0, width // LANES, part, q * width, width, lhq, llq, invh.at[q], invl.at[q])


def rest_kernel(children, blocks, width, refs):
    refs = list(refs)
    place_ref, rows_ref, route_ref, spread_ref = refs[:4]
    con_refs = refs[4 : 4 + children]
    lh, ll, invh, invl, out_ref, s_ref, xh, xl = refs[4 + children :]
    pivots = lh.shape[0]
    count = rows_ref.shape[0]
    dense = pivots // blocks
    at = place_ref[1]

    @pl.when(at < pivots)
    def _():
        row = ds(jnp.minimum(at, pivots - count), count)
        out_ref[...] = lh[row, :].astype(F32) + ll[row, :].astype(F32)

    @pl.when(at >= pivots)
    def _():
        routed = []
        for c in range(children):
            high, low = split(con_refs[c][...])
            route = route_ref[c]
            routed.append(split(dot(route, high, NN) + dot(route, low, NN)))
        for b in range(blocks):
            lanes = slice(b * LANES, (b + 1) * LANES)
            high = jnp.concatenate([routed[c][0][:, lanes] for c in range(children)], axis=1)
            low = jnp.concatenate([routed[c][1][:, lanes] for c in range(children)], axis=1)
            right = spread_ref[b]
            cols = slice(b * dense, (b + 1) * dense)
            s_ref[:, cols] = rows_ref[:, cols] - (dot(high, right, NT) + dot(low, right, NT))
        for q in range(pivots // width):
            cut = slice(q * width, (q + 1) * width)
            part = s_ref.at[:, cut]
            subtract_products(part, count, width, xh, xl, lh.at[cut, :], ll.at[cut, :], q * width)
            times_inverse(part, xh, xl, q * width, count, width, invh.at[q], invl.at[q])
        out_ref[...] = xh[...].astype(F32) + xl[...].astype(F32)


def on_device(child_pivot, child_coupling, parent_arrow, row_map, block_pattern):
    front = lax.axis_size("front")
    bulk = lax.axis_size("bulk")
    me = lax.axis_index("front")
    mine = child_pivot[0]
    coupling = child_coupling[0]
    own, total = mine.shape
    count, pivots = parent_arrow.shape
    width = min(STAGE, total)
    stages = total // width
    per_stage = width // own
    first_row = (lax.axis_index("bulk") * front + me) * count
    sources = pivots // count
    cap = min(CAP, count, own)
    blocks = sources * cap // LANES

    table = send_plan(front, per_stage)
    rounds = table.shape[0]
    bulk_me = lax.axis_index("bulk")
    early = max(
        (r + 1 for r in range(rounds) for f, c in enumerate(table[r]) if c >= 0 and max(f, c) // per_stage <= 1),
        default=0,
    )
    half = own // 2
    own_map = row_map[0]
    own_block = lax.dynamic_slice_in_dim(mine, me * own, own, 1)
    even = lax.dynamic_slice_in_dim(mine, jnp.minimum(me + 1, front - 1) * own, half, 1)
    odd = lax.dynamic_slice_in_dim(mine[half:], jnp.maximum(me - 1, 0) * own, own, 1).T
    head = jnp.concatenate([own_block, jnp.where(me % 2 == 0, even, odd)], axis=1)
    tail = jnp.pad(own_map.astype(F32)[None], ((0, SUB - 1), (0, half)))
    chunks = [jnp.concatenate([head, tail], axis=0)]
    mine_later, table_me = after((mine, jnp.asarray(table)[:, me]), chunks[0])
    for rnd in range(rounds):
        col = jnp.maximum(table_me[rnd], 0)
        chunks.append(lax.dynamic_slice_in_dim(mine_later, col * own, own, 1))
    owners = slot_owners("front", front)
    gathered = [ring_gather(chunks[0], "front", front)]
    started = gathered[0][-1]
    for rnd in range(1, early + 1):
        gathered.append(ring_gather(after(chunks[rnd], gathered[-1][-1]), "front", front))
    here = gathered[-1][1:]
    late = Ring(after(jnp.concatenate(chunks[early + 1 :], axis=1), here), "front", front)
    table_in = jnp.asarray(table)
    place = jnp.stack([(me % per_stage) * own, first_row, bulk_me]).astype(jnp.int32)

    own_lands = own_map < pivots
    own_rank = jnp.where(own_lands, jnp.cumsum(own_lands.astype(jnp.int32)) - 1, -1)
    pick = (own_rank[None, :] == jnp.arange(cap)[:, None]).astype(F32)
    spreads = front // sources

    def spread_out(x):
        rows = x.shape[0] // spreads
        part = x[:rows]
        for k in range(1, spreads):
            moved = lax.ppermute(
                x[k * rows : (k + 1) * rows],
                "front",
                [(s, s + k * sources) for s in range(sources)],
            )
            part = jnp.where(me // sources == k, moved, part)
        return part

    compact = jnp.dot(pick, coupling, precision=HIGHEST_PRECISION)
    landing_part = spread_out(after(compact, started))
    place = after(place, here)

    block_rows = (first_row + jnp.arange(count)) // BLOCK
    row_mask = jnp.take(block_pattern, block_rows, axis=0).astype(F32)
    arrow = parent_arrow * jnp.repeat(row_mask, BLOCK, axis=1)
    piece = count // bulk
    part = after(arrow, chunks[0])
    pieces = part[:piece]
    for g in range(1, bulk):
        moved = lax.ppermute(part[g * piece : (g + 1) * piece], "bulk", [(0, g)])
        pieces = jnp.where(bulk_me == g, moved, pieces)
    line_part = spread_out(pieces)
    share = landing_part.shape[0]
    extra = line_part.reshape(-1, total)
    padding = jnp.zeros((-extra.shape[0] % SUB, total), F32)
    both = jnp.concatenate([landing_part, extra, padding], axis=0)
    place = after(place, both)
    both = lax.all_gather(both, "front", axis=0, tiled=False)
    line = both[:, share : share + extra.shape[0]].reshape((front,) + line_part.shape)

    my_maps = jnp.stack([slot[own, :own] for slot in gathered[0]])
    ordered = jnp.sum(
        jnp.where(owners[None, :, None] == jnp.arange(front)[:, None, None], my_maps[None], 0.0), axis=1
    )
    maps = jnp.stack(bulk_gather(ordered, "bulk", bulk)).astype(jnp.int32)
    place = after(place, maps)
    lands = maps[:, :sources] < pivots
    rank = jnp.cumsum(lands.astype(jnp.int32), axis=2) - 1
    overflow = jnp.any(rank[:, :, -1] >= cap)
    chosen = jnp.where(lands, rank, -1)[:, :, None, :] == jnp.arange(cap)[:, None]
    target = jnp.max(jnp.where(chosen, maps[:, :sources, None, :], -1), axis=3)
    target = jnp.where(overflow, -1, target).reshape(bulk, blocks, LANES)
    dense = pivots // blocks
    rows_of = (jnp.arange(blocks)[:, None] * dense + jnp.arange(dense)[None, :])[:, :, None, None]
    spread = (jnp.transpose(target, (1, 0, 2))[:, None] == rows_of).astype(BF16)
    spread = spread.reshape(blocks, dense, bulk * LANES)
    route = (
        lax.dynamic_index_in_dim(maps, me, 1, False)[:, None, :]
        == (first_row + jnp.arange(count))[None, :, None]
    ).astype(BF16)

    panels = width // LANES
    total_landing = sources * cap
    lh, ll, ih, il, owned = ([] for _ in range(5))
    xs = None
    for q in range(stages):
        final = q == stages - 1
        if q == 2 or (q < 2 and final):
            late.finish()
        split_at = [0, panels // 2, panels] if q < 2 and not final else [0, panels]
        needed = [
            any(c >= 0 and max(f, c) // per_stage == q for f, c in enumerate(row)) for row in table
        ]
        used = [gathered[0]] + [gathered[rnd + 1] if needed[rnd] else [] for rnd in range(early)]
        late_rounds = [(rnd - early, rnd) for rnd in range(early, rounds) if needed[rnd]]
        used.append(late.slots() if late_rounds else [])
        counts = [len(u) for u in used]
        deep = (q + 1) * width
        state = None
        for start, stop in zip(split_at[:-1], split_at[1:], strict=True):
            couples = 0 < q < stages - 1 and stop == panels
            landing = final
            if q < 2 and not final:
                place = late.advance(place)
            operands = [place]
            smem = 1
            aliases = {}
            if start == 0:
                operands += [owners, table_in] + [x for u in used for x in u]
                smem = 3
            else:
                operands += state
                aliases = {1 + k: k for k in range(5)}
            operands += lh + ll + ih + il
            if couples:
                operands.append(coupling[:, (q - 1) * width : q * width])
                if q > 1:
                    operands += xs
            if landing:
                operands.append(both)
            outs = [
                shaped((width, width), F32),
                shaped((width, deep), BF16),
                shaped((width, deep), BF16),
                shaped((width, width), BF16),
                shaped((width, width), BF16),
            ]
            scratch = []
            if couples:
                outs += [shaped((own, q * width), BF16)] * 2
            if stop == panels:
                outs.append(shaped((own, deep), F32))
            if landing:
                outs += [shaped((total_landing, total), BF16)] * 2
                outs.append(shaped((blocks * (blocks + 1) // 2, LANES, LANES), F32))
            if start == 0:
                scratch.append(pltpu.VMEM((width, deep), F32))
            if landing:
                scratch.append(pltpu.VMEM((total_landing, total), F32))
                scratch.append(pltpu.SemaphoreType.DMA((front,)))
            out = list(
                vmem_call(
                    functools.partial(
                        lambda *refs, args: child_stage(*args, refs),
                        args=(
                            q, width, own, front, late_rounds, counts, (start, stop),
                            (total_landing, front, sources, cap), couples, landing,
                        ),
                    ),
                    outs,
                    [True] * smem
                    + [False] * (len(operands) - smem - landing)
                    + [None] * landing,
                    scratch,
                    pl.CostEstimate(
                        flops=6_000_000_000 * (stop - start), bytes_accessed=1 << 20, transcendentals=0
                    ),
                    aliases,
                )(*operands)
            )
            state = out[:5]
            rest = out[5:]
            if couples:
                xs, rest = rest[:2], rest[2:]
            if stop == panels:
                owned.append(rest[0])
                rest = rest[1:]
            if landing:
                th, tl, squares = rest
            if q < 2 and not final:
                place = late.arrive(place, state[0])
        for held, new in zip((lh, ll, ih, il), state[1:], strict=True):
            held.append(new)

    lower_rows = jnp.zeros((own, total), F32)
    for q in range(stages):
        padded = jnp.pad(owned[q], ((0, 0), (0, total - (q + 1) * width)))
        lower_rows = jnp.where(me // per_stage == q, padded, lower_rows)

    solved = max(stages - 2, 0)
    operands = [coupling[:, solved * width :]] + (xs if solved > 0 else [])
    operands += lh[solved:] + ll[solved:] + ih[solved:] + il[solved:] + [th, tl]
    x_own, con = vmem_call(
        lambda *refs: own_kernel(solved, stages, width, refs),
        [shaped((own, total), F32), shaped((own, total_landing), F32)],
        [False] * len(operands),
        [pltpu.VMEM((own, total), BF16)] * 2,
        pl.CostEstimate(flops=10_000_000_000, bytes_accessed=1 << 20, transcendentals=0),
    )(*operands)
    all_squares = bulk_gather(squares, "bulk", bulk, beside=lambda: con)

    def unchanged(lines, arrow, x_own):
        return lines, arrow

    def landing_whole(lines, arrow, x_own):
        slot = own_map - me * count
        hits = (slot[:, None] == jnp.arange(count)[None, :]).astype(F32)
        piece_rows = jnp.dot(hits.T, x_own, precision=HIGHEST_PRECISION)
        whole = lax.all_gather(piece_rows, "front", axis=0, tiled=True)[:pivots]
        reached = jnp.dot(x_own, whole.T, precision=HIGHEST_PRECISION)
        slot_index = own_map // count // front * count + own_map % count
        routing = (slot_index[:, None] == jnp.arange(bulk * count)[None, :]).astype(F32)
        added = lax.psum_scatter(
            jnp.dot(routing.T, reached, precision=HIGHEST_PRECISION),
            "bulk",
            scatter_dimension=0,
            tiled=True,
        )
        square = lax.psum(jnp.dot(whole, whole.T, precision=HIGHEST_PRECISION), "bulk")
        square = square.reshape(sources, bulk, spreads, piece // spreads, pivots)
        square = jnp.transpose(square, (1, 2, 0, 3, 4)).reshape(bulk, front, piece // spreads, pivots)
        changed = [
            lines[m] - lax.dynamic_index_in_dim(square, bulk_me ^ m, 0, False) for m in range(bulk)
        ]
        return changed, arrow - added

    lines = bulk_gather(line, "bulk", bulk)
    lines, arrow = lax.cond(overflow, landing_whole, unchanged, lines, arrow, x_own)

    all_con = bulk_gather(con, "bulk", bulk, low_first=True)
    plh, pll, pih, pil = vmem_call(
        lambda *refs: parent_kernel(bulk, blocks, width, sources, refs),
        [
            shaped((pivots, pivots), BF16),
            shaped((pivots, pivots), BF16),
            shaped((pivots // width, width, width), BF16),
            shaped((pivots // width, width, width), BF16),
        ],
        [True] + [False] * (1 + 2 * bulk),
        [pltpu.VMEM((pivots, pivots), F32)] * 2,
        pl.CostEstimate(flops=60_000_000_000, bytes_accessed=1 << 24, transcendentals=0),
    )(place, spread, *lines, *all_squares)

    (parent_rows,) = vmem_call(
        lambda *refs: rest_kernel(bulk, blocks, width, refs),
        [shaped((count, pivots), F32)],
        [True] + [False] * (7 + bulk),
        [
            pltpu.VMEM((count, pivots), F32),
            pltpu.VMEM((count, pivots), BF16),
            pltpu.VMEM((count, pivots), BF16),
        ],
    )(place, arrow, route, spread, *all_con, plh, pll, pih, pil)
    return (lower_rows[None], x_own[None], parent_rows)


def solution(mesh):
    placed = (
        P("bulk", "front", None),
        P("bulk", "front", None),
        P(("bulk", "front"), None),
        P("bulk", "front"),
        P(),
    )
    return jax.shard_map(
        on_device,
        mesh=mesh,
        in_specs=placed,
        out_specs=(P("bulk", "front", None), P("bulk", "front", None), P(("bulk", "front"), None)),
        check_vma=False,
    )
```

```python
import functools

import jax
import jax.numpy as jnp
import numpy as np
from jax import lax
from jax.experimental import pallas as pl
from jax.experimental.pallas import tpu as pltpu
from jax.sharding import PartitionSpec as P

BLOCK = 128
STAGE = 512
CAP = 128
LANES = 128
SUB = 8
VMEM_LIMIT = 60 << 20

HIGHEST_PRECISION = lax.Precision.HIGHEST
NT = (((1,), (1,)), ((), ()))
NN = (((1,), (0,)), ((), ()))
F32 = jnp.float32
BF16 = jnp.bfloat16


def split(x):
    high = x.astype(BF16)
    return high, (x - high.astype(F32)).astype(BF16)


def dot(a, b, dims):
    return lax.dot_general(a, b, dims, preferred_element_type=F32)


def dot3(a, b, dims):
    return dot(a[0], b[0], dims) + (dot(a[0], b[1], dims) + dot(a[1], b[0], dims))


def ds(start, size):
    return pl.ds(pl.multiple_of(start, size), size)


def tiles(rows, cols, body, tile=256):
    tr, tc = min(tile, rows), min(tile, cols)
    nr, nc = rows // tr, cols // tc

    def step(t, carry):
        body((t // nc) * tr, tr, (t % nc) * tc, tc)
        return carry

    lax.fori_loop(0, nr * nc, step, 0)


def lane(x, c):
    return jnp.broadcast_to(x[:, c : c + 1], x.shape)


def sub(x, r):
    return jnp.broadcast_to(x[r : r + 1, :], x.shape)


def tree_sum(terms):
    terms = list(terms)
    while len(terms) > 1:
        terms = [
            terms[i] + terms[i + 1] if i + 1 < len(terms) else terms[i]
            for i in range(0, len(terms), 2)
        ]
    return terms[0]


def invert_small(s):
    n = len(s)
    s = list(s)
    row_id = lax.broadcasted_iota(jnp.int32, (SUB, LANES), 0)
    m = [None] * n
    for p in range(0, n, 2):
        q = p + 1
        a, b, d = sub(s[p], p), sub(s[q], p), sub(s[q], q)
        det = a * d - b * b
        scale = 1.0 / det
        ra = lax.rsqrt(a)
        rq = lax.rsqrt(det) * (a * ra)
        ba = b * ra * ra
        at_p, at_q = row_id == p, row_id == q
        sp, sq = s[p], s[q]
        fp, fq = (sp * d - sq * b) * scale, (sq * a - sp * b) * scale
        for k in range(n):
            if k in (p, q):
                continue
            u, v = sub(s[k], p), sub(s[k], q)
            if k < p:
                m[k] = jnp.where(at_p, -(u * ra), jnp.where(at_q, (u * ba - v) * rq, m[k]))
            s[k] = jnp.where(at_p, sub(fp, k), jnp.where(at_q, sub(fq, k), s[k] - (fp * u + fq * v)))
        s[p] = jnp.where(at_p, -(d * scale), jnp.where(at_q, b * scale, fp))
        s[q] = jnp.where(at_q, -(a * scale), jnp.where(at_p, b * scale, fq))
        m[p] = jnp.where(at_p, ra, jnp.where(at_q, -(ba * rq), 0.0))
        m[q] = jnp.where(at_q, rq, 0.0)
    return s, m


def factor_block(rows):
    n = len(rows)
    row_id = lax.broadcasted_iota(jnp.int32, (SUB, LANES), 0)
    lane_id = lax.broadcasted_iota(jnp.int32, (SUB, LANES), 1)
    a = list(rows)
    out = []
    for s in range(n):
        here = jnp.logical_and(lane_id >= SUB * s, lane_id < SUB * (s + 1))
        cols = [lane(a[s], SUB * s + r) for r in range(SUB)]
        r = jnp.where(here, jnp.where(row_id + SUB * s == lane_id, 1.0, 0.0), a[s])
        rb = [sub(r, q) for q in range(SUB)]
        t, m = invert_small(cols)
        v = tree_sum(m[q] * rb[q] for q in range(SUB))
        out.append(jnp.where(lane_id < SUB * (s + 1), v, 0.0))
        if s + 1 == n:
            break
        y = tree_sum(t[q] * rb[q] for q in range(SUB))
        yb = [sub(y, q) for q in range(SUB)]
        for i in range(s + 1, n):
            w = [lane(a[i], SUB * s + q) for q in range(SUB)]
            a[i] = jnp.where(here, 0.0, a[i]) + tree_sum(w[q] * yb[q] for q in range(SUB))
    return out


def subtract_products(dst, rows, cols, ah, al, bh, bl, depth, lower=False):
    if depth == 0:
        return
    tile = min(256, cols)
    for c in range(0, cols, tile):
        top = c if lower else 0
        a = (ah[top:rows, :depth], al[top:rows, :depth])
        b = (bh[c : c + tile, :depth], bl[c : c + tile, :depth])
        dst[top:rows, c : c + tile] = dst[top:rows, c : c + tile] - dot3(a, b, NT)


def times_inverse(src, outh, outl, out_at, rows, width, invh, invl):
    tile = min(256, width)
    a = split(src[:rows, :])
    for c in range(0, width, tile):
        part = tuple(x[:, : c + tile] for x in a)
        b = (invh[c : c + tile, : c + tile], invl[c : c + tile, : c + tile])
        high, low = split(dot3(part, b, NT))
        outh[:rows, out_at + c : out_at + c + tile] = high
        outl[:rows, out_at + c : out_at + c + tile] = low


def clear_inverse(invh, invl):
    invh[...] = jnp.zeros(invh.shape, BF16)
    invl[...] = jnp.zeros(invl.shape, BF16)


def inverse_row(r, at, width, lh, ll, invh, invl):
    here = ds(r * LANES, LANES)
    left = lax.broadcasted_iota(jnp.int32, (LANES, width), 1) < r * LANES
    none = jnp.zeros((LANES, width), BF16)
    low = tuple(jnp.where(left, ref[here, at : at + width], none) for ref in (lh, ll))
    mixed = split(dot3(low, (invh[...], invl[...]), NN))
    high, low = split(-dot3((invh[here, here], invl[here, here]), mixed, NN))
    invh[here, :] = jnp.where(left, high, invh[here, :])
    invl[here, :] = jnp.where(left, low, invl[here, :])


def factor_panels(start, stop, s_ref, at, width, lh, ll, invh, invl, job=None):
    row_id = lax.broadcasted_iota(jnp.int32, (width, LANES), 0)
    col_id = lax.broadcasted_iota(jnp.int32, (width, LANES), 1)
    none = jnp.zeros((width, LANES), BF16)
    last = width // LANES - 1

    def column(r, some):
        here = ds(r * LANES, LANES)
        inv = (invh[here, here], invl[here, here])
        solved = dot3(split(s_ref[:, here]), inv, NT)
        solved = jnp.where(jnp.logical_and(row_id >= col_id + r * LANES, some), solved, 0.0)
        high, low = split(solved)
        lh[:, ds(at + r * LANES, LANES)] = high
        ll[:, ds(at + r * LANES, LANES)] = low
        return high, low

    def panel(p, carry):
        first = p * LANES
        here = ds(first, LANES)
        block = [
            s_ref[pl.ds(pl.multiple_of(first + SUB * i, SUB), SUB), here]
            for i in range(LANES // SUB)
        ]
        before = jnp.maximum(p - 1, 0)
        high, low = column(before, p > 0)
        high = jnp.where(row_id >= first, high, none)
        low = jnp.where(row_id >= first, low, none)
        below = tuple(jnp.where(row_id >= first + LANES, x, none) for x in (high, low))
        for c in range(1, last + 1):
            rows = slice(c * LANES, None)
            cols = slice(c * LANES, (c + 1) * LANES)
            s_ref[rows, cols] = s_ref[rows, cols] - dot3(
                (below[0][rows], below[1][rows]), (high[cols], low[cols]), NT
            )
        inverse_row(before, at, width, lh, ll, invh, invl)
        if job is not None:
            job(p)

        inv = split(jnp.concatenate(factor_block(block), axis=0))
        invh[here, here] = inv[0]
        invl[here, here] = inv[1]
        following = ds(jnp.minimum(p + 1, last) * LANES, LANES)
        beside = split(jnp.where(p < last, dot3(split(s_ref[following, here]), inv, NT), 0.0))
        s_ref[following, following] = s_ref[following, following] - dot3(beside, beside, NT)
        return carry

    lax.fori_loop(start, stop, panel, 0)
    if stop == last + 1:
        column(last, True)
        inverse_row(last, at, width, lh, ll, invh, invl)


def solve_some(rows, src, q, width, xh, xl, l_rows, inv):
    part = src
    if q > 0:
        deep = q * width
        part = part - dot3(
            (xh[rows, :deep], xl[rows, :deep]), (l_rows[0][:, :deep], l_rows[1][:, :deep]), NT
        )
    high, low = split(dot3(split(part), (inv[0][...], inv[1][...]), NT))
    xh[rows, q * width : (q + 1) * width] = high
    xl[rows, q * width : (q + 1) * width] = low


def vmem_call(body, out_shapes, in_kinds, scratch, cost=None, aliases=None):
    spaces = {True: pltpu.SMEM, False: pltpu.VMEM, None: pl.ANY}
    specs = [pl.BlockSpec(memory_space=spaces[k]) for k in in_kinds]
    return pl.pallas_call(
        body,
        out_shape=out_shapes,
        in_specs=specs,
        out_specs=[pl.BlockSpec(memory_space=pltpu.VMEM)] * len(out_shapes),
        scratch_shapes=scratch,
        compiler_params=pltpu.CompilerParams(vmem_limit_bytes=VMEM_LIMIT),
        cost_estimate=cost,
        input_output_aliases=aliases or {},
    )


def shaped(shape, dtype):
    return jax.ShapeDtypeStruct(shape, dtype)


def send_plan(groups, per_stage):
    pairs = [
        (j, i)
        for i in range(groups)
        for j in range(i)
        if not (i == j + 1 and j % 2 == 0)
    ]
    pairs.sort(key=lambda pair: (pair[1] // per_stage, pair))
    taken = {}

    last = {}

    def place(pair, seen):
        for rnd in range(last[pair]):
            for dev in (pair[1], pair[0]):
                slot = (rnd, dev)
                if slot in seen:
                    continue
                seen.add(slot)
                if slot not in taken or place(taken[slot], seen):
                    taken[slot] = pair
                    return True
        return False

    limit = 1
    for pair in pairs:
        last[pair] = limit
        while not place(pair, set()):
            limit += 1
            last[pair] = limit
    rounds = 1 + max((slot[0] for slot in taken), default=-1)
    table = np.full((max(rounds, 1), groups), -1, np.int32)
    for (rnd, dev), (j, i) in taken.items():
        table[rnd, dev] = j if dev == i else i
    return table[:rounds]


def ring_order(groups):
    return [i for i in range(0, groups, 2)] + [i for i in range(groups - 1, 0, -2)]


def ring_gather(chunk, axis, groups):
    ring = Ring(chunk, axis, groups)
    for _ in range(ring.steps):
        ring.advance(None)
        ring.going, ring.coming = lax.optimization_barrier((ring.going, ring.coming))
    return ring.slots()


class Ring:
    def __init__(self, chunk, axis, groups):
        order = ring_order(groups)
        self.axis = axis
        self.ahead = [(order[i], order[(i + 1) % groups]) for i in range(groups)]
        self.back = [(b, a) for a, b in self.ahead]
        self.steps = groups // 2
        self.steps_back = groups - 1 - self.steps
        self.own = chunk
        self.aheads, self.backs = [], []
        self.going = self.coming = chunk

    def advance(self, token):
        if len(self.aheads) < self.steps:
            self.going = lax.ppermute(self.going, self.axis, self.ahead)
            self.aheads.append(self.going)
            if len(self.backs) < self.steps_back:
                self.coming = lax.ppermute(self.coming, self.axis, self.back)
                self.backs.append(self.coming)
        return token

    def arrive(self, token, beside):
        token, self.going, self.coming, _ = lax.optimization_barrier((token, self.going, self.coming, beside))
        return token

    def finish(self):
        while len(self.aheads) < self.steps:
            self.advance(None)

    def slots(self):
        return [self.own] + self.aheads + self.backs


def slot_owners(axis, groups):
    order = np.array(ring_order(groups), np.int32)
    place = np.argsort(order)
    me = jnp.asarray(place)[lax.axis_index(axis)]
    steps_ahead = groups // 2
    steps_back = groups - 1 - steps_ahead
    shifts = [0] + [-s for s in range(1, steps_ahead + 1)] + list(range(1, steps_back + 1))
    return jnp.asarray(order)[(me + jnp.asarray(shifts, jnp.int32)) % groups].astype(jnp.int32)


def direct_gather(x, axis, groups, sources):
    moved = [
        lax.ppermute(x, axis, [(s, (s + k) % groups) for s in range(sources)])
        for k in range(1, groups)
    ]
    return [x] + moved


def bulk_gather(x, axis, size, low_first=False, beside=None):
    held = {0: x}
    steps = [1 << bit for bit in range(size.bit_length() - 1)]
    for step in steps if low_first else reversed(steps):
        new = {
            mask | step: lax.ppermute(held[mask], axis, [(i, i ^ step) for i in range(size)])
            for mask in held
        }
        if beside is not None:
            new = {mask: after(value, beside()) for mask, value in new.items()}
            beside = None
        held.update(new)
    return [held[m] for m in range(size)]


def ranks(chosen):
    size = chosen.shape[-1]
    upto = jnp.arange(size)[:, None] <= jnp.arange(size)[None, :]
    counts = jnp.matmul(chosen.astype(BF16), upto.astype(BF16), preferred_element_type=F32)
    return counts.astype(jnp.int32) - 1


def after(x, dep):
    return lax.optimization_barrier((x, dep))[0]


def assemble_rows(q, width, own, groups, owner_ref, table_ref, chunks, late_rounds, a_ref):
    per_stage = width // own
    first_group = q * per_stage
    for k in range(groups):
        f = owner_ref[k]

        @pl.when(f // per_stage == q)
        def _(f=f, k=k):
            chunk = chunks[0][k]
            at = (f - first_group) * own
            a_ref[ds(at, own), ds(f * own, own)] = chunk[:own, :own]
            half = own // 2
            odd = f % 2
            row = (f - odd + 1 - first_group) * own + odd * half
            a_ref[ds(row, half), ds((f - odd) * own, own)] = chunk[:own, own:].T

    sent = [(rnd, chunk, 0) for rnd, chunk in enumerate(chunks[1:-1]) if chunk]
    sent += [(rnd, chunks[-1], at * own) for at, rnd in late_rounds]
    for rnd, chunk, cut in sent:
        for k in range(groups):
            f = owner_ref[k]
            c = table_ref[rnd, f]
            high = jnp.maximum(f, c)
            low = jnp.minimum(f, c)
            mine = jnp.logical_and(c >= 0, high // per_stage == q)
            row = jnp.clip((high - first_group) * own, 0, width - own)
            col = jnp.clip(low * own, 0, (q + 1) * width - own)

            @pl.when(jnp.logical_and(mine, f > c))
            def _(chunk=chunk, cut=cut, k=k, row=row, col=col):
                a_ref[ds(row, own), ds(col, own)] = chunk[k][:, cut : cut + own]

            @pl.when(jnp.logical_and(mine, f < c))
            def _(chunk=chunk, cut=cut, k=k, row=row, col=col):
                a_ref[ds(row, own), ds(col, own)] = chunk[k][:, cut : cut + own].T


def child_stage(q, width, own, groups, late_rounds, counts, span, couples, refs):
    start, stop = span
    panels = width // LANES
    refs = list(refs)

    def take(count):
        out, refs[:count] = refs[:count], []
        return out

    (place_ref,) = take(1)
    if start == 0:
        owner_ref, table_ref = take(2)
        chunks = [take(count) for count in counts]
    else:
        state = take(5)
    prev_lh, prev_ll, prev_ih, prev_il = (take(q) for _ in range(4))
    if couples:
        b_ref = take(1)[0]
        old_x = take(2) if q > 1 else None
    s_out, lh, ll, invh, invl = take(5)
    if couples:
        xh, xl = take(2)
    if stop == panels:
        own_ref = take(1)[0]
    if start == 0:
        a_ref = take(1)[0]

    if start == 0:
        assemble_rows(q, width, own, groups, owner_ref, table_ref, chunks, late_rounds, a_ref)
        for j in range(q):
            part = a_ref.at[:, j * width : (j + 1) * width]
            subtract_products(part, width, width, lh, ll, prev_lh[j], prev_ll[j], j * width)
            times_inverse(part, lh, ll, j * width, width, width, prev_ih[j], prev_il[j])
        s_out[...] = a_ref[:, q * width : (q + 1) * width]
        subtract_products(s_out, width, width, lh, ll, lh, ll, q * width, True)
        clear_inverse(invh, invl)
    else:
        for new, held in zip((s_out, lh, ll, invh, invl), state, strict=True):
            new[...] = held[...]
    if couples and q > 1:
        xh[:, : (q - 1) * width] = old_x[0][...]
        xl[:, : (q - 1) * width] = old_x[1][...]
    def job(p):
        if couples:
            some = own // (stop - start)
            rows = ds((p - start) * some, some)
            solve_some(
                rows, b_ref[rows, :], q - 1, width, xh, xl,
                (prev_lh[q - 1], prev_ll[q - 1]), (prev_ih[q - 1], prev_il[q - 1]),
            )

    factor_panels(start, stop, s_out, q * width, width, lh, ll, invh, invl, job)
    if stop == panels:
        at = place_ref[0]
        own_ref[...] = lh[ds(at, own), :].astype(F32) + ll[ds(at, own), :].astype(F32)


def landing_kernel(stages, sources, cap, refs):
    refs = list(refs)

    def take(count):
        out, refs[:count] = refs[:count], []
        return out

    lh, ll, ih, il = (take(stages) for _ in range(4))
    (raw_ref, th, tl, sq_ref, t_ref, copy_sems) = take(6)
    front = raw_ref.shape[0]
    total = sources * cap
    width = ih[0].shape[0]
    share = total // front
    copies = []
    for f in range(front):
        at = (f % sources) * cap + (f // sources) * share
        copies.append(
            pltpu.make_async_copy(
                raw_ref.at[f, :share, :], t_ref.at[at : at + share, :], copy_sems.at[f]
            )
        )
        copies[-1].start()
    for copy in copies:
        copy.wait()
    for q in range(stages):
        part = t_ref.at[:, q * width : (q + 1) * width]
        subtract_products(part, total, width, th, tl, lh[q], ll[q], q * width)
        times_inverse(part, th, tl, q * width, total, width, ih[q], il[q])

    def square(t, carry):
        i, j = carry
        a = (th[ds(i * LANES, LANES), :], tl[ds(i * LANES, LANES), :])
        b = (th[ds(j * LANES, LANES), :], tl[ds(j * LANES, LANES), :])
        sq_ref[t] = dot3(a, b, NT)
        end = j == i
        return (jnp.where(end, i + 1, i), jnp.where(end, 0, j + 1))

    blocks = total // LANES
    lax.fori_loop(0, blocks * (blocks + 1) // 2, square, (jnp.int32(0), jnp.int32(0)))


def own_kernel(first, stages, width, refs):
    refs = list(refs)

    def take(count):
        out, refs[:count] = refs[:count], []
        return out

    (b_ref,) = take(1)
    old_h, old_l = take(2) if first > 0 else (None, None)
    left = stages - first
    lh, ll, ih, il = (take(left) for _ in range(4))
    th, tl = take(2)
    x_ref, con_ref = take(2)
    xh, xl = take(2)
    own = b_ref.shape[0]
    if first > 0:
        xh[:, : first * width] = old_h[...]
        xl[:, : first * width] = old_l[...]
    for k in range(left):
        q = first + k
        for c in range(1):
            part = b_ref.at[:, k * width : (k + 1) * width]
            x_ref[:, q * width : (q + 1) * width] = part[...]
            part = x_ref.at[:, q * width : (q + 1) * width]
            subtract_products(part, own, width, xh, xl, lh[k], ll[k], q * width)
            times_inverse(part, xh, xl, q * width, own, width, ih[k], il[k])
    x_ref[...] = xh[...].astype(F32) + xl[...].astype(F32)

    def body(r, nr, c, nc):
        a = (xh[ds(r, nr), :], xl[ds(r, nr), :])
        b = (th[ds(c, nc), :], tl[ds(c, nc), :])
        con_ref[ds(r, nr), ds(c, nc)] = dot3(a, b, NT)

    tiles(own, con_ref.shape[1], body)


def parent_kernel(children, blocks, width, sources, refs):
    refs = list(refs)
    place_ref, spread_ref = refs[:2]
    tops, squares = refs[2 : 2 + children], refs[2 + children : 2 + 2 * children]
    lh, ll, invh, invl, s_ref, top_ref = refs[2 + 2 * children :]
    pivots = lh.shape[0]
    dense = pivots // blocks
    groups, part_rows, _ = tops[0].shape
    spreads = groups // sources
    piece = part_rows * spreads
    for m in range(children):
        g = place_ref[2] ^ m
        for f in range(groups):
            at = (f % sources) * (children * piece) + g * piece + (f // sources) * part_rows
            top_ref[ds(at, part_rows), :] = tops[m][f]
    for i in range(blocks):
        for j in range(i + 1):
            at = i * (i + 1) // 2 + j
            parts = []
            for c in range(children):
                left = spread_ref[i, :, c * LANES : (c + 1) * LANES]
                high, low = split(squares[c][at])
                parts.append(dot(left, high, NN) + dot(left, low, NN))
            high, low = split(jnp.concatenate(parts, axis=1))
            right = spread_ref[j]
            rows = slice(i * dense, (i + 1) * dense)
            cols = slice(j * dense, (j + 1) * dense)
            s_ref[rows, cols] = top_ref[rows, cols] - (
                dot(high, right, NT) + dot(low, right, NT)
            )
    for q in range(pivots // width):
        rows = slice(q * width, (q + 1) * width)
        lhq, llq = lh.at[rows, :], ll.at[rows, :]
        if q + 1 < pivots // width:
            lhq[:, (q + 1) * width :] = jnp.zeros((width, pivots - (q + 1) * width), BF16)
            llq[:, (q + 1) * width :] = jnp.zeros((width, pivots - (q + 1) * width), BF16)
        for j in range(q):
            part = s_ref.at[rows, j * width : (j + 1) * width]
            cut = slice(j * width, (j + 1) * width)
            subtract_products(part, width, width, lhq, llq, lh.at[cut, :], ll.at[cut, :], j * width)
            times_inverse(part, lhq, llq, j * width, width, width, invh.at[j], invl.at[j])
        part = s_ref.at[rows, q * width : (q + 1) * width]
        subtract_products(part, width, width, lhq, llq, lhq, llq, q * width, True)
        clear_inverse(invh.at[q], invl.at[q])
        factor_panels(0, width // LANES, part, q * width, width, lhq, llq, invh.at[q], invl.at[q])


def rest_kernel(children, blocks, width, refs):
    refs = list(refs)
    place_ref, rows_ref, route_ref, spread_ref = refs[:4]
    con_refs = refs[4 : 4 + children]
    lh, ll, invh, invl, out_ref, s_ref, xh, xl = refs[4 + children :]
    pivots = lh.shape[0]
    count = rows_ref.shape[0]
    dense = pivots // blocks
    at = place_ref[1]

    @pl.when(at < pivots)
    def _():
        row = ds(jnp.minimum(at, pivots - count), count)
        out_ref[...] = lh[row, :].astype(F32) + ll[row, :].astype(F32)

    @pl.when(at >= pivots)
    def _():
        routed = []
        for c in range(children):
            high, low = split(con_refs[c][...])
            route = route_ref[c]
            routed.append(split(dot(route, high, NN) + dot(route, low, NN)))
        for b in range(blocks):
            lanes = slice(b * LANES, (b + 1) * LANES)
            high = jnp.concatenate([routed[c][0][:, lanes] for c in range(children)], axis=1)
            low = jnp.concatenate([routed[c][1][:, lanes] for c in range(children)], axis=1)
            right = spread_ref[b]
            cols = slice(b * dense, (b + 1) * dense)
            s_ref[:, cols] = rows_ref[:, cols] - (dot(high, right, NT) + dot(low, right, NT))
        for q in range(pivots // width):
            cut = slice(q * width, (q + 1) * width)
            part = s_ref.at[:, cut]
            subtract_products(part, count, width, xh, xl, lh.at[cut, :], ll.at[cut, :], q * width)
            times_inverse(part, xh, xl, q * width, count, width, invh.at[q], invl.at[q])
        out_ref[...] = xh[...].astype(F32) + xl[...].astype(F32)


def on_device(child_pivot, child_coupling, parent_arrow, row_map, block_pattern):
    front = lax.axis_size("front")
    bulk = lax.axis_size("bulk")
    me = lax.axis_index("front")
    mine = child_pivot[0]
    coupling = child_coupling[0]
    own, total = mine.shape
    count, pivots = parent_arrow.shape
    width = min(STAGE, total)
    stages = total // width
    per_stage = width // own
    first_row = (lax.axis_index("bulk") * front + me) * count
    sources = pivots // count
    cap = min(CAP, count, own)
    blocks = sources * cap // LANES

    table = send_plan(front, per_stage)
    rounds = table.shape[0]
    bulk_me = lax.axis_index("bulk")
    early = max(
        (r + 1 for r in range(rounds) for f, c in enumerate(table[r]) if c >= 0 and max(f, c) // per_stage <= 1),
        default=0,
    )
    half = own // 2
    own_map = row_map[0]
    own_block = lax.dynamic_slice_in_dim(mine, me * own, own, 1)
    even = lax.dynamic_slice_in_dim(mine, jnp.minimum(me + 1, front - 1) * own, half, 1)
    odd = lax.dynamic_slice_in_dim(mine[half:], jnp.maximum(me - 1, 0) * own, own, 1).T
    head = jnp.concatenate([own_block, jnp.where(me % 2 == 0, even, odd)], axis=1)
    tail = jnp.pad(own_map.astype(F32)[None], ((0, SUB - 1), (0, half)))
    chunks = [jnp.concatenate([head, tail], axis=0)]
    mine_later, table_me = after((mine, jnp.asarray(table)[:, me]), chunks[0])
    for rnd in range(rounds):
        col = jnp.maximum(table_me[rnd], 0)
        chunks.append(lax.dynamic_slice_in_dim(mine_later, col * own, own, 1))
    owners = slot_owners("front", front)
    gathered = [ring_gather(chunks[0], "front", front)]
    started = gathered[0][1:]
    for rnd in range(1, early + 1):
        gathered.append(ring_gather(after(chunks[rnd], gathered[-1][1:]), "front", front))
    here = gathered[-1][1:]
    late = Ring(after(jnp.concatenate(chunks[early + 1 :], axis=1), here), "front", front)
    table_in = jnp.asarray(table)
    place = jnp.stack([(me % per_stage) * own, first_row, bulk_me]).astype(jnp.int32)

    own_lands = own_map < pivots
    own_rank = jnp.where(own_lands, ranks(own_lands), -1)
    pick = (own_rank[None, :] == jnp.arange(cap)[:, None]).astype(F32)
    spreads = front // sources

    def spread_out(x):
        rows = x.shape[0] // spreads
        part = x[:rows]
        for k in range(1, spreads):
            moved = lax.ppermute(
                x[k * rows : (k + 1) * rows],
                "front",
                [(s, s + k * sources) for s in range(sources)],
            )
            part = jnp.where(me // sources == k, moved, part)
        return part

    compact = jnp.dot(pick, coupling, precision=HIGHEST_PRECISION)
    place = after(place, here)
    block_rows = (first_row + jnp.arange(count)) // BLOCK
    row_mask = jnp.take(block_pattern, block_rows, axis=0).astype(F32)
    arrow = parent_arrow * jnp.repeat(row_mask, BLOCK, axis=1)
    piece = count // bulk
    my_maps = jnp.stack([slot[own, :own] for slot in gathered[0]])
    ordered = jnp.sum(
        jnp.where(owners[None, :, None] == jnp.arange(front)[:, None, None], my_maps[None], 0.0), axis=1
    )
    sent = {}

    def send_first(token):
        part = after(arrow, token)
        pieces = part[:piece]
        for g in range(1, bulk):
            moved = lax.ppermute(part[g * piece : (g + 1) * piece], "bulk", [(0, g)])
            pieces = jnp.where(bulk_me == g, moved, pieces)
        sent["pieces"] = pieces
        sent["maps"] = jnp.stack(bulk_gather(after(ordered, token), "bulk", bulk)).astype(jnp.int32)
        return pieces, sent["maps"]

    def send_second(token):
        sent["landing"] = spread_out(after(compact, token))
        sent["line"] = spread_out(after(sent["pieces"], token))
        return sent["landing"], sent["line"]

    def send_third(token):
        landing, line = sent["landing"], sent["line"]
        extra = line.reshape(-1, total)
        padding = jnp.zeros((-extra.shape[0] % SUB, total), F32)
        both = after(jnp.concatenate([landing, extra, padding], axis=0), token)
        sent["all"] = lax.all_gather(both, "front", axis=0, tiled=False)
        share = landing.shape[0]
        sent["lines"] = sent["all"][:, share : share + extra.shape[0]].reshape((front,) + line.shape)
        return both

    hooks = [send_first, send_second, send_third]

    panels = width // LANES
    total_landing = sources * cap
    lh, ll, ih, il, owned = ([] for _ in range(5))
    xs = None
    for q in range(stages):
        final = q == stages - 1
        if q == 2 or (q < 2 and final):
            late.finish()
        split_at = [0, panels // 2, panels] if q < 2 and not final else [0, panels]
        needed = [
            any(c >= 0 and max(f, c) // per_stage == q for f, c in enumerate(row)) for row in table
        ]
        used = [gathered[0]] + [gathered[rnd + 1] if needed[rnd] else [] for rnd in range(early)]
        late_rounds = [(rnd - early, rnd) for rnd in range(early, rounds) if needed[rnd]]
        used.append(late.slots() if late_rounds else [])
        counts = [len(u) for u in used]
        deep = (q + 1) * width
        state = None
        for start, stop in zip(split_at[:-1], split_at[1:], strict=True):
            couples = 0 < q < stages - 1 and stop == panels
            if q < 2 and not final:
                place = late.advance(place)
            operands = [place]
            smem = 1
            aliases = {}
            if start == 0:
                operands += [owners, table_in] + [x for u in used for x in u]
                smem = 3
            else:
                operands += state
                aliases = {1 + k: k for k in range(5)}
            operands += lh + ll + ih + il
            if couples:
                operands.append(coupling[:, (q - 1) * width : q * width])
                if q > 1:
                    operands += xs
            outs = [
                shaped((width, width), F32),
                shaped((width, deep), BF16),
                shaped((width, deep), BF16),
                shaped((width, width), BF16),
                shaped((width, width), BF16),
            ]
            scratch = []
            if couples:
                outs += [shaped((own, q * width), BF16)] * 2
            if stop == panels:
                outs.append(shaped((own, deep), F32))
            if start == 0:
                scratch.append(pltpu.VMEM((width, deep), F32))
            out = list(
                vmem_call(
                    functools.partial(
                        lambda *refs, args: child_stage(*args, refs),
                        args=(
                            q, width, own, front, late_rounds, counts, (start, stop),
                            couples,
                        ),
                    ),
                    outs,
                    [True] * smem
                    + [False] * (len(operands) - smem),
                    scratch,
                    pl.CostEstimate(
                        flops=6_000_000_000 * (stop - start), bytes_accessed=1 << 20, transcendentals=0
                    ),
                    aliases,
                )(*operands)
            )
            state = out[:5]
            rest = out[5:]
            if couples:
                xs, rest = rest[:2], rest[2:]
            if stop == panels:
                owned.append(rest[0])
                rest = rest[1:]
            if q < 2 and not final:
                place = late.arrive(place, state[0])
                if hooks:
                    place = after(place, hooks.pop(0)((late.going, late.coming, place)))
        for held, new in zip((lh, ll, ih, il), state[1:], strict=True):
            held.append(new)

    for hook in hooks:
        hook(place)
    maps = sent["maps"]
    lands = maps[:, :sources] < pivots
    rank = ranks(lands)
    overflow = jnp.any(rank[:, :, -1] >= cap)
    chosen = jnp.where(lands, rank, -1)[:, :, None, :] == jnp.arange(cap)[:, None]
    target = jnp.max(jnp.where(chosen, maps[:, :sources, None, :], -1), axis=3)
    target = jnp.where(overflow, -1, target).reshape(bulk, blocks, LANES)
    dense = pivots // blocks
    rows_of = (jnp.arange(blocks)[:, None] * dense + jnp.arange(dense)[None, :])[:, :, None, None]
    spread = (jnp.transpose(target, (1, 0, 2))[:, None] == rows_of).astype(BF16)
    spread = spread.reshape(blocks, dense, bulk * LANES)
    route = (
        lax.dynamic_index_in_dim(maps, me, 1, False)[:, None, :]
        == (first_row + jnp.arange(count))[None, :, None]
    ).astype(BF16)

    operands = lh + ll + ih + il
    th, tl, squares = vmem_call(
        lambda *refs: landing_kernel(stages, sources, cap, refs),
        [
            shaped((total_landing, total), BF16),
            shaped((total_landing, total), BF16),
            shaped((blocks * (blocks + 1) // 2, LANES, LANES), F32),
        ],
        [False] * len(operands) + [None],
        [pltpu.VMEM((total_landing, total), F32), pltpu.SemaphoreType.DMA((front,))],
        pl.CostEstimate(flops=20_000_000_000, bytes_accessed=1 << 20, transcendentals=0),
    )(*operands, sent["all"])

    lower_rows = jnp.zeros((own, total), F32)
    for q in range(stages):
        padded = jnp.pad(owned[q], ((0, 0), (0, total - (q + 1) * width)))
        lower_rows = jnp.where(me // per_stage == q, padded, lower_rows)

    solved = max(stages - 2, 0)
    operands = [coupling[:, solved * width :]] + (xs if solved > 0 else [])
    operands += lh[solved:] + ll[solved:] + ih[solved:] + il[solved:] + [th, tl]
    x_own, con = vmem_call(
        lambda *refs: own_kernel(solved, stages, width, refs),
        [shaped((own, total), F32), shaped((own, total_landing), F32)],
        [False] * len(operands),
        [pltpu.VMEM((own, total), BF16)] * 2,
        pl.CostEstimate(flops=10_000_000_000, bytes_accessed=1 << 20, transcendentals=0),
    )(*operands)
    all_squares = bulk_gather(squares, "bulk", bulk, beside=lambda: con)

    def unchanged(lines, arrow, x_own):
        return lines, arrow

    def landing_whole(lines, arrow, x_own):
        slot = own_map - me * count
        hits = (slot[:, None] == jnp.arange(count)[None, :]).astype(F32)
        piece_rows = jnp.dot(hits.T, x_own, precision=HIGHEST_PRECISION)
        whole = lax.all_gather(piece_rows, "front", axis=0, tiled=True)[:pivots]
        reached = jnp.dot(x_own, whole.T, precision=HIGHEST_PRECISION)
        slot_index = own_map // count // front * count + own_map % count
        routing = (slot_index[:, None] == jnp.arange(bulk * count)[None, :]).astype(F32)
        added = lax.psum_scatter(
            jnp.dot(routing.T, reached, precision=HIGHEST_PRECISION),
            "bulk",
            scatter_dimension=0,
            tiled=True,
        )
        square = lax.psum(jnp.dot(whole, whole.T, precision=HIGHEST_PRECISION), "bulk")
        square = square.reshape(sources, bulk, spreads, piece // spreads, pivots)
        square = jnp.transpose(square, (1, 2, 0, 3, 4)).reshape(bulk, front, piece // spreads, pivots)
        changed = [
            lines[m] - lax.dynamic_index_in_dim(square, bulk_me ^ m, 0, False) for m in range(bulk)
        ]
        return changed, arrow - added

    lines = bulk_gather(sent["lines"], "bulk", bulk)
    lines, arrow = lax.cond(overflow, landing_whole, unchanged, lines, arrow, x_own)

    all_con = bulk_gather(con, "bulk", bulk, low_first=True)
    plh, pll, pih, pil = vmem_call(
        lambda *refs: parent_kernel(bulk, blocks, width, sources, refs),
        [
            shaped((pivots, pivots), BF16),
            shaped((pivots, pivots), BF16),
            shaped((pivots // width, width, width), BF16),
            shaped((pivots // width, width, width), BF16),
        ],
        [True] + [False] * (1 + 2 * bulk),
        [pltpu.VMEM((pivots, pivots), F32)] * 2,
        pl.CostEstimate(flops=60_000_000_000, bytes_accessed=1 << 24, transcendentals=0),
    )(place, spread, *lines, *all_squares)

    (parent_rows,) = vmem_call(
        lambda *refs: rest_kernel(bulk, blocks, width, refs),
        [shaped((count, pivots), F32)],
        [True] + [False] * (7 + bulk),
        [
            pltpu.VMEM((count, pivots), F32),
            pltpu.VMEM((count, pivots), BF16),
            pltpu.VMEM((count, pivots), BF16),
        ],
    )(place, arrow, route, spread, *all_con, plh, pll, pih, pil)
    return (lower_rows[None], x_own[None], parent_rows)


def solution(mesh):
    placed = (
        P("bulk", "front", None),
        P("bulk", "front", None),
        P(("bulk", "front"), None),
        P("bulk", "front"),
        P(),
    )
    return jax.shard_map(
        on_device,
        mesh=mesh,
        in_specs=placed,
        out_specs=(P("bulk", "front", None), P("bulk", "front", None), P(("bulk", "front"), None)),
        check_vma=False,
    )
```

```python
import functools

import jax
import jax.numpy as jnp
import numpy as np
from jax import lax
from jax.experimental import pallas as pl
from jax.experimental.pallas import tpu as pltpu
from jax.sharding import PartitionSpec as P

BLOCK = 128
STAGE = 512
CAP = 128
LANES = 128
SUB = 8
VMEM_LIMIT = 60 << 20

HIGHEST_PRECISION = lax.Precision.HIGHEST
NT = (((1,), (1,)), ((), ()))
NN = (((1,), (0,)), ((), ()))
TN = (((0,), (0,)), ((), ()))
F32 = jnp.float32
BF16 = jnp.bfloat16


def split(x):
    high = x.astype(BF16)
    return high, (x - high.astype(F32)).astype(BF16)


def dot(a, b, dims):
    return lax.dot_general(a, b, dims, preferred_element_type=F32)


def dot3(a, b, dims):
    return dot(a[0], b[0], dims) + (dot(a[0], b[1], dims) + dot(a[1], b[0], dims))


def ds(start, size):
    return pl.ds(pl.multiple_of(start, size), size)


def tiles(rows, cols, body, tile=256):
    tr, tc = min(tile, rows), min(tile, cols)
    nr, nc = rows // tr, cols // tc

    def step(t, carry):
        body((t // nc) * tr, tr, (t % nc) * tc, tc)
        return carry

    lax.fori_loop(0, nr * nc, step, 0)


def lane(x, c):
    return jnp.broadcast_to(x[:, c : c + 1], x.shape)


def sub(x, r):
    return jnp.broadcast_to(x[r : r + 1, :], x.shape)


def tree_sum(terms):
    terms = list(terms)
    while len(terms) > 1:
        terms = [
            terms[i] + terms[i + 1] if i + 1 < len(terms) else terms[i]
            for i in range(0, len(terms), 2)
        ]
    return terms[0]


def invert_small(s):
    n = len(s)
    s = list(s)
    row_id = lax.broadcasted_iota(jnp.int32, (SUB, LANES), 0)
    m = [None] * n
    for p in range(0, n, 2):
        q = p + 1
        a, b, d = sub(s[p], p), sub(s[q], p), sub(s[q], q)
        det = a * d - b * b
        scale = 1.0 / det
        ra = lax.rsqrt(a)
        rq = lax.rsqrt(det) * (a * ra)
        ba = b * ra * ra
        at_p, at_q = row_id == p, row_id == q
        sp, sq = s[p], s[q]
        fp, fq = (sp * d - sq * b) * scale, (sq * a - sp * b) * scale
        for k in range(n):
            if k in (p, q):
                continue
            u, v = sub(s[k], p), sub(s[k], q)
            if k < p:
                m[k] = jnp.where(at_p, -(u * ra), jnp.where(at_q, (u * ba - v) * rq, m[k]))
            s[k] = jnp.where(at_p, sub(fp, k), jnp.where(at_q, sub(fq, k), s[k] - (fp * u + fq * v)))
        s[p] = jnp.where(at_p, -(d * scale), jnp.where(at_q, b * scale, fp))
        s[q] = jnp.where(at_q, -(a * scale), jnp.where(at_p, b * scale, fq))
        m[p] = jnp.where(at_p, ra, jnp.where(at_q, -(ba * rq), 0.0))
        m[q] = jnp.where(at_q, rq, 0.0)
    return s, m


def factor_block(rows):
    n = len(rows)
    row_id = lax.broadcasted_iota(jnp.int32, (SUB, LANES), 0)
    lane_id = lax.broadcasted_iota(jnp.int32, (SUB, LANES), 1)
    a = list(rows)
    out = []
    for s in range(n):
        here = jnp.logical_and(lane_id >= SUB * s, lane_id < SUB * (s + 1))
        cols = [lane(a[s], SUB * s + r) for r in range(SUB)]
        r = jnp.where(here, jnp.where(row_id + SUB * s == lane_id, 1.0, 0.0), a[s])
        rb = [sub(r, q) for q in range(SUB)]
        t, m = invert_small(cols)
        v = tree_sum(m[q] * rb[q] for q in range(SUB))
        out.append(jnp.where(lane_id < SUB * (s + 1), v, 0.0))
        if s + 1 == n:
            break
        y = tree_sum(t[q] * rb[q] for q in range(SUB))
        yb = [sub(y, q) for q in range(SUB)]
        for i in range(s + 1, n):
            w = [lane(a[i], SUB * s + q) for q in range(SUB)]
            a[i] = jnp.where(here, 0.0, a[i]) + tree_sum(w[q] * yb[q] for q in range(SUB))
    return out


def subtract_products(dst, rows, cols, ah, al, bh, bl, depth, lower=False):
    if depth == 0:
        return
    tile = min(256, cols)
    for c in range(0, cols, tile):
        top = c if lower else 0
        a = (ah[top:rows, :depth], al[top:rows, :depth])
        b = (bh[c : c + tile, :depth], bl[c : c + tile, :depth])
        dst[top:rows, c : c + tile] = dst[top:rows, c : c + tile] - dot3(a, b, NT)


def times_inverse(src, outh, outl, out_at, rows, width, invh, invl):
    tile = min(256, width)
    a = split(src[:rows, :])
    for c in range(0, width, tile):
        part = tuple(x[:, : c + tile] for x in a)
        b = (invh[c : c + tile, : c + tile], invl[c : c + tile, : c + tile])
        high, low = split(dot3(part, b, NT))
        outh[:rows, out_at + c : out_at + c + tile] = high
        outl[:rows, out_at + c : out_at + c + tile] = low


def clear_inverse(invh, invl):
    invh[...] = jnp.zeros(invh.shape, BF16)
    invl[...] = jnp.zeros(invl.shape, BF16)


def inverse_row(r, at, width, lh, ll, invh, invl):
    here = ds(r * LANES, LANES)
    left = lax.broadcasted_iota(jnp.int32, (LANES, width), 1) < r * LANES
    none = jnp.zeros((LANES, width), BF16)
    low = tuple(jnp.where(left, ref[here, at : at + width], none) for ref in (lh, ll))
    mixed = split(dot3(low, (invh[...], invl[...]), NN))
    high, low = split(-dot3((invh[here, here], invl[here, here]), mixed, NN))
    invh[here, :] = jnp.where(left, high, invh[here, :])
    invl[here, :] = jnp.where(left, low, invl[here, :])


def factor_panels(start, stop, s_ref, at, width, lh, ll, invh, invl, job=None):
    row_id = lax.broadcasted_iota(jnp.int32, (width, LANES), 0)
    col_id = lax.broadcasted_iota(jnp.int32, (width, LANES), 1)
    none = jnp.zeros((width, LANES), BF16)
    last = width // LANES - 1

    def column(r, some):
        here = ds(r * LANES, LANES)
        inv = (invh[here, here], invl[here, here])
        solved = dot3(split(s_ref[:, here]), inv, NT)
        solved = jnp.where(jnp.logical_and(row_id >= col_id + r * LANES, some), solved, 0.0)
        high, low = split(solved)
        lh[:, ds(at + r * LANES, LANES)] = high
        ll[:, ds(at + r * LANES, LANES)] = low
        return high, low

    def panel(p, carry):
        first = p * LANES
        here = ds(first, LANES)
        block = [
            s_ref[pl.ds(pl.multiple_of(first + SUB * i, SUB), SUB), here]
            for i in range(LANES // SUB)
        ]
        before = jnp.maximum(p - 1, 0)
        high, low = column(before, p > 0)
        high = jnp.where(row_id >= first, high, none)
        low = jnp.where(row_id >= first, low, none)
        below = tuple(jnp.where(row_id >= first + LANES, x, none) for x in (high, low))
        for c in range(1, last + 1):
            rows = slice(c * LANES, None)
            cols = slice(c * LANES, (c + 1) * LANES)
            s_ref[rows, cols] = s_ref[rows, cols] - dot3(
                (below[0][rows], below[1][rows]), (high[cols], low[cols]), NT
            )
        inverse_row(before, at, width, lh, ll, invh, invl)
        if job is not None:
            job(p)

        inv = split(jnp.concatenate(factor_block(block), axis=0))
        invh[here, here] = inv[0]
        invl[here, here] = inv[1]
        following = ds(jnp.minimum(p + 1, last) * LANES, LANES)
        beside = split(jnp.where(p < last, dot3(inv, split(s_ref[following, here]), NT), 0.0))
        s_ref[following, following] = s_ref[following, following] - dot3(beside, beside, TN)
        return carry

    lax.fori_loop(start, stop, panel, 0)
    if stop == last + 1:
        column(last, True)
        inverse_row(last, at, width, lh, ll, invh, invl)


def solve_some(rows, src, q, width, xh, xl, l_rows, inv):
    part = src
    if q > 0:
        deep = q * width
        part = part - dot3(
            (xh[rows, :deep], xl[rows, :deep]), (l_rows[0][:, :deep], l_rows[1][:, :deep]), NT
        )
    high, low = split(dot3(split(part), (inv[0][...], inv[1][...]), NT))
    xh[rows, q * width : (q + 1) * width] = high
    xl[rows, q * width : (q + 1) * width] = low


def vmem_call(body, out_shapes, in_kinds, scratch, cost=None, aliases=None, out_kinds=None):
    spaces = {True: pltpu.SMEM, False: pltpu.VMEM, None: pl.ANY}
    specs = [pl.BlockSpec(memory_space=spaces[k]) for k in in_kinds]
    return pl.pallas_call(
        body,
        out_shape=out_shapes,
        in_specs=specs,
        out_specs=[
            pl.BlockSpec(memory_space=spaces[k]) for k in out_kinds or [False] * len(out_shapes)
        ],
        scratch_shapes=scratch,
        compiler_params=pltpu.CompilerParams(vmem_limit_bytes=VMEM_LIMIT),
        cost_estimate=cost,
        input_output_aliases=aliases or {},
    )


def shaped(shape, dtype):
    return jax.ShapeDtypeStruct(shape, dtype)


def send_plan(groups, per_stage):
    pairs = [
        (j, i)
        for i in range(groups)
        for j in range(i)
        if not (i == j + 1 and j % 2 == 0)
    ]
    pairs.sort(key=lambda pair: (pair[1] // per_stage, pair))
    taken = {}

    last = {}

    def place(pair, seen):
        for rnd in range(last[pair]):
            for dev in (pair[1], pair[0]):
                slot = (rnd, dev)
                if slot in seen:
                    continue
                seen.add(slot)
                if slot not in taken or place(taken[slot], seen):
                    taken[slot] = pair
                    return True
        return False

    limit = 1
    for pair in pairs:
        last[pair] = limit
        while not place(pair, set()):
            limit += 1
            last[pair] = limit
    rounds = 1 + max((slot[0] for slot in taken), default=-1)
    table = np.full((max(rounds, 1), groups), -1, np.int32)
    for (rnd, dev), (j, i) in taken.items():
        table[rnd, dev] = j if dev == i else i
    return table[:rounds]


def ring_order(groups):
    return [i for i in range(0, groups, 2)] + [i for i in range(groups - 1, 0, -2)]


def ring_gather(chunk, axis, groups):
    ring = Ring(chunk, axis, groups)
    for _ in range(ring.steps):
        ring.advance(None)
        ring.going, ring.coming = lax.optimization_barrier((ring.going, ring.coming))
    return ring.slots()


class Ring:
    def __init__(self, chunk, axis, groups):
        order = ring_order(groups)
        self.axis = axis
        self.ahead = [(order[i], order[(i + 1) % groups]) for i in range(groups)]
        self.back = [(b, a) for a, b in self.ahead]
        self.steps = groups // 2
        self.steps_back = groups - 1 - self.steps
        self.own = chunk
        self.aheads, self.backs = [], []
        self.going = self.coming = chunk

    def advance(self, token):
        if len(self.aheads) < self.steps:
            self.going = lax.ppermute(self.going, self.axis, self.ahead)
            self.aheads.append(self.going)
            if len(self.backs) < self.steps_back:
                self.coming = lax.ppermute(self.coming, self.axis, self.back)
                self.backs.append(self.coming)
        return token

    def arrive(self, token, beside):
        token, self.going, self.coming, _ = lax.optimization_barrier((token, self.going, self.coming, beside))
        return token

    def finish(self):
        while len(self.aheads) < self.steps:
            self.advance(None)

    def slots(self):
        return [self.own] + self.aheads + self.backs


def slot_owners(axis, groups):
    order = np.array(ring_order(groups), np.int32)
    place = np.argsort(order)
    me = jnp.asarray(place)[lax.axis_index(axis)]
    steps_ahead = groups // 2
    steps_back = groups - 1 - steps_ahead
    shifts = [0] + [-s for s in range(1, steps_ahead + 1)] + list(range(1, steps_back + 1))
    return jnp.asarray(order)[(me + jnp.asarray(shifts, jnp.int32)) % groups].astype(jnp.int32)


def direct_gather(x, axis, groups, sources):
    moved = [
        lax.ppermute(x, axis, [(s, (s + k) % groups) for s in range(sources)])
        for k in range(1, groups)
    ]
    return [x] + moved


def bulk_gather(x, axis, size, low_first=False, beside=None):
    held = {0: x}
    steps = [1 << bit for bit in range(size.bit_length() - 1)]
    for step in steps if low_first else reversed(steps):
        new = {
            mask | step: lax.ppermute(held[mask], axis, [(i, i ^ step) for i in range(size)])
            for mask in held
        }
        if beside is not None:
            new = {mask: after(value, beside()) for mask, value in new.items()}
            beside = None
        held.update(new)
    return [held[m] for m in range(size)]


def ranks(chosen):
    size = chosen.shape[-1]
    upto = jnp.arange(size)[:, None] <= jnp.arange(size)[None, :]
    counts = jnp.matmul(chosen.astype(BF16), upto.astype(BF16), preferred_element_type=F32)
    return counts.astype(jnp.int32) - 1


def after(x, dep):
    return lax.optimization_barrier((x, dep))[0]


def assemble_rows(q, width, own, groups, owner_ref, table_ref, chunks, late_rounds, a_ref):
    per_stage = width // own
    first_group = q * per_stage
    for k in range(groups):
        f = owner_ref[k]

        @pl.when(f // per_stage == q)
        def _(f=f, k=k):
            chunk = chunks[0][k]
            at = (f - first_group) * own
            a_ref[ds(at, own), ds(f * own, own)] = chunk[:own, :own]
            half = own // 2
            odd = f % 2
            row = (f - odd + 1 - first_group) * own + odd * half
            a_ref[ds(row, half), ds((f - odd) * own, own)] = chunk[:own, own:].T

    sent = [(rnd, chunk, 0) for rnd, chunk in enumerate(chunks[1:-1]) if chunk]
    sent += [(rnd, chunks[-1], at * own) for at, rnd in late_rounds]
    for rnd, chunk, cut in sent:
        for k in range(groups):
            f = owner_ref[k]
            c = table_ref[rnd, f]
            high = jnp.maximum(f, c)
            low = jnp.minimum(f, c)
            mine = jnp.logical_and(c >= 0, high // per_stage == q)
            row = jnp.clip((high - first_group) * own, 0, width - own)
            col = jnp.clip(low * own, 0, (q + 1) * width - own)

            @pl.when(jnp.logical_and(mine, f > c))
            def _(chunk=chunk, cut=cut, k=k, row=row, col=col):
                a_ref[ds(row, own), ds(col, own)] = chunk[k][:, cut : cut + own]

            @pl.when(jnp.logical_and(mine, f < c))
            def _(chunk=chunk, cut=cut, k=k, row=row, col=col):
                a_ref[ds(row, own), ds(col, own)] = chunk[k][:, cut : cut + own].T


def child_stage(q, width, own, groups, late_rounds, counts, span, couples, refs):
    start, stop = span
    panels = width // LANES
    refs = list(refs)

    def take(count):
        out, refs[:count] = refs[:count], []
        return out

    (place_ref,) = take(1)
    if start == 0:
        owner_ref, table_ref = take(2)
        chunks = [take(count) for count in counts]
    else:
        state = take(5)
    prev_lh, prev_ll, prev_ih, prev_il = (take(q) for _ in range(4))
    if couples:
        b_ref = take(1)[0]
        old_x = take(2) if q > 1 else None
    if stop == panels:
        take(1)
    s_out, lh, ll, invh, invl = take(5)
    if couples:
        xh, xl = take(2)
    if stop == panels:
        lower_ref = take(1)[0]
    if start == 0:
        a_ref = take(1)[0]
    if stop == panels:
        own_ref, own_sem = take(2)

    if start == 0:
        assemble_rows(q, width, own, groups, owner_ref, table_ref, chunks, late_rounds, a_ref)
        for j in range(q):
            part = a_ref.at[:, j * width : (j + 1) * width]
            subtract_products(part, width, width, lh, ll, prev_lh[j], prev_ll[j], j * width)
            times_inverse(part, lh, ll, j * width, width, width, prev_ih[j], prev_il[j])
        s_out[...] = a_ref[:, q * width : (q + 1) * width]
        subtract_products(s_out, width, width, lh, ll, lh, ll, q * width, True)
        clear_inverse(invh, invl)
    else:
        for new, held in zip((s_out, lh, ll, invh, invl), state, strict=True):
            new[...] = held[...]
    if couples and q > 1:
        xh[:, : (q - 1) * width] = old_x[0][...]
        xl[:, : (q - 1) * width] = old_x[1][...]
    def job(p):
        if couples:
            some = own // (stop - start)
            rows = ds((p - start) * some, some)
            solve_some(
                rows, b_ref[rows, :], q - 1, width, xh, xl,
                (prev_lh[q - 1], prev_ll[q - 1]), (prev_ih[q - 1], prev_il[q - 1]),
            )

    factor_panels(start, stop, s_out, q * width, width, lh, ll, invh, invl, job)
    if stop == panels:

        @pl.when(place_ref[3] == q)
        def _():
            rows = ds(place_ref[0], own)
            own_ref[...] = lh[rows, :].astype(F32) + ll[rows, :].astype(F32)
            copy = pltpu.make_async_copy(own_ref, lower_ref.at[:, : own_ref.shape[1]], own_sem)
            copy.start()
            copy.wait()


def landing_kernel(stages, sources, cap, refs):
    refs = list(refs)

    def take(count):
        out, refs[:count] = refs[:count], []
        return out

    given = take(4 * stages)
    (raw_ref, th, tl, sq_ref, t_ref) = take(5)
    held = take(4 * stages)
    (copy_sems,) = take(1)
    lh, ll, ih, il = (held[k * stages : (k + 1) * stages] for k in range(4))
    front = raw_ref.shape[0]
    total = sources * cap
    width = ih[0].shape[0]
    share = total // front
    copies = []
    for f in range(front):
        at = (f % sources) * cap + (f // sources) * share
        copies.append(
            pltpu.make_async_copy(
                raw_ref.at[f, :share, :], t_ref.at[at : at + share, :], copy_sems.at[f]
            )
        )
        copies[-1].start()
    factors = [
        [
            pltpu.make_async_copy(
                given[k * stages + q], held[k * stages + q], copy_sems.at[front + 4 * q + k]
            )
            for k in range(4)
        ]
        for q in range(stages)
    ]
    for stage in factors:
        for copy in stage:
            copy.start()
    for copy in copies:
        copy.wait()
    for q in range(stages):
        for copy in factors[q]:
            copy.wait()
        part = t_ref.at[:, q * width : (q + 1) * width]
        subtract_products(part, total, width, th, tl, lh[q], ll[q], q * width)
        times_inverse(part, th, tl, q * width, total, width, ih[q], il[q])

    def square(t, carry):
        i, j = carry
        a = (th[ds(i * LANES, LANES), :], tl[ds(i * LANES, LANES), :])
        b = (th[ds(j * LANES, LANES), :], tl[ds(j * LANES, LANES), :])
        sq_ref[t] = dot3(a, b, NT)
        end = j == i
        return (jnp.where(end, i + 1, i), jnp.where(end, 0, j + 1))

    blocks = total // LANES
    lax.fori_loop(0, blocks * (blocks + 1) // 2, square, (jnp.int32(0), jnp.int32(0)))


def own_kernel(first, stages, width, refs):
    refs = list(refs)

    def take(count):
        out, refs[:count] = refs[:count], []
        return out

    (b_ref,) = take(1)
    old_h, old_l = take(2) if first > 0 else (None, None)
    left = stages - first
    lh, ll, ih, il = (take(left) for _ in range(4))
    th, tl = take(2)
    x_ref, con_ref = take(2)
    xh, xl = take(2)
    own = b_ref.shape[0]
    if first > 0:
        xh[:, : first * width] = old_h[...]
        xl[:, : first * width] = old_l[...]
    for k in range(left):
        q = first + k
        for c in range(1):
            part = b_ref.at[:, k * width : (k + 1) * width]
            x_ref[:, q * width : (q + 1) * width] = part[...]
            part = x_ref.at[:, q * width : (q + 1) * width]
            subtract_products(part, own, width, xh, xl, lh[k], ll[k], q * width)
            times_inverse(part, xh, xl, q * width, own, width, ih[k], il[k])
    x_ref[...] = xh[...].astype(F32) + xl[...].astype(F32)

    def body(r, nr, c, nc):
        a = (xh[ds(r, nr), :], xl[ds(r, nr), :])
        b = (th[ds(c, nc), :], tl[ds(c, nc), :])
        con_ref[ds(r, nr), ds(c, nc)] = dot3(a, b, NT)

    tiles(own, con_ref.shape[1], body)


def parent_kernel(children, blocks, width, sources, refs):
    refs = list(refs)
    place_ref, spread_ref = refs[:2]
    tops, squares = refs[2 : 2 + children], refs[2 + children : 2 + 2 * children]
    lh, ll, invh, invl, s_ref, top_ref = refs[2 + 2 * children :]
    pivots = lh.shape[0]
    dense = pivots // blocks
    groups, part_rows, _ = tops[0].shape
    spreads = groups // sources
    piece = part_rows * spreads
    for m in range(children):
        g = place_ref[2] ^ m
        for f in range(groups):
            at = (f % sources) * (children * piece) + g * piece + (f // sources) * part_rows
            top_ref[ds(at, part_rows), :] = tops[m][f]
    for i in range(blocks):
        for j in range(i + 1):
            at = i * (i + 1) // 2 + j
            parts = []
            for c in range(children):
                left = spread_ref[i, :, c * LANES : (c + 1) * LANES]
                high, low = split(squares[c][at])
                parts.append(dot(left, high, NN) + dot(left, low, NN))
            high, low = split(jnp.concatenate(parts, axis=1))
            right = spread_ref[j]
            rows = slice(i * dense, (i + 1) * dense)
            cols = slice(j * dense, (j + 1) * dense)
            s_ref[rows, cols] = top_ref[rows, cols] - (
                dot(high, right, NT) + dot(low, right, NT)
            )
    for q in range(pivots // width):
        rows = slice(q * width, (q + 1) * width)
        lhq, llq = lh.at[rows, :], ll.at[rows, :]
        if q + 1 < pivots // width:
            lhq[:, (q + 1) * width :] = jnp.zeros((width, pivots - (q + 1) * width), BF16)
            llq[:, (q + 1) * width :] = jnp.zeros((width, pivots - (q + 1) * width), BF16)
        for j in range(q):
            part = s_ref.at[rows, j * width : (j + 1) * width]
            cut = slice(j * width, (j + 1) * width)
            subtract_products(part, width, width, lhq, llq, lh.at[cut, :], ll.at[cut, :], j * width)
            times_inverse(part, lhq, llq, j * width, width, width, invh.at[j], invl.at[j])
        part = s_ref.at[rows, q * width : (q + 1) * width]
        subtract_products(part, width, width, lhq, llq, lhq, llq, q * width, True)
        clear_inverse(invh.at[q], invl.at[q])
        factor_panels(0, width // LANES, part, q * width, width, lhq, llq, invh.at[q], invl.at[q])


def rest_kernel(children, blocks, width, refs):
    refs = list(refs)
    place_ref, rows_ref, route_ref, spread_ref = refs[:4]
    con_refs = refs[4 : 4 + children]
    lh, ll, invh, invl, out_ref, s_ref, xh, xl = refs[4 + children :]
    pivots = lh.shape[0]
    count = rows_ref.shape[0]
    dense = pivots // blocks
    at = place_ref[1]

    @pl.when(at < pivots)
    def _():
        row = ds(jnp.minimum(at, pivots - count), count)
        out_ref[...] = lh[row, :].astype(F32) + ll[row, :].astype(F32)

    @pl.when(at >= pivots)
    def _():
        routed = []
        for c in range(children):
            high, low = split(con_refs[c][...])
            route = route_ref[c]
            routed.append(split(dot(route, high, NN) + dot(route, low, NN)))
        for b in range(blocks):
            lanes = slice(b * LANES, (b + 1) * LANES)
            high = jnp.concatenate([routed[c][0][:, lanes] for c in range(children)], axis=1)
            low = jnp.concatenate([routed[c][1][:, lanes] for c in range(children)], axis=1)
            right = spread_ref[b]
            cols = slice(b * dense, (b + 1) * dense)
            s_ref[:, cols] = rows_ref[:, cols] - (dot(high, right, NT) + dot(low, right, NT))
        for q in range(pivots // width):
            cut = slice(q * width, (q + 1) * width)
            part = s_ref.at[:, cut]
            subtract_products(part, count, width, xh, xl, lh.at[cut, :], ll.at[cut, :], q * width)
            times_inverse(part, xh, xl, q * width, count, width, invh.at[q], invl.at[q])
        out_ref[...] = xh[...].astype(F32) + xl[...].astype(F32)


def on_device(child_pivot, child_coupling, parent_arrow, row_map, block_pattern):
    front = lax.axis_size("front")
    bulk = lax.axis_size("bulk")
    me = lax.axis_index("front")
    mine = child_pivot[0]
    coupling = child_coupling[0]
    own, total = mine.shape
    count, pivots = parent_arrow.shape
    width = min(STAGE, total)
    stages = total // width
    per_stage = width // own
    first_row = (lax.axis_index("bulk") * front + me) * count
    sources = pivots // count
    cap = min(CAP, count, own)
    blocks = sources * cap // LANES

    table = send_plan(front, per_stage)
    rounds = table.shape[0]
    bulk_me = lax.axis_index("bulk")
    early = max(
        (r + 1 for r in range(rounds) for f, c in enumerate(table[r]) if c >= 0 and max(f, c) // per_stage <= 1),
        default=0,
    )
    half = own // 2
    own_map = row_map[0]
    own_block = lax.dynamic_slice_in_dim(mine, me * own, own, 1)
    even = lax.dynamic_slice_in_dim(mine, jnp.minimum(me + 1, front - 1) * own, half, 1)
    odd = lax.dynamic_slice_in_dim(mine[half:], jnp.maximum(me - 1, 0) * own, own, 1).T
    head = jnp.concatenate([own_block, jnp.where(me % 2 == 0, even, odd)], axis=1)
    tail = jnp.pad(own_map.astype(F32)[None], ((0, SUB - 1), (0, half)))
    chunks = [jnp.concatenate([head, tail], axis=0)]
    mine_later, table_me = after((mine, jnp.asarray(table)[:, me]), chunks[0])
    for rnd in range(rounds):
        col = jnp.maximum(table_me[rnd], 0)
        chunks.append(lax.dynamic_slice_in_dim(mine_later, col * own, own, 1))
    owners = slot_owners("front", front)
    gathered = [ring_gather(chunks[0], "front", front)]
    started = gathered[0][1:]
    for rnd in range(1, early + 1):
        gathered.append(ring_gather(after(chunks[rnd], gathered[-1][1:]), "front", front))
    here = gathered[-1][1:]
    late = Ring(after(jnp.concatenate(chunks[early + 1 :], axis=1), here), "front", front)
    table_in = jnp.asarray(table)
    place = jnp.stack([(me % per_stage) * own, first_row, bulk_me, me // per_stage]).astype(jnp.int32)

    own_lands = own_map < pivots
    own_rank = jnp.where(own_lands, ranks(own_lands), -1)
    pick = (own_rank[None, :] == jnp.arange(cap)[:, None]).astype(F32)
    spreads = front // sources

    def spread_out(x):
        rows = x.shape[0] // spreads
        part = x[:rows]
        for k in range(1, spreads):
            moved = lax.ppermute(
                x[k * rows : (k + 1) * rows],
                "front",
                [(s, s + k * sources) for s in range(sources)],
            )
            part = jnp.where(me // sources == k, moved, part)
        return part

    compact = jnp.dot(pick, coupling, precision=HIGHEST_PRECISION)
    place = after(place, here)
    block_rows = (first_row + jnp.arange(count)) // BLOCK
    row_mask = jnp.take(block_pattern, block_rows, axis=0).astype(F32)
    arrow = parent_arrow * jnp.repeat(row_mask, BLOCK, axis=1)
    piece = count // bulk
    my_maps = jnp.stack([slot[own, :own] for slot in gathered[0]])
    ordered = jnp.sum(
        jnp.where(owners[None, :, None] == jnp.arange(front)[:, None, None], my_maps[None], 0.0), axis=1
    )
    sent = {}

    def send_first(token):
        part = after(arrow, token)
        pieces = part[:piece]
        for g in range(1, bulk):
            moved = lax.ppermute(part[g * piece : (g + 1) * piece], "bulk", [(0, g)])
            pieces = jnp.where(bulk_me == g, moved, pieces)
        sent["pieces"] = pieces
        sent["maps"] = jnp.stack(bulk_gather(after(ordered, token), "bulk", bulk)).astype(jnp.int32)
        return pieces, sent["maps"]

    def send_second(token):
        sent["landing"] = spread_out(after(compact, token))
        sent["line"] = spread_out(after(sent["pieces"], token))
        return sent["landing"], sent["line"]

    def send_third(token):
        landing, line = sent["landing"], sent["line"]
        extra = line.reshape(-1, total)
        padding = jnp.zeros((-extra.shape[0] % SUB, total), F32)
        both = after(jnp.concatenate([landing, extra, padding], axis=0), token)
        sent["all"] = lax.all_gather(both, "front", axis=0, tiled=False)
        share = landing.shape[0]
        sent["lines"] = sent["all"][:, share : share + extra.shape[0]].reshape((front,) + line.shape)
        return both

    place = after(place, send_first(started))
    hooks = [lambda token: place, send_second, send_third]

    panels = width // LANES
    total_landing = sources * cap
    lh, ll, ih, il = ([] for _ in range(4))
    lower_rows = jnp.zeros((own, total), F32)
    xs = None
    for q in range(stages):
        final = q == stages - 1
        if q == 2 or (q < 2 and final):
            late.finish()
        split_at = [0, panels // 2, panels] if q < 2 and not final else [0, panels]
        needed = [
            any(c >= 0 and max(f, c) // per_stage == q for f, c in enumerate(row)) for row in table
        ]
        used = [gathered[0]] + [gathered[rnd + 1] if needed[rnd] else [] for rnd in range(early)]
        late_rounds = [(rnd - early, rnd) for rnd in range(early, rounds) if needed[rnd]]
        used.append(late.slots() if late_rounds else [])
        counts = [len(u) for u in used]
        deep = (q + 1) * width
        state = None
        for start, stop in zip(split_at[:-1], split_at[1:], strict=True):
            couples = 0 < q < stages - 1 and stop == panels
            if q < 2 and not final:
                place = late.advance(place)
            operands = [place]
            smem = 1
            aliases = {}
            if start == 0:
                operands += [owners, table_in] + [x for u in used for x in u]
                smem = 3
            else:
                operands += state
                aliases = {1 + k: k for k in range(5)}
            operands += lh + ll + ih + il
            if couples:
                operands.append(coupling[:, (q - 1) * width : q * width])
                if q > 1:
                    operands += xs
            outs = [
                shaped((width, width), F32),
                shaped((width, deep), BF16),
                shaped((width, deep), BF16),
                shaped((width, width), BF16),
                shaped((width, width), BF16),
            ]
            scratch = []
            if couples:
                outs += [shaped((own, q * width), BF16)] * 2
            out_kinds = [False] * len(outs)
            if stop == panels:
                aliases[len(operands)] = len(outs)
                operands.append(lower_rows)
                outs.append(shaped((own, total), F32))
                out_kinds.append(None)
            if start == 0:
                scratch.append(pltpu.VMEM((width, deep), F32))
            if stop == panels:
                scratch += [pltpu.VMEM((own, deep), F32), pltpu.SemaphoreType.DMA(())]
            out = list(
                vmem_call(
                    functools.partial(
                        lambda *refs, args: child_stage(*args, refs),
                        args=(
                            q, width, own, front, late_rounds, counts, (start, stop),
                            couples,
                        ),
                    ),
                    outs,
                    [True] * smem
                    + [False] * (len(operands) - smem - (stop == panels))
                    + [None] * (stop == panels),
                    scratch,
                    pl.CostEstimate(
                        flops=6_000_000_000 * (stop - start), bytes_accessed=1 << 20, transcendentals=0
                    ),
                    aliases,
                    out_kinds,
                )(*operands)
            )
            state = out[:5]
            rest = out[5:]
            if couples:
                xs, rest = rest[:2], rest[2:]
            if stop == panels:
                lower_rows = rest[0]
            if q < 2 and not final:
                place = late.arrive(place, state[0])
                if hooks:
                    place = after(place, hooks.pop(0)((late.going, late.coming, place)))
        for held, new in zip((lh, ll, ih, il), state[1:], strict=True):
            held.append(new)

    for hook in hooks:
        hook(place)
    maps = sent["maps"]
    lands = maps[:, :sources] < pivots
    rank = ranks(lands)
    overflow = jnp.any(rank[:, :, -1] >= cap)
    chosen = jnp.where(lands, rank, -1)[:, :, None, :] == jnp.arange(cap)[:, None]
    target = jnp.max(jnp.where(chosen, maps[:, :sources, None, :], -1), axis=3)
    target = jnp.where(overflow, -1, target).reshape(bulk, blocks, LANES)
    dense = pivots // blocks
    rows_of = (jnp.arange(blocks)[:, None] * dense + jnp.arange(dense)[None, :])[:, :, None, None]
    spread = (jnp.transpose(target, (1, 0, 2))[:, None] == rows_of).astype(BF16)
    spread = spread.reshape(blocks, dense, bulk * LANES)
    route = (
        lax.dynamic_index_in_dim(maps, me, 1, False)[:, None, :]
        == (first_row + jnp.arange(count))[None, :, None]
    ).astype(BF16)

    operands = lh + ll + ih + il
    th, tl, squares = vmem_call(
        lambda *refs: landing_kernel(stages, sources, cap, refs),
        [
            shaped((total_landing, total), BF16),
            shaped((total_landing, total), BF16),
            shaped((blocks * (blocks + 1) // 2, LANES, LANES), F32),
        ],
        [None] * (len(operands) + 1),
        [pltpu.VMEM((total_landing, total), F32)]
        + [pltpu.VMEM(x.shape, x.dtype) for x in operands]
        + [pltpu.SemaphoreType.DMA((front + 4 * stages,))],
        pl.CostEstimate(flops=20_000_000_000, bytes_accessed=1 << 20, transcendentals=0),
    )(*operands, sent["all"])

    solved = max(stages - 2, 0)
    operands = [coupling[:, solved * width :]] + (xs if solved > 0 else [])
    operands += lh[solved:] + ll[solved:] + ih[solved:] + il[solved:] + [th, tl]
    x_own, con = vmem_call(
        lambda *refs: own_kernel(solved, stages, width, refs),
        [shaped((own, total), F32), shaped((own, total_landing), F32)],
        [False] * len(operands),
        [pltpu.VMEM((own, total), BF16)] * 2,
        pl.CostEstimate(flops=10_000_000_000, bytes_accessed=1 << 20, transcendentals=0),
    )(*operands)
    all_squares = bulk_gather(squares, "bulk", bulk, beside=lambda: con)

    def unchanged(lines, arrow, x_own):
        return lines, arrow

    def landing_whole(lines, arrow, x_own):
        slot = own_map - me * count
        hits = (slot[:, None] == jnp.arange(count)[None, :]).astype(F32)
        piece_rows = jnp.dot(hits.T, x_own, precision=HIGHEST_PRECISION)
        whole = lax.all_gather(piece_rows, "front", axis=0, tiled=True)[:pivots]
        reached = jnp.dot(x_own, whole.T, precision=HIGHEST_PRECISION)
        slot_index = own_map // count // front * count + own_map % count
        routing = (slot_index[:, None] == jnp.arange(bulk * count)[None, :]).astype(F32)
        added = lax.psum_scatter(
            jnp.dot(routing.T, reached, precision=HIGHEST_PRECISION),
            "bulk",
            scatter_dimension=0,
            tiled=True,
        )
        square = lax.psum(jnp.dot(whole, whole.T, precision=HIGHEST_PRECISION), "bulk")
        square = square.reshape(sources, bulk, spreads, piece // spreads, pivots)
        square = jnp.transpose(square, (1, 2, 0, 3, 4)).reshape(bulk, front, piece // spreads, pivots)
        changed = [
            lines[m] - lax.dynamic_index_in_dim(square, bulk_me ^ m, 0, False) for m in range(bulk)
        ]
        return changed, arrow - added

    lines = bulk_gather(sent["lines"], "bulk", bulk)
    lines, arrow = lax.cond(overflow, landing_whole, unchanged, lines, arrow, x_own)

    all_con = bulk_gather(con, "bulk", bulk, low_first=True)
    plh, pll, pih, pil = vmem_call(
        lambda *refs: parent_kernel(bulk, blocks, width, sources, refs),
        [
            shaped((pivots, pivots), BF16),
            shaped((pivots, pivots), BF16),
            shaped((pivots // width, width, width), BF16),
            shaped((pivots // width, width, width), BF16),
        ],
        [True] + [False] * (1 + 2 * bulk),
        [pltpu.VMEM((pivots, pivots), F32)] * 2,
        pl.CostEstimate(flops=60_000_000_000, bytes_accessed=1 << 24, transcendentals=0),
    )(place, spread, *lines, *all_squares)

    (parent_rows,) = vmem_call(
        lambda *refs: rest_kernel(bulk, blocks, width, refs),
        [shaped((count, pivots), F32)],
        [True] + [False] * (7 + bulk),
        [
            pltpu.VMEM((count, pivots), F32),
            pltpu.VMEM((count, pivots), BF16),
            pltpu.VMEM((count, pivots), BF16),
        ],
    )(place, arrow, route, spread, *all_con, plh, pll, pih, pil)
    return (lower_rows[None], x_own[None], parent_rows)


def solution(mesh):
    placed = (
        P("bulk", "front", None),
        P("bulk", "front", None),
        P(("bulk", "front"), None),
        P("bulk", "front"),
        P(),
    )
    return jax.shard_map(
        on_device,
        mesh=mesh,
        in_specs=placed,
        out_specs=(P("bulk", "front", None), P("bulk", "front", None), P(("bulk", "front"), None)),
        check_vma=False,
    )
```
